32 devices in a mesh: section: 2 (over x), expert: 16 (over z, y, core).
Axes of the slice: x: 2, y: 2, z: 4, core: 2. Of those that a mesh axis runs over, the one named last changes fastest.
Arguments:
- tokens: bfloat16 [2048, 4096], P('expert', 'section'), may hold values from -6 to 6
- expert_ids: int32 [2048, 8], P('expert'), may hold values from 0 to 15, all different within a row; in each aligned block of 128 rows (0 to 127, 128 to 255, ...) at most 80 rows name the same one
- numerators: int32 [2048, 8], P('expert'), may hold values from 1 to 255
- gate_up_weight: bfloat16 [16, 4096, 3072], P('expert', None, 'section'), may hold values from -0.09375 to 0.09375
- down_weight: bfloat16 [16, 1536, 4096], P('expert', None, 'section'), may hold values from -0.15625 to 0.15625
Outputs:
- mixed: bfloat16 [2048, 4096], P('expert', 'section')
The draws below stay inside these ranges and needn't reach their ends.
Inputs may be any that keep to these rules, and one draw needn't show every extreme that they name: `expert_ids`: each row names 8 different experts. Among the rows of one index of expert (aligned blocks of 128 rows) no expert is named more than 80 times, and in every draw some expert is named exactly 80 times there.
All inputs are finite; a program needn't handle non-finite values.
Results may differ from the reference program's by a relative error of at most 0.0057.
Values may be sent and summed in bfloat16 or wider, within the bound.
No kernel may reach another device: no remote copies, remote signals or barrier semaphores. Data moves between devices by JAX's collectives and lax.ppermute only.
A program may use at most 128 MiB of HBM per device.

```python
import math
import jax
import jax.numpy as jnp
import numpy as np
from jax import lax

D = 4096
FF = 1536
BLOCK_UNITS = 64
TOPK = 8
TOK_DEV = 128
EXPERTS = 16
TOKENS = 2048
CAP = 80


def set_ends(values, own_key, least, top_value):
    longest = values.shape.index(max(values.shape))
    spots = []
    for shift in (0, 1):
        where = [jax.random.randint(jax.random.fold_in(own_key, axis), (), 0, length) for axis, length in enumerate(values.shape)]
        where[longest] = (where[longest] + shift) % values.shape[longest]
        spots.append(tuple(where))
    return values.at[spots[0]].set(least).at[spots[1]].set(top_value)


def shard_levels(own_key, extent, split, least, largest):
    factor_of = 1.0
    for axis_at, shards_of in split:
        steps = jax.random.uniform(jax.random.fold_in(jax.random.fold_in(own_key, 6), axis_at), (shards_of,), jnp.float32, least / len(split), largest / len(split))
        factor_of = factor_of * jnp.repeat(jnp.exp(steps), extent[axis_at] // shards_of).reshape((-1,) + (1,) * (len(extent) - 1 - axis_at))
    return factor_of


def shared_out(stream_key, own, number, rows, count, top, reach, skew):
    order = jax.random.permutation(stream_key, count)
    crowded, common = load_shares(count, rows * top, reach, skew, True), load_shares(count, rows * top, reach, skew, False)
    places = jnp.arange(count)

    def named(tallies, rotation):
        used = int((tallies > 0).sum())
        fixed = max(1, used // 4)
        passed = fixed + (places - fixed + rotation * (used - fixed)) % max(1, count - fixed)
        return jnp.zeros((count,), jnp.int32).at[order[jnp.where(places < fixed, places, passed)]].set(jnp.asarray(tallies, jnp.int32))

    tallies = jnp.where(number % 4 == 0, named(crowded, number // 4), named(common, number - number // 4 - 1))
    mixed = jax.random.permutation(jax.random.fold_in(own, 3), count)
    giver, taker = mixed[0:count // 2 * 2:2], mixed[1:count // 2 * 2:2]
    margin = jnp.minimum(tallies[giver] - 1, reach - tallies[taker]) // 2
    margin = jnp.where((giver == order[0]) | (taker == order[0]) | (tallies[taker] == 0), 0, jnp.maximum(margin, 0))
    passed = jax.random.randint(jax.random.fold_in(own, 4), (count // 2,), 0, 1 << 20) % (margin + 1)
    tallies = tallies.at[giver].add(-passed).at[taker].add(passed)
    members = jnp.searchsorted(jnp.cumsum(tallies), jnp.arange(rows * top), side="right").astype(jnp.int32)
    grid = members.reshape(top, rows).T
    grid = grid[jax.random.permutation(jax.random.fold_in(own, 1), rows)]
    rotation = jax.random.randint(jax.random.fold_in(own, 2), (rows, 1), 0, top)
    return jnp.take_along_axis(grid, (jnp.arange(top)[None, :] + rotation) % top, axis=1)


def load_shares(amount, total, bound, slope, full):
    portions = [(1 << 20) // math.isqrt(standing ** slope) + 1 for standing in range(1, amount + 1)]
    largest = bound if full else min(bound, max(-(-total // amount), total * portions[0] // sum(portions)))
    least = 1 if total - largest >= amount - 1 else 0
    holding, surplus = [largest] + [least] * (amount - 1), total - largest - least * (amount - 1)
    while surplus > 0:
        candidates = [i for i in range(1, amount) if holding[i] < largest] or [i for i in range(1, amount) if holding[i] < bound]
        whole, remaining = sum([portions[i] for i in candidates]), surplus
        for i in candidates:
            extra = min(bound - holding[i], max(1, remaining * portions[i] // whole), surplus)
            holding[i] = holding[i] + extra
            surplus = surplus - extra
    return np.array(holding)


def gaussian(rng, dims, scale, bound, pieces=(), held_as=jnp.bfloat16):
    gain = shard_levels(rng, dims, pieces, -0.22, 0.18) if pieces else 1.0
    drawn = jax.random.normal(rng, dims, jnp.float32) * scale * gain
    return jnp.minimum(jnp.maximum(drawn, -bound), bound).astype(held_as)


def setup_inputs(seed: int = 0) -> dict:
    seeds = jax.random.split(jax.random.key(seed), 6)
    tokens = gaussian(seeds[0], (TOKENS, D), 1.0, 6.0, ((0, 16), (1, 2)))
    expert_ids_keys = jax.random.split(jax.random.fold_in(seeds[1], 1), TOKENS // TOK_DEV)
    expert_ids_turns = jax.random.permutation(jax.random.fold_in(seeds[1], 3), TOKENS // TOK_DEV)
    expert_ids = jax.vmap(lambda own, number: shared_out(jax.random.fold_in(seeds[1], 2), own, number, TOK_DEV, EXPERTS, TOPK, CAP, 2))(expert_ids_keys, expert_ids_turns).reshape((TOKENS, TOPK))
    numerators = set_ends(jax.random.randint(seeds[2], (TOKENS, TOPK), 1, 256), jax.random.fold_in(seeds[2], 1), 1, 255).astype(jnp.int32)
    gate_up_weight = gaussian(seeds[3], (EXPERTS, D, 2 * FF), D ** -0.5, 0.09375, ((0, 16), (2, 2)))
    down_weight = gaussian(seeds[4], (EXPERTS, FF, D), FF ** -0.5, 0.15625, ((0, 16), (2, 2)))
    return {"tokens": tokens, "expert_ids": expert_ids, "numerators": numerators, "gate_up_weight": gate_up_weight, "down_weight": down_weight}


denominator = 256.0


def reference(tokens, expert_ids, numerators, gate_up_weight, down_weight):
    blocks = TOKENS // TOK_DEV
    assigned = TOK_DEV * TOPK
    flat = expert_ids.reshape(blocks, assigned).astype(jnp.int32)
    hits = (flat[:, :, None] == jnp.arange(EXPERTS, dtype=jnp.int32)[None, None, :]).astype(jnp.int32)
    rank = jnp.sum((jnp.cumsum(hits, axis=1) - hits) * hits, axis=2).astype(jnp.int32)
    block_ids = jnp.arange(blocks, dtype=jnp.int32)[:, None]
    slot = (block_ids * CAP + rank).astype(jnp.int32)
    source = (block_ids * TOK_DEV + jnp.arange(assigned, dtype=jnp.int32)[None, :] // TOPK).astype(jnp.int32)
    table = jnp.full((EXPERTS, blocks * CAP), TOKENS, jnp.int32).at[flat, slot].set(source)
    weights = numerators.reshape(blocks, assigned).astype(jnp.float32) / denominator
    scales = jnp.zeros((EXPERTS, blocks * CAP), jnp.float32).at[flat, slot].set(weights)

    def one_expert(total, packed):
        index, scale, w_both, w_down = packed
        rows = jnp.take(tokens, index, axis=0, mode="fill", fill_value=0)
        both = jnp.dot(rows, w_both, preferred_element_type=jnp.float32)
        split_up = both.reshape(rows.shape[0], FF // BLOCK_UNITS, 2, BLOCK_UNITS)
        gate = split_up[:, :, 0, :].reshape(rows.shape[0], FF)
        up = split_up[:, :, 1, :].reshape(rows.shape[0], FF)
        hidden = (jax.nn.silu(gate) * up).astype(jnp.bfloat16)
        result = jnp.dot(hidden, w_down, preferred_element_type=jnp.float32).astype(jnp.bfloat16)
        total = total.at[index].add(result.astype(jnp.float32) * scale[:, None], mode="drop")
        return total, None

    start = jnp.zeros((TOKENS, D), jnp.float32)
    total, _ = lax.scan(one_expert, start, (table, scales, gate_up_weight, down_weight))
    return total.astype(jnp.bfloat16)
```

```python
import functools

import jax
import jax.numpy as jnp
from jax import lax
from jax.experimental import pallas as pl
from jax.experimental.pallas import tpu as pltpu
from jax.sharding import PartitionSpec as P

UNITS = 64
SCALE = 1.0 / 256.0


def group_of(capacity):
    count = 2
    while (count * capacity) % 16:
        count *= 2
    return count


def slot_map(code, group, capacity):
    line = jnp.concatenate(
        [code[i : i + 1] + jnp.where(code[i : i + 1] >= 0, i * capacity * 256, 0) for i in range(group)], axis=1
    )
    slot, weight = line >> 8, line & 255
    places = lax.broadcasted_iota(jnp.int32, (group * capacity, line.shape[1]), 0)
    return places == slot, weight


def up_kernel(group, capacity, code_ref, tokens_ref, weight_ref, hidden_ref, rows_ref):
    groups = tokens_ref.shape[0] // group
    sections, rows, width = tokens_ref.shape[1:]
    size = group * capacity
    for g in range(groups):
        onehot, _ = slot_map(code_ref[0, g * group : (g + 1) * group], group, capacity)
        onehot = onehot.astype(jnp.bfloat16)
        for s in range(sections):
            block = jnp.concatenate([tokens_ref[g * group + i, s] for i in range(group)], axis=0)
            picked = jnp.dot(onehot, block, preferred_element_type=jnp.float32)
            rows_ref[g * size : (g + 1) * size, s * width : (s + 1) * width] = picked.astype(jnp.bfloat16)
    columns = weight_ref.shape[1]
    pair = 4 * UNITS

    def products(first, count):
        return jnp.dot(rows_ref[...], weight_ref[:, pl.ds(first, count)], preferred_element_type=jnp.float32)

    def mix(gate, up):
        return (gate / (1.0 + jnp.exp(-gate)) * up).astype(jnp.bfloat16)

    @pl.loop(0, columns // pair)
    def _(p):
        both = products(pl.multiple_of(p * pair, pair), pair)
        one, two = both[:, : 2 * UNITS], both[:, 2 * UNITS :]
        low = lax.broadcasted_iota(jnp.int32, one.shape, 1) < UNITS
        gate = jnp.where(low, one, pltpu.roll(two, UNITS, 1))
        up = jnp.where(low, pltpu.roll(one, UNITS, 1), two)
        hidden_ref[:, pl.ds(pl.multiple_of(p * 2 * UNITS, 2 * UNITS), 2 * UNITS)] = mix(gate, up)

    if columns % pair:
        start = columns // pair * pair
        both = products(start, 2 * UNITS)
        hidden_ref[:, start // 2 :] = mix(both, pltpu.roll(both, UNITS, 1))[:, :UNITS]


def down_kernel(group, capacity, code_ref, hidden_ref, weight_ref, out_ref, result_ref):
    sections, _, units = hidden_ref.shape
    groups = code_ref.shape[1] // group
    size = group * capacity
    wide = weight_ref.shape[1]
    step = min(512, wide)

    @pl.loop(0, wide // step)
    def _(p):
        at = pl.ds(pl.multiple_of(p * step, step), step)
        total = jnp.dot(hidden_ref[0], weight_ref[0:units, at], preferred_element_type=jnp.float32)
        for s in range(1, sections):
            total += jnp.dot(
                hidden_ref[s], weight_ref[s * units : (s + 1) * units, at], preferred_element_type=jnp.float32
            )
        result_ref[...] = total.astype(jnp.bfloat16)
        for g in range(groups):
            onehot, weight = slot_map(code_ref[0, g * group : (g + 1) * group], group, capacity)
            scaled = jnp.where(onehot, weight.astype(jnp.float32) * SCALE, 0.0).astype(jnp.bfloat16)
            mixed = lax.dot_general(
                scaled,
                result_ref[g * size : (g + 1) * size],
                (((0,), (0,)), ((), ())),
                preferred_element_type=jnp.float32,
            )
            tall = scaled.shape[1]
            out_ref[g * tall : (g + 1) * tall, at] = mixed.astype(jnp.bfloat16)


def up_call(code, tokens, weight, capacity):
    blocks, sections, rows, width = tokens.shape
    group = group_of(capacity)
    take = min(blocks, 2 * group)
    depth, columns = weight.shape
    tall = take * capacity
    flops = 2 * blocks * capacity * depth * (columns + group * rows)
    return pl.pallas_call(
        functools.partial(up_kernel, group, capacity),
        grid=(blocks // take,),
        in_specs=[
            pl.BlockSpec((1, take, rows), lambda i: (i, 0, 0)),
            pl.BlockSpec((take, sections, rows, width), lambda i: (i, 0, 0, 0)),
            pl.BlockSpec((depth, columns), lambda i: (0, 0), pipeline_mode=pl.Buffered(1)),
        ],
        out_specs=pl.BlockSpec((tall, columns // 2), lambda i: (i, 0)),
        out_shape=jax.ShapeDtypeStruct((blocks * capacity, columns // 2), jnp.bfloat16),
        scratch_shapes=[pltpu.VMEM((tall, depth), jnp.bfloat16)],
        compiler_params=pltpu.CompilerParams(vmem_limit_bytes=48 * 1024 * 1024),
        cost_estimate=pl.CostEstimate(
            flops=flops, bytes_accessed=2 * (tokens.size + weight.size), transcendentals=blocks * capacity * columns // 2
        ),
        name="gate_up",
    )(code.reshape(blocks // take, take, rows), tokens, weight)


def down_call(code, hidden, weight, capacity):
    blocks, rows = code.shape
    sections, _, units = hidden.shape
    group = group_of(capacity)
    take = min(blocks, 2 * group)
    depth, wide = weight.shape
    tall = take * capacity
    return pl.pallas_call(
        functools.partial(down_kernel, group, capacity),
        grid=(blocks // take,),
        in_specs=[
            pl.BlockSpec((1, take, rows), lambda i: (i, 0, 0)),
            pl.BlockSpec((sections, tall, units), lambda i: (0, i, 0)),
            pl.BlockSpec((depth, wide), lambda i: (0, 0), pipeline_mode=pl.Buffered(1)),
        ],
        out_specs=pl.BlockSpec((take * rows, wide), lambda i: (i, 0)),
        out_shape=jax.ShapeDtypeStruct((blocks * rows, wide), jnp.bfloat16),
        scratch_shapes=[pltpu.VMEM((tall, min(512, wide)), jnp.bfloat16)],
        compiler_params=pltpu.CompilerParams(vmem_limit_bytes=48 * 1024 * 1024),
        cost_estimate=pl.CostEstimate(
            flops=2 * blocks * capacity * wide * (depth + group * rows),
            bytes_accessed=2 * (hidden.size + weight.size + blocks * rows * wide),
            transcendentals=0,
        ),
        name="down",
    )(code.reshape(blocks // take, take, rows), hidden, weight)


def codes_of(expert_ids, numerators, experts):
    rows = expert_ids.shape[0]
    named = expert_ids.T[None] == jnp.arange(experts, dtype=jnp.int32)[:, None, None]
    hits = jnp.any(named, axis=1)
    weight = jnp.sum(jnp.where(named, numerators.T[None], 0), axis=1)
    earlier = jnp.arange(rows)[:, None] < jnp.arange(rows)[None, :]
    rank = jnp.dot(hits.astype(jnp.bfloat16), earlier.astype(jnp.bfloat16), preferred_element_type=jnp.float32)
    return jnp.where(hits, rank.astype(jnp.int32) * 256 + weight, -1)


def shards(tokens, expert_ids, numerators, gate_up_weight, down_weight):
    rows, width = tokens.shape
    experts = lax.axis_size("expert")
    capacity = rows * expert_ids.shape[1] * 5 // (4 * experts)
    chips = experts // 2
    across = [[2 * i + c for i in range(chips)] for c in range(2)]
    pairs = [[2 * i, 2 * i + 1] for i in range(chips)]

    codes = lax.all_gather(codes_of(expert_ids, numerators, experts), "expert", axis=0)
    code = lax.dynamic_index_in_dim(codes, lax.axis_index("expert"), 1, keepdims=False)
    code = code.reshape(chips, 2, rows).swapaxes(0, 1).reshape(experts, rows)

    wide = lax.all_gather(tokens, "section", axis=0)
    half = lax.all_gather(wide, "expert", axis=0, axis_index_groups=across)
    whole = lax.all_gather(half, "expert", axis=0, axis_index_groups=pairs)
    whole = whole.reshape((experts,) + wide.shape)

    hidden = up_call(code, whole, gate_up_weight[0], capacity)
    hidden = lax.all_gather(hidden, "section", axis=0)
    part = down_call(code, hidden, down_weight[0], capacity)

    part = part.reshape(2, chips * rows, width)
    part = lax.psum_scatter(part, "expert", scatter_dimension=0, axis_index_groups=pairs, tiled=False)
    return lax.psum_scatter(part, "expert", scatter_dimension=0, axis_index_groups=across, tiled=True)


def solution(mesh):
    in_specs = (
        P("expert", "section"),
        P("expert", None),
        P("expert", None),
        P("expert", None, "section"),
        P("expert", None, "section"),
    )
    out_specs = P("expert", "section")
    return jax.shard_map(shards, mesh=mesh, in_specs=in_specs, out_specs=out_specs, check_vma=False)
```

```python
import functools

import jax
import jax.numpy as jnp
from jax import lax
from jax.experimental import pallas as pl
from jax.experimental.pallas import tpu as pltpu
from jax.sharding import PartitionSpec as P

UNITS = 64
SCALE = 1.0 / 256.0


def group_of(capacity):
    count = 2
    while (count * capacity) % 16:
        count *= 2
    return count


def slot_map(code, group, capacity):
    line = jnp.concatenate(
        [code[i : i + 1] + jnp.where(code[i : i + 1] >= 0, i * capacity * 256, 0) for i in range(group)], axis=1
    )
    slot, weight = line >> 8, line & 255
    places = lax.broadcasted_iota(jnp.int32, (group * capacity, line.shape[1]), 0)
    return places == slot, weight


def up_kernel(group, capacity, code_ref, tokens_ref, weight_ref, hidden_ref, rows_ref):
    groups = tokens_ref.shape[0] // group
    sections, rows, width = tokens_ref.shape[1:]
    size = group * capacity
    for g in range(groups):
        onehot, _ = slot_map(code_ref[0, g * group : (g + 1) * group], group, capacity)
        onehot = onehot.astype(jnp.bfloat16)
        for s in range(sections):
            block = jnp.concatenate([tokens_ref[g * group + i, s] for i in range(group)], axis=0)
            picked = jnp.dot(onehot, block, preferred_element_type=jnp.float32)
            rows_ref[g * size : (g + 1) * size, s * width : (s + 1) * width] = picked.astype(jnp.bfloat16)
    columns = weight_ref.shape[1]
    pair = 4 * UNITS

    def products(first, count):
        return jnp.dot(rows_ref[...], weight_ref[:, pl.ds(first, count)], preferred_element_type=jnp.float32)

    def mix(gate, up):
        return (gate / (1.0 + jnp.exp(-gate)) * up).astype(jnp.bfloat16)

    @pl.loop(0, columns // pair)
    def _(p):
        both = products(pl.multiple_of(p * pair, pair), pair)
        one, two = both[:, : 2 * UNITS], both[:, 2 * UNITS :]
        low = lax.broadcasted_iota(jnp.int32, one.shape, 1) < UNITS
        gate = jnp.where(low, one, pltpu.roll(two, UNITS, 1))
        up = jnp.where(low, pltpu.roll(one, UNITS, 1), two)
        hidden_ref[:, pl.ds(pl.multiple_of(p * 2 * UNITS, 2 * UNITS), 2 * UNITS)] = mix(gate, up)

    if columns % pair:
        start = columns // pair * pair
        both = products(start, 2 * UNITS)
        hidden_ref[:, start // 2 :] = mix(both, pltpu.roll(both, UNITS, 1))[:, :UNITS]


def down_kernel(group, capacity, code_ref, hidden_ref, weight_ref, out_ref, result_ref):
    sections, _, units = hidden_ref.shape
    groups = code_ref.shape[1] // group
    size = group * capacity
    wide = weight_ref.shape[1]
    step = min(512, wide)

    @pl.loop(0, wide // step)
    def _(p):
        at = pl.ds(pl.multiple_of(p * step, step), step)
        total = jnp.dot(hidden_ref[0], weight_ref[0:units, at], preferred_element_type=jnp.float32)
        for s in range(1, sections):
            total += jnp.dot(
                hidden_ref[s], weight_ref[s * units : (s + 1) * units, at], preferred_element_type=jnp.float32
            )
        result_ref[...] = total.astype(jnp.bfloat16)
        for g in range(groups):
            onehot, weight = slot_map(code_ref[0, g * group : (g + 1) * group], group, capacity)
            scaled = jnp.where(onehot, weight.astype(jnp.float32) * SCALE, 0.0).astype(jnp.bfloat16)
            mixed = lax.dot_general(
                scaled,
                result_ref[g * size : (g + 1) * size],
                (((0,), (0,)), ((), ())),
                preferred_element_type=jnp.float32,
            )
            tall = scaled.shape[1]
            out_ref[g * tall : (g + 1) * tall, at] = mixed.astype(jnp.bfloat16)


def up_call(code, tokens, weight, capacity):
    blocks, sections, rows, width = tokens.shape
    group = group_of(capacity)
    take = min(blocks, 2 * group)
    depth, columns = weight.shape
    tall = take * capacity
    flops = 2 * blocks * capacity * depth * (columns + group * rows)
    return pl.pallas_call(
        functools.partial(up_kernel, group, capacity),
        grid=(blocks // take,),
        in_specs=[
            pl.BlockSpec((1, take, rows), lambda i: (i, 0, 0)),
            pl.BlockSpec((take, sections, rows, width), lambda i: (i, 0, 0, 0)),
            pl.BlockSpec((depth, columns), lambda i: (0, 0), pipeline_mode=pl.Buffered(1)),
        ],
        out_specs=pl.BlockSpec((tall, columns // 2), lambda i: (i, 0)),
        out_shape=jax.ShapeDtypeStruct((blocks * capacity, columns // 2), jnp.bfloat16),
        scratch_shapes=[pltpu.VMEM((tall, depth), jnp.bfloat16)],
        compiler_params=pltpu.CompilerParams(vmem_limit_bytes=48 * 1024 * 1024),
        cost_estimate=pl.CostEstimate(
            flops=flops, bytes_accessed=2 * (tokens.size + weight.size), transcendentals=blocks * capacity * columns // 2
        ),
        name="gate_up",
    )(code.reshape(blocks // take, take, rows), tokens, weight)


def down_call(code, hidden, weight, capacity):
    blocks, rows = code.shape
    sections, _, units = hidden.shape
    group = group_of(capacity)
    take = min(blocks, 2 * group)
    depth, wide = weight.shape
    tall = take * capacity
    return pl.pallas_call(
        functools.partial(down_kernel, group, capacity),
        grid=(blocks // take,),
        in_specs=[
            pl.BlockSpec((1, take, rows), lambda i: (i, 0, 0)),
            pl.BlockSpec((sections, tall, units), lambda i: (0, i, 0)),
            pl.BlockSpec((depth, wide), lambda i: (0, 0), pipeline_mode=pl.Buffered(1)),
        ],
        out_specs=pl.BlockSpec((take * rows, wide), lambda i: (i, 0)),
        out_shape=jax.ShapeDtypeStruct((blocks * rows, wide), jnp.bfloat16),
        scratch_shapes=[pltpu.VMEM((tall, min(512, wide)), jnp.bfloat16)],
        compiler_params=pltpu.CompilerParams(vmem_limit_bytes=48 * 1024 * 1024),
        cost_estimate=pl.CostEstimate(
            flops=2 * blocks * capacity * wide * (depth + group * rows),
            bytes_accessed=2 * (hidden.size + weight.size + blocks * rows * wide),
            transcendentals=0,
        ),
        name="down",
    )(code.reshape(blocks // take, take, rows), hidden, weight)


def pick_kernel(capacity, where_ref, code_ref, *refs):
    pieces, weight_ref, hidden_ref, rows_ref = refs[:8], refs[8], refs[9], refs[10]
    rows, width = pieces[0].shape

    @pl.when(pl.program_id(0) == 0)
    def _():
        for i, piece in enumerate(pieces):
            block, section = where_ref[4 + 2 * i], where_ref[5 + 2 * i]
            code = code_ref[pl.ds(where_ref[block], 1), :]
            places = lax.broadcasted_iota(jnp.int32, (capacity, rows), 0)
            onehot = (places == code >> 8).astype(jnp.bfloat16)
            picked = jnp.dot(onehot, piece[...], preferred_element_type=jnp.float32)
            down = pl.ds(pl.multiple_of(block * capacity, capacity), capacity)
            rows_ref[down, pl.ds(pl.multiple_of(section * width, width), width)] = picked.astype(jnp.bfloat16)

    both = jnp.dot(rows_ref[...], weight_ref[...], preferred_element_type=jnp.float32)
    one, two = both[:, : 2 * UNITS], both[:, 2 * UNITS :]
    low = lax.broadcasted_iota(jnp.int32, one.shape, 1) < UNITS
    gate = jnp.where(low, one, pltpu.roll(two, UNITS, 1))
    up = jnp.where(low, pltpu.roll(one, UNITS, 1), two)
    hidden_ref[...] = (gate / (1.0 + jnp.exp(-gate)) * up).astype(jnp.bfloat16)


def sum_kernel(capacity, where_ref, code_ref, mine_ref, other_ref, weight_ref, keep_ref, send_ref):
    rows = code_ref.shape[1]
    units = mine_ref.shape[1]
    me = where_ref[5]
    total = jnp.dot(
        mine_ref[...],
        weight_ref[pl.ds(pl.multiple_of(me * units, units), units), :],
        preferred_element_type=jnp.float32,
    )
    total += jnp.dot(
        other_ref[...],
        weight_ref[pl.ds(pl.multiple_of((1 - me) * units, units), units), :],
        preferred_element_type=jnp.float32,
    )
    result = total.astype(jnp.bfloat16)
    for b in range(4):
        code = code_ref[pl.ds(where_ref[b], 1), :]
        places = lax.broadcasted_iota(jnp.int32, (capacity, rows), 0)
        scale = (code & 255).astype(jnp.float32) * SCALE
        scaled = jnp.where(places == code >> 8, scale, 0.0).astype(jnp.bfloat16)
        mixed = lax.dot_general(
            scaled,
            result[b * capacity : (b + 1) * capacity],
            (((0,), (0,)), ((), ())),
            preferred_element_type=jnp.float32,
        )
        out_ref = keep_ref if b < 2 else send_ref
        out_ref[b % 2] = mixed.astype(jnp.bfloat16)


def pick_call(where, code, pieces, weight, capacity):
    rows, width = pieces[0].shape
    depth, columns = weight.shape
    tall = 4 * capacity
    pair = 4 * UNITS
    return pl.pallas_call(
        functools.partial(pick_kernel, capacity),
        grid=(columns // pair,),
        in_specs=[
            pl.BlockSpec(memory_space=pltpu.SMEM),
            pl.BlockSpec(code.shape, lambda i: (0, 0)),
            *[pl.BlockSpec((rows, width), lambda i: (0, 0), pipeline_mode=pl.Buffered(1)) for _ in pieces],
            pl.BlockSpec((depth, pair), lambda i: (0, i)),
        ],
        out_specs=pl.BlockSpec((tall, pair // 2), lambda i: (0, i)),
        out_shape=jax.ShapeDtypeStruct((tall, columns // 2), jnp.bfloat16),
        scratch_shapes=[pltpu.VMEM((tall, depth), jnp.bfloat16)],
        compiler_params=pltpu.CompilerParams(vmem_limit_bytes=28 * 1024 * 1024),
        cost_estimate=pl.CostEstimate(
            flops=2 * tall * depth * (columns + rows),
            bytes_accessed=2 * (8 * rows * width + weight.size + tall * columns // 2),
            transcendentals=tall * columns // 2,
        ),
        name="gate_up",
    )(where, code, *pieces, weight)


def sum_call(where, code, mine, other, weight, capacity):
    rows = code.shape[1]
    depth, wide = weight.shape
    tall, units = mine.shape
    step = 512
    return pl.pallas_call(
        functools.partial(sum_kernel, capacity),
        grid=(wide // step,),
        in_specs=[
            pl.BlockSpec(memory_space=pltpu.SMEM),
            pl.BlockSpec(code.shape, lambda i: (0, 0)),
            pl.BlockSpec((tall, units), lambda i: (0, 0), pipeline_mode=pl.Buffered(1)),
            pl.BlockSpec((tall, units), lambda i: (0, 0), pipeline_mode=pl.Buffered(1)),
            pl.BlockSpec((depth, step), lambda i: (0, i)),
        ],
        out_specs=[pl.BlockSpec((2, rows, step), lambda i: (0, 0, i))] * 2,
        out_shape=[jax.ShapeDtypeStruct((2, rows, wide), jnp.bfloat16)] * 2,
        compiler_params=pltpu.CompilerParams(vmem_limit_bytes=28 * 1024 * 1024),
        cost_estimate=pl.CostEstimate(
            flops=2 * wide * (tall * depth + 4 * rows * capacity),
            bytes_accessed=2 * (2 * mine.size + weight.size + 4 * rows * wide),
            transcendentals=0,
        ),
        name="down",
    )(where, code, mine, other, weight)


def codes_of(expert_ids, numerators, experts):
    rows = expert_ids.shape[0]
    named = expert_ids.T[None] == jnp.arange(experts, dtype=jnp.int32)[:, None, None]
    hits = jnp.any(named, axis=1)
    weight = jnp.sum(jnp.where(named, numerators.T[None], 0), axis=1)
    earlier = jnp.arange(rows)[:, None] < jnp.arange(rows)[None, :]
    rank = jnp.dot(hits.astype(jnp.bfloat16), earlier.astype(jnp.bfloat16), preferred_element_type=jnp.float32)
    return jnp.where(hits, rank.astype(jnp.int32) * 256 + weight, -1)


def shards(tokens, expert_ids, numerators, gate_up_weight, down_weight):
    rows, width = tokens.shape
    experts = lax.axis_size("expert")
    capacity = rows * expert_ids.shape[1] * 5 // (4 * experts)
    chips = experts // 2
    across = [[2 * i + c for i in range(chips)] for c in range(2)]
    pairs = [[2 * i, 2 * i + 1] for i in range(chips)]

    codes = lax.all_gather(codes_of(expert_ids, numerators, experts), "expert", axis=0)
    code = lax.dynamic_index_in_dim(codes, lax.axis_index("expert"), 1, keepdims=False)
    code = code.reshape(chips, 2, rows).swapaxes(0, 1).reshape(experts, rows)

    wide = lax.all_gather(tokens, "section", axis=0)
    half = lax.all_gather(wide, "expert", axis=0, axis_index_groups=across)
    whole = lax.all_gather(half, "expert", axis=0, axis_index_groups=pairs)
    whole = whole.reshape((experts,) + wide.shape)

    hidden = up_call(code, whole, gate_up_weight[0], capacity)
    hidden = lax.all_gather(hidden, "section", axis=0)
    part = down_call(code, hidden, down_weight[0], capacity)

    part = part.reshape(2, chips * rows, width)
    part = lax.psum_scatter(part, "expert", scatter_dimension=0, axis_index_groups=pairs, tiled=False)
    return lax.psum_scatter(part, "expert", scatter_dimension=0, axis_index_groups=across, tiled=True)


def pair_shards(tokens, expert_ids, numerators, gate_up_weight, down_weight):
    rows, width = tokens.shape
    experts = lax.axis_size("expert")
    layers = experts // 4
    capacity = rows * expert_ids.shape[1] * 5 // (4 * experts)
    axes = ("section", "expert")
    ring = [0, *range(1, layers, 2), *reversed(range(2, layers, 2))]
    following = {z: ring[(p + 1) % layers] for p, z in enumerate(ring)}

    def perm(place):
        moves = []
        for x in range(2):
            for z in range(layers):
                for y in range(2):
                    for c in range(2):
                        tx, tz, ty, tc = place(x, z, y, c)
                        moves.append(((x * layers + z) * 4 + y * 2 + c, (tx * layers + tz) * 4 + ty * 2 + tc))
        return moves

    onward = perm(lambda x, z, y, c: (x, following[z], y, c))
    first = perm(lambda x, z, y, c: (x ^ (1 - c), z, y ^ c, c))
    second = perm(lambda x, z, y, c: (x ^ c, z, y ^ (1 - c), c))
    sibling = perm(lambda x, z, y, c: (x, z, y, 1 - c))
    over_x = perm(lambda x, z, y, c: (1 - x, z, y, c))
    over_y = perm(lambda x, z, y, c: (x, z, 1 - y, c))

    def move(value, moves):
        return lax.ppermute(value, axes, moves)

    x, e = lax.axis_index("section"), lax.axis_index("expert")
    z, y, c = e // 4, e // 2 % 2, e % 2
    places = jnp.array([ring.index(i) for i in range(layers)], jnp.int32)
    code = lax.all_to_all(codes_of(expert_ids, numerators, experts), "expert", split_axis=0, concat_axis=0, tiled=True)

    def where(k):
        at = jnp.array(ring, jnp.int32)[(places[z] - k) % layers] * 4
        blocks = [at + (y ^ (i & 1)) * 2 + (c ^ (i >> 1)) for i in range(4)]
        spots = []
        for own in (0, 1):
            core = c ^ own
            base = 2 * own
            spots += [base, x]
            spots += [base + core, x ^ (1 - core)]
            spots += [base + 1 - core, x ^ core]
            spots += [base + 1, 1 - x]
        return jnp.stack([jnp.asarray(v, jnp.int32) for v in blocks + spots])

    wheres = [where(k) for k in range(layers)]
    shard, kept = tokens, []
    for k in range(layers):
        later = move(shard, onward) if k < layers - 1 else None
        a = move(shard, first)
        b = move(shard, second)
        d = move(a, second)
        pieces = [shard, a, b, d]
        pieces += [move(v, sibling) for v in pieces]
        mine = pick_call(wheres[k], code, pieces, gate_up_weight[0], capacity)
        other = move(mine, over_x)
        keep, send = sum_call(wheres[k], code, mine, other, down_weight[0], capacity)
        got = move(send, sibling)
        away = (keep[1].astype(jnp.float32) + got[1].astype(jnp.float32)).astype(jnp.bfloat16)
        back = move(away, over_y)
        kept.append((keep[0], got[0], back))
        shard = later

    total = None
    for k in [*range(1, layers), 0]:
        terms = [v.astype(jnp.float32) for v in kept[k]]
        if total is not None:
            terms.append(move(total, onward).astype(jnp.float32))
        total = functools.reduce(jnp.add, terms).astype(jnp.bfloat16)
    return total


def solution(mesh):
    in_specs = (
        P("expert", "section"),
        P("expert", None),
        P("expert", None),
        P("expert", None, "section"),
        P("expert", None, "section"),
    )
    out_specs = P("expert", "section")
    fits = mesh.shape["section"] == 2 and mesh.shape["expert"] % 4 == 0
    return jax.shard_map(pair_shards if fits else shards, mesh=mesh, in_specs=in_specs, out_specs=out_specs, check_vma=False)
```

```python
import functools

import jax
import jax.numpy as jnp
import numpy as np
from jax import lax
from jax.experimental import pallas as pl
from jax.experimental.pallas import tpu as pltpu
from jax.sharding import PartitionSpec as P

UNITS = 64
SCALE = 1.0 / 256.0
VMEM = 60 * 1024 * 1024


def group_of(capacity):
    count = 2
    while (count * capacity) % 16:
        count *= 2
    return count


def slot_map(code, group, capacity):
    line = jnp.concatenate(
        [code[i : i + 1] + jnp.where(code[i : i + 1] >= 0, i * capacity * 256, 0) for i in range(group)], axis=1
    )
    slot, weight = line >> 8, line & 255
    places = lax.broadcasted_iota(jnp.int32, (group * capacity, line.shape[1]), 0)
    return places == slot, weight


def up_kernel(group, capacity, code_ref, tokens_ref, weight_ref, hidden_ref, rows_ref):
    groups = tokens_ref.shape[0] // group
    sections, rows, width = tokens_ref.shape[1:]
    size = group * capacity
    for g in range(groups):
        onehot, _ = slot_map(code_ref[0, g * group : (g + 1) * group], group, capacity)
        onehot = onehot.astype(jnp.bfloat16)
        for s in range(sections):
            block = jnp.concatenate([tokens_ref[g * group + i, s] for i in range(group)], axis=0)
            picked = jnp.dot(onehot, block, preferred_element_type=jnp.float32)
            rows_ref[g * size : (g + 1) * size, s * width : (s + 1) * width] = picked.astype(jnp.bfloat16)
    columns = weight_ref.shape[1]
    pair = 4 * UNITS

    def products(first, count):
        return jnp.dot(rows_ref[...], weight_ref[:, pl.ds(first, count)], preferred_element_type=jnp.float32)

    def mix(gate, up):
        return (gate / (1.0 + jnp.exp(-gate)) * up).astype(jnp.bfloat16)

    @pl.loop(0, columns // pair)
    def _(p):
        both = products(pl.multiple_of(p * pair, pair), pair)
        one, two = both[:, : 2 * UNITS], both[:, 2 * UNITS :]
        low = lax.broadcasted_iota(jnp.int32, one.shape, 1) < UNITS
        gate = jnp.where(low, one, pltpu.roll(two, UNITS, 1))
        up = jnp.where(low, pltpu.roll(one, UNITS, 1), two)
        hidden_ref[:, pl.ds(pl.multiple_of(p * 2 * UNITS, 2 * UNITS), 2 * UNITS)] = mix(gate, up)

    if columns % pair:
        start = columns // pair * pair
        both = products(start, 2 * UNITS)
        hidden_ref[:, start // 2 :] = mix(both, pltpu.roll(both, UNITS, 1))[:, :UNITS]


def down_kernel(group, capacity, code_ref, hidden_ref, weight_ref, out_ref, result_ref):
    sections, _, units = hidden_ref.shape
    groups = code_ref.shape[1] // group
    size = group * capacity
    wide = weight_ref.shape[1]
    step = min(512, wide)

    @pl.loop(0, wide // step)
    def _(p):
        at = pl.ds(pl.multiple_of(p * step, step), step)
        total = jnp.dot(hidden_ref[0], weight_ref[0:units, at], preferred_element_type=jnp.float32)
        for s in range(1, sections):
            total += jnp.dot(
                hidden_ref[s], weight_ref[s * units : (s + 1) * units, at], preferred_element_type=jnp.float32
            )
        result_ref[...] = total.astype(jnp.bfloat16)
        for g in range(groups):
            onehot, weight = slot_map(code_ref[0, g * group : (g + 1) * group], group, capacity)
            scaled = jnp.where(onehot, weight.astype(jnp.float32) * SCALE, 0.0).astype(jnp.bfloat16)
            mixed = lax.dot_general(
                scaled,
                result_ref[g * size : (g + 1) * size],
                (((0,), (0,)), ((), ())),
                preferred_element_type=jnp.float32,
            )
            tall = scaled.shape[1]
            out_ref[g * tall : (g + 1) * tall, at] = mixed.astype(jnp.bfloat16)


def up_call(code, tokens, weight, capacity):
    blocks, sections, rows, width = tokens.shape
    group = group_of(capacity)
    take = min(blocks, 2 * group)
    depth, columns = weight.shape
    tall = take * capacity
    flops = 2 * blocks * capacity * depth * (columns + group * rows)
    return pl.pallas_call(
        functools.partial(up_kernel, group, capacity),
        grid=(blocks // take,),
        in_specs=[
            pl.BlockSpec((1, take, rows), lambda i: (i, 0, 0)),
            pl.BlockSpec((take, sections, rows, width), lambda i: (i, 0, 0, 0)),
            pl.BlockSpec((depth, columns), lambda i: (0, 0), pipeline_mode=pl.Buffered(1)),
        ],
        out_specs=pl.BlockSpec((tall, columns // 2), lambda i: (i, 0)),
        out_shape=jax.ShapeDtypeStruct((blocks * capacity, columns // 2), jnp.bfloat16),
        scratch_shapes=[pltpu.VMEM((tall, depth), jnp.bfloat16)],
        compiler_params=pltpu.CompilerParams(vmem_limit_bytes=48 * 1024 * 1024),
        cost_estimate=pl.CostEstimate(
            flops=flops, bytes_accessed=2 * (tokens.size + weight.size), transcendentals=blocks * capacity * columns // 2
        ),
        name="gate_up",
    )(code.reshape(blocks // take, take, rows), tokens, weight)


def down_call(code, hidden, weight, capacity):
    blocks, rows = code.shape
    sections, _, units = hidden.shape
    group = group_of(capacity)
    take = min(blocks, 2 * group)
    depth, wide = weight.shape
    tall = take * capacity
    return pl.pallas_call(
        functools.partial(down_kernel, group, capacity),
        grid=(blocks // take,),
        in_specs=[
            pl.BlockSpec((1, take, rows), lambda i: (i, 0, 0)),
            pl.BlockSpec((sections, tall, units), lambda i: (0, i, 0)),
            pl.BlockSpec((depth, wide), lambda i: (0, 0), pipeline_mode=pl.Buffered(1)),
        ],
        out_specs=pl.BlockSpec((take * rows, wide), lambda i: (i, 0)),
        out_shape=jax.ShapeDtypeStruct((blocks * rows, wide), jnp.bfloat16),
        scratch_shapes=[pltpu.VMEM((tall, min(512, wide)), jnp.bfloat16)],
        compiler_params=pltpu.CompilerParams(vmem_limit_bytes=48 * 1024 * 1024),
        cost_estimate=pl.CostEstimate(
            flops=2 * blocks * capacity * wide * (depth + group * rows),
            bytes_accessed=2 * (hidden.size + weight.size + blocks * rows * wide),
            transcendentals=0,
        ),
        name="down",
    )(code.reshape(blocks // take, take, rows), hidden, weight)


def pick_kernel(capacity, k, where_ref, code_ref, *refs):
    pieces, weight_ref = refs[:8], refs[8]
    hidden_ref, rows_ref = refs[-2:]
    rows, width = pieces[0].shape

    @pl.when(pl.program_id(0) == 0)
    def _():
        for i, piece in enumerate(pieces):
            block, section = where_ref[k, 4 + 2 * i], where_ref[k, 5 + 2 * i]
            code = code_ref[pl.ds(where_ref[k, block], 1), :]
            places = lax.broadcasted_iota(jnp.int32, (capacity, rows), 0)
            onehot = (places == code >> 8).astype(jnp.bfloat16)
            picked = jnp.dot(onehot, piece[...], preferred_element_type=jnp.float32)
            down = pl.ds(pl.multiple_of(block * capacity, capacity), capacity)
            rows_ref[down, pl.ds(pl.multiple_of(section * width, width), width)] = picked.astype(jnp.bfloat16)

    both = jnp.dot(rows_ref[...], weight_ref[...], preferred_element_type=jnp.float32)
    one, two = both[:, : 2 * UNITS], both[:, 2 * UNITS :]
    low = lax.broadcasted_iota(jnp.int32, one.shape, 1) < UNITS
    gate = jnp.where(low, one, pltpu.roll(two, UNITS, 1))
    up = jnp.where(low, pltpu.roll(one, UNITS, 1), two)
    hidden_ref[...] = (gate / (1.0 + jnp.exp(-gate)) * up).astype(jnp.bfloat16)


def sum_kernel(capacity, k, where_ref, code_ref, mine_ref, other_ref, weight_ref, keep_ref, send_ref):
    rows = code_ref.shape[1]
    units = mine_ref.shape[1]
    me = where_ref[k, 5]
    total = jnp.dot(
        mine_ref[...],
        weight_ref[pl.ds(pl.multiple_of(me * units, units), units), :],
        preferred_element_type=jnp.float32,
    )
    total += jnp.dot(
        other_ref[...],
        weight_ref[pl.ds(pl.multiple_of((1 - me) * units, units), units), :],
        preferred_element_type=jnp.float32,
    )
    result = total.astype(jnp.bfloat16)
    for b in range(4):
        code = code_ref[pl.ds(where_ref[k, b], 1), :]
        places = lax.broadcasted_iota(jnp.int32, (capacity, rows), 0)
        scale = (code & 255).astype(jnp.float32) * SCALE
        scaled = jnp.where(places == code >> 8, scale, 0.0).astype(jnp.bfloat16)
        mixed = lax.dot_general(
            scaled,
            result[b * capacity : (b + 1) * capacity],
            (((0,), (0,)), ((), ())),
            preferred_element_type=jnp.float32,
        )
        out_ref = keep_ref if b < 2 else send_ref
        out_ref[b % 2] = mixed.astype(jnp.bfloat16)


def pick_call(k, where, code, pieces, weight, earlier, capacity):
    rows, width = pieces[0].shape
    depth, columns = weight.shape
    tall = 4 * capacity
    pair = 4 * UNITS
    return pl.pallas_call(
        functools.partial(pick_kernel, capacity, k),
        grid=(columns // pair,),
        in_specs=[
            pl.BlockSpec(memory_space=pltpu.SMEM),
            pl.BlockSpec(code.shape, lambda i: (0, 0)),
            *[pl.BlockSpec((rows, width), lambda i: (0, 0), pipeline_mode=pl.Buffered(1)) for _ in pieces],
            pl.BlockSpec((depth, pair), lambda i: (0, i)),
            *[pl.BlockSpec(memory_space=pl.ANY) for _ in earlier],
        ],
        out_specs=pl.BlockSpec((tall, pair // 2), lambda i: (0, i)),
        out_shape=jax.ShapeDtypeStruct((tall, columns // 2), jnp.bfloat16),
        scratch_shapes=[pltpu.VMEM((tall, depth), jnp.bfloat16)],
        compiler_params=pltpu.CompilerParams(vmem_limit_bytes=VMEM),
        cost_estimate=pl.CostEstimate(
            flops=2 * tall * depth * (columns + rows),
            bytes_accessed=2 * (8 * rows * width + weight.size + tall * columns // 2),
            transcendentals=tall * columns // 2,
        ),
        name="gate_up",
    )(where, code, *pieces, weight, *earlier)


def sum_call(k, where, code, mine, other, weight, capacity):
    rows = code.shape[1]
    depth, wide = weight.shape
    tall, units = mine.shape
    step = 512
    return pl.pallas_call(
        functools.partial(sum_kernel, capacity, k),
        grid=(wide // step,),
        in_specs=[
            pl.BlockSpec(memory_space=pltpu.SMEM),
            pl.BlockSpec(code.shape, lambda i: (0, 0)),
            pl.BlockSpec((tall, units), lambda i: (0, 0), pipeline_mode=pl.Buffered(1)),
            pl.BlockSpec((tall, units), lambda i: (0, 0), pipeline_mode=pl.Buffered(1)),
            pl.BlockSpec((depth, step), lambda i: (0, i)),
        ],
        out_specs=[pl.BlockSpec((2, rows, step), lambda i: (0, 0, i))] * 2,
        out_shape=[jax.ShapeDtypeStruct((2, rows, wide), jnp.bfloat16)] * 2,
        compiler_params=pltpu.CompilerParams(vmem_limit_bytes=VMEM),
        cost_estimate=pl.CostEstimate(
            flops=2 * wide * (tall * depth + 4 * rows * capacity),
            bytes_accessed=2 * (2 * mine.size + weight.size + 4 * rows * wide),
            transcendentals=0,
        ),
        name="down",
    )(where, code, mine, other, weight)


def codes_of(expert_ids, numerators, experts):
    rows = expert_ids.shape[0]
    named = expert_ids.T[None] == jnp.arange(experts, dtype=jnp.int32)[:, None, None]
    hits = jnp.any(named, axis=1)
    weight = jnp.sum(jnp.where(named, numerators.T[None], 0), axis=1)
    earlier = jnp.arange(rows)[:, None] < jnp.arange(rows)[None, :]
    rank = jnp.dot(hits.astype(jnp.bfloat16), earlier.astype(jnp.bfloat16), preferred_element_type=jnp.float32)
    return jnp.where(hits, rank.astype(jnp.int32) * 256 + weight, -1)


def shards(tokens, expert_ids, numerators, gate_up_weight, down_weight):
    rows, width = tokens.shape
    experts = lax.axis_size("expert")
    capacity = rows * expert_ids.shape[1] * 5 // (4 * experts)
    chips = experts // 2
    across = [[2 * i + c for i in range(chips)] for c in range(2)]
    pairs = [[2 * i, 2 * i + 1] for i in range(chips)]

    codes = lax.all_gather(codes_of(expert_ids, numerators, experts), "expert", axis=0)
    code = lax.dynamic_index_in_dim(codes, lax.axis_index("expert"), 1, keepdims=False)
    code = code.reshape(chips, 2, rows).swapaxes(0, 1).reshape(experts, rows)

    wide = lax.all_gather(tokens, "section", axis=0)
    half = lax.all_gather(wide, "expert", axis=0, axis_index_groups=across)
    whole = lax.all_gather(half, "expert", axis=0, axis_index_groups=pairs)
    whole = whole.reshape((experts,) + wide.shape)

    hidden = up_call(code, whole, gate_up_weight[0], capacity)
    hidden = lax.all_gather(hidden, "section", axis=0)
    part = down_call(code, hidden, down_weight[0], capacity)

    part = part.reshape(2, chips * rows, width)
    part = lax.psum_scatter(part, "expert", scatter_dimension=0, axis_index_groups=pairs, tiled=False)
    return lax.psum_scatter(part, "expert", scatter_dimension=0, axis_index_groups=across, tiled=True)


def pair_shards(tokens, expert_ids, numerators, gate_up_weight, down_weight):
    rows, width = tokens.shape
    experts = lax.axis_size("expert")
    layers = experts // 4
    capacity = rows * expert_ids.shape[1] * 5 // (4 * experts)
    axes = ("section", "expert")
    ring = [0, *range(1, layers, 2), *reversed(range(2, layers, 2))]
    following = {z: ring[(p + 1) % layers] for p, z in enumerate(ring)}

    def perm(place):
        moves = []
        for x in range(2):
            for z in range(layers):
                for y in range(2):
                    for c in range(2):
                        tx, tz, ty, tc = place(x, z, y, c)
                        moves.append(((x * layers + z) * 4 + y * 2 + c, (tx * layers + tz) * 4 + ty * 2 + tc))
        return moves

    onward = perm(lambda x, z, y, c: (x, following[z], y, c))
    first = perm(lambda x, z, y, c: (x ^ (1 - c), z, y ^ c, c))
    second = perm(lambda x, z, y, c: (x ^ c, z, y ^ (1 - c), c))
    sibling = perm(lambda x, z, y, c: (x, z, y, 1 - c))
    over_x = perm(lambda x, z, y, c: (1 - x, z, y, c))
    over_y = perm(lambda x, z, y, c: (x, z, 1 - y, c))

    def move(value, moves):
        return lax.ppermute(value, axes, moves)

    table = np.zeros((2, layers, 2, 2, layers, 20), np.int32)
    for x, z, y, c, k in np.ndindex(2, layers, 2, 2, layers):
        at = ring[(ring.index(z) - k) % layers] * 4
        row = [at + (y ^ (i & 1)) * 2 + (c ^ (i >> 1)) for i in range(4)]
        for own in (0, 1):
            core, base = c ^ own, 2 * own
            row += [base, x, base + core, x ^ (1 - core), base + 1 - core, x ^ core, base + 1, 1 - x]
        table[x, z, y, c, k] = row
    device = lax.axis_index("section") * experts + lax.axis_index("expert")
    where = lax.dynamic_index_in_dim(jnp.asarray(table.reshape(2 * experts, layers, 20)), device, 0, keepdims=False)
    code = lax.all_to_all(codes_of(expert_ids, numerators, experts), "expert", split_axis=0, concat_axis=0, tiled=True)

    shard, kept, hiddens = tokens, [], []
    for k in range(layers):
        later = move(shard, onward) if k < layers - 1 else None
        a = move(shard, first)
        b = move(shard, second)
        if k == 0:
            a, code, where = lax.optimization_barrier((a, code, where))
        d = move(a, second)
        pieces = [shard, a, b, d]
        pieces += [move(v, sibling) for v in pieces]
        earlier = hiddens[-1:] + [keep for keep, _, _ in kept[-2:-1]]
        mine = pick_call(k, where, code, pieces, gate_up_weight[0], earlier, capacity)
        other = move(mine, over_x)
        keep, send = sum_call(k, where, code, mine, other, down_weight[0], capacity)
        got = move(send, sibling)
        away = (keep[1].astype(jnp.float32) + got[1].astype(jnp.float32)).astype(jnp.bfloat16)
        back = move(away, over_y)
        kept.append((keep, got, back))
        hiddens.append(mine)
        shard = later

    total = None
    for k in [*range(1, layers), 0]:
        keep, got, back = kept[k]
        terms = [v.astype(jnp.float32) for v in (keep[0], got[0], back)]
        if total is not None:
            terms.append(move(total, onward).astype(jnp.float32))
        total = functools.reduce(jnp.add, terms).astype(jnp.bfloat16)
    return total


def solution(mesh):
    in_specs = (
        P("expert", "section"),
        P("expert", None),
        P("expert", None),
        P("expert", None, "section"),
        P("expert", None, "section"),
    )
    out_specs = P("expert", "section")
    fits = mesh.shape["section"] == 2 and mesh.shape["expert"] % 4 == 0
    return jax.shard_map(pair_shards if fits else shards, mesh=mesh, in_specs=in_specs, out_specs=out_specs, check_vma=False)
```

```python
import functools

import jax
import jax.numpy as jnp
import numpy as np
from jax import lax
from jax.experimental import pallas as pl
from jax.experimental.pallas import tpu as pltpu
from jax.sharding import PartitionSpec as P

UNITS = 64
SCALE = 1.0 / 256.0
VMEM = 60 * 1024 * 1024


def group_of(capacity):
    count = 2
    while (count * capacity) % 16:
        count *= 2
    return count


def slot_map(code, group, capacity):
    line = jnp.concatenate(
        [code[i : i + 1] + jnp.where(code[i : i + 1] >= 0, i * capacity * 256, 0) for i in range(group)], axis=1
    )
    slot, weight = line >> 8, line & 255
    places = lax.broadcasted_iota(jnp.int32, (group * capacity, line.shape[1]), 0)
    return places == slot, weight


def up_kernel(group, capacity, code_ref, tokens_ref, weight_ref, hidden_ref, rows_ref):
    groups = tokens_ref.shape[0] // group
    sections, rows, width = tokens_ref.shape[1:]
    size = group * capacity
    for g in range(groups):
        onehot, _ = slot_map(code_ref[0, g * group : (g + 1) * group], group, capacity)
        onehot = onehot.astype(jnp.bfloat16)
        for s in range(sections):
            block = jnp.concatenate([tokens_ref[g * group + i, s] for i in range(group)], axis=0)
            picked = jnp.dot(onehot, block, preferred_element_type=jnp.float32)
            rows_ref[g * size : (g + 1) * size, s * width : (s + 1) * width] = picked.astype(jnp.bfloat16)
    columns = weight_ref.shape[1]
    pair = 4 * UNITS

    def products(first, count):
        return jnp.dot(rows_ref[...], weight_ref[:, pl.ds(first, count)], preferred_element_type=jnp.float32)

    def mix(gate, up):
        return (gate / (1.0 + jnp.exp(-gate)) * up).astype(jnp.bfloat16)

    @pl.loop(0, columns // pair)
    def _(p):
        both = products(pl.multiple_of(p * pair, pair), pair)
        one, two = both[:, : 2 * UNITS], both[:, 2 * UNITS :]
        low = lax.broadcasted_iota(jnp.int32, one.shape, 1) < UNITS
        gate = jnp.where(low, one, pltpu.roll(two, UNITS, 1))
        up = jnp.where(low, pltpu.roll(one, UNITS, 1), two)
        hidden_ref[:, pl.ds(pl.multiple_of(p * 2 * UNITS, 2 * UNITS), 2 * UNITS)] = mix(gate, up)

    if columns % pair:
        start = columns // pair * pair
        both = products(start, 2 * UNITS)
        hidden_ref[:, start // 2 :] = mix(both, pltpu.roll(both, UNITS, 1))[:, :UNITS]


def down_kernel(group, capacity, code_ref, hidden_ref, weight_ref, out_ref, result_ref):
    sections, _, units = hidden_ref.shape
    groups = code_ref.shape[1] // group
    size = group * capacity
    wide = weight_ref.shape[1]
    step = min(512, wide)

    @pl.loop(0, wide // step)
    def _(p):
        at = pl.ds(pl.multiple_of(p * step, step), step)
        total = jnp.dot(hidden_ref[0], weight_ref[0:units, at], preferred_element_type=jnp.float32)
        for s in range(1, sections):
            total += jnp.dot(
                hidden_ref[s], weight_ref[s * units : (s + 1) * units, at], preferred_element_type=jnp.float32
            )
        result_ref[...] = total.astype(jnp.bfloat16)
        for g in range(groups):
            onehot, weight = slot_map(code_ref[0, g * group : (g + 1) * group], group, capacity)
            scaled = jnp.where(onehot, weight.astype(jnp.float32) * SCALE, 0.0).astype(jnp.bfloat16)
            mixed = lax.dot_general(
                scaled,
                result_ref[g * size : (g + 1) * size],
                (((0,), (0,)), ((), ())),
                preferred_element_type=jnp.float32,
            )
            tall = scaled.shape[1]
            out_ref[g * tall : (g + 1) * tall, at] = mixed.astype(jnp.bfloat16)


def up_call(code, tokens, weight, capacity):
    blocks, sections, rows, width = tokens.shape
    group = group_of(capacity)
    take = min(blocks, 2 * group)
    depth, columns = weight.shape
    tall = take * capacity
    flops = 2 * blocks * capacity * depth * (columns + group * rows)
    return pl.pallas_call(
        functools.partial(up_kernel, group, capacity),
        grid=(blocks // take,),
        in_specs=[
            pl.BlockSpec((1, take, rows), lambda i: (i, 0, 0)),
            pl.BlockSpec((take, sections, rows, width), lambda i: (i, 0, 0, 0)),
            pl.BlockSpec((depth, columns), lambda i: (0, 0), pipeline_mode=pl.Buffered(1)),
        ],
        out_specs=pl.BlockSpec((tall, columns // 2), lambda i: (i, 0)),
        out_shape=jax.ShapeDtypeStruct((blocks * capacity, columns // 2), jnp.bfloat16),
        scratch_shapes=[pltpu.VMEM((tall, depth), jnp.bfloat16)],
        compiler_params=pltpu.CompilerParams(vmem_limit_bytes=48 * 1024 * 1024),
        cost_estimate=pl.CostEstimate(
            flops=flops, bytes_accessed=2 * (tokens.size + weight.size), transcendentals=blocks * capacity * columns // 2
        ),
        name="gate_up",
    )(code.reshape(blocks // take, take, rows), tokens, weight)


def down_call(code, hidden, weight, capacity):
    blocks, rows = code.shape
    sections, _, units = hidden.shape
    group = group_of(capacity)
    take = min(blocks, 2 * group)
    depth, wide = weight.shape
    tall = take * capacity
    return pl.pallas_call(
        functools.partial(down_kernel, group, capacity),
        grid=(blocks // take,),
        in_specs=[
            pl.BlockSpec((1, take, rows), lambda i: (i, 0, 0)),
            pl.BlockSpec((sections, tall, units), lambda i: (0, i, 0)),
            pl.BlockSpec((depth, wide), lambda i: (0, 0), pipeline_mode=pl.Buffered(1)),
        ],
        out_specs=pl.BlockSpec((take * rows, wide), lambda i: (i, 0)),
        out_shape=jax.ShapeDtypeStruct((blocks * rows, wide), jnp.bfloat16),
        scratch_shapes=[pltpu.VMEM((tall, min(512, wide)), jnp.bfloat16)],
        compiler_params=pltpu.CompilerParams(vmem_limit_bytes=48 * 1024 * 1024),
        cost_estimate=pl.CostEstimate(
            flops=2 * blocks * capacity * wide * (depth + group * rows),
            bytes_accessed=2 * (hidden.size + weight.size + blocks * rows * wide),
            transcendentals=0,
        ),
        name="down",
    )(code.reshape(blocks // take, take, rows), hidden, weight)


def onehot_of(code, capacity):
    return lax.broadcasted_iota(jnp.int32, (capacity, code.shape[1]), 0) == code >> 8


def pick_kernel(capacity, k, where_ref, code_ref, *refs):
    pairs, weight_hbm = refs[:4], refs[4]
    hidden_ref, pair_ref, weight_ref, rows_ref, sems = refs[-5:]
    rows, width = pairs[0].shape[1:]
    span = 4 * UNITS
    spans = weight_hbm.shape[1] // span

    def weight_copy(j):
        at = pl.ds(pl.multiple_of(j * span, span), span)
        return pltpu.make_async_copy(weight_hbm.at[:, at], weight_ref.at[:, at], sems.at[4 + j])

    copies = [pltpu.make_async_copy(v, pair_ref.at[i], sems.at[i]) for i, v in enumerate(pairs)]
    for copy in copies:
        copy.start()
    for j in range(spans):
        weight_copy(j).start()
    for i, copy in enumerate(copies):
        copy.wait()
        for h in range(2):
            spot = 4 + 2 * (2 * i + h)
            block, section = where_ref[k, spot], where_ref[k, spot + 1]
            onehot = onehot_of(code_ref[pl.ds(where_ref[k, block], 1), :], capacity).astype(jnp.bfloat16)
            picked = jnp.dot(onehot, pair_ref[i, h], preferred_element_type=jnp.float32)
            down = pl.ds(pl.multiple_of(block * capacity, capacity), capacity)
            rows_ref[down, pl.ds(pl.multiple_of(section * width, width), width)] = picked.astype(jnp.bfloat16)

    @pl.loop(0, spans)
    def _(j):
        weight_copy(j).wait()
        at = pl.ds(pl.multiple_of(j * span, span), span)
        both = jnp.dot(rows_ref[...], weight_ref[:, at], preferred_element_type=jnp.float32)
        one, two = both[:, : 2 * UNITS], both[:, 2 * UNITS :]
        low = lax.broadcasted_iota(jnp.int32, one.shape, 1) < UNITS
        gate = jnp.where(low, one, pltpu.roll(two, UNITS, 1))
        up = jnp.where(low, pltpu.roll(one, UNITS, 1), two)
        half = pl.ds(pl.multiple_of(j * 2 * UNITS, 2 * UNITS), 2 * UNITS)
        hidden_ref[:, half] = (gate / (1.0 + jnp.exp(-gate)) * up).astype(jnp.bfloat16)


def sum_kernel(capacity, k, where_ref, code_ref, mine_hbm, other_hbm, weight_hbm, keep_hbm, send_hbm, *refs):
    hidden_ref, weight_ref, out_ref, sems = refs
    rows = code_ref.shape[1]
    units = mine_hbm.shape[1]
    span = 512
    spans = weight_hbm.shape[1] // span

    def weight_copy(j):
        at = pl.ds(pl.multiple_of(j * span, span), span)
        return pltpu.make_async_copy(weight_hbm.at[:, at], weight_ref.at[:, at], sems.at[2 + j])

    def out_copy(j, i, to):
        at = pl.ds(pl.multiple_of(j * span, span), span)
        sem = sems.at[2 + spans + 2 * j + i]
        return pltpu.make_async_copy(out_ref.at[pl.ds(2 * i, 2), :, at], to.at[:, :, at], sem)

    copies = [pltpu.make_async_copy(v, hidden_ref.at[i], sems.at[i]) for i, v in enumerate((mine_hbm, other_hbm))]
    for copy in copies:
        copy.start()
    for j in range(spans):
        weight_copy(j).start()
    scaled = []
    for b in range(4):
        code = code_ref[pl.ds(where_ref[k, b], 1), :]
        scale = (code & 255).astype(jnp.float32) * SCALE
        scaled.append(jnp.where(onehot_of(code, capacity), scale, 0.0).astype(jnp.bfloat16))
    me = where_ref[k, 5]
    mine_at = pl.ds(pl.multiple_of(me * units, units), units)
    other_at = pl.ds(pl.multiple_of((1 - me) * units, units), units)
    for copy in copies:
        copy.wait()

    @pl.loop(0, spans)
    def _(j):
        weight_copy(j).wait()
        at = pl.ds(pl.multiple_of(j * span, span), span)
        total = jnp.dot(hidden_ref[0], weight_ref[mine_at, at], preferred_element_type=jnp.float32)
        total += jnp.dot(hidden_ref[1], weight_ref[other_at, at], preferred_element_type=jnp.float32)
        result = total.astype(jnp.bfloat16)
        for b in range(4):
            mixed = lax.dot_general(
                scaled[b],
                result[b * capacity : (b + 1) * capacity],
                (((0,), (0,)), ((), ())),
                preferred_element_type=jnp.float32,
            )
            out_ref[b, :, at] = mixed.astype(jnp.bfloat16)
        out_copy(j, 0, keep_hbm).start()
        out_copy(j, 1, send_hbm).start()

    for j in range(spans):
        out_copy(j, 0, keep_hbm).wait()
        out_copy(j, 1, send_hbm).wait()


def pick_call(k, where, code, pairs, weight, earlier, capacity):
    _, rows, width = pairs[0].shape
    depth, columns = weight.shape
    tall = 4 * capacity
    anywhere = pl.BlockSpec(memory_space=pl.ANY)
    return pl.pallas_call(
        functools.partial(pick_kernel, capacity, k),
        in_specs=[
            pl.BlockSpec(memory_space=pltpu.SMEM),
            pl.BlockSpec(memory_space=pltpu.VMEM),
            *[anywhere] * (5 + len(earlier)),
        ],
        out_specs=pl.BlockSpec(memory_space=pltpu.VMEM),
        out_shape=jax.ShapeDtypeStruct((tall, columns // 2), jnp.bfloat16),
        scratch_shapes=[
            pltpu.VMEM((4, 2, rows, width), jnp.bfloat16),
            pltpu.VMEM((depth, columns), jnp.bfloat16),
            pltpu.VMEM((tall, depth), jnp.bfloat16),
            pltpu.SemaphoreType.DMA((4 + columns // (4 * UNITS),)),
        ],
        compiler_params=pltpu.CompilerParams(vmem_limit_bytes=VMEM),
        cost_estimate=pl.CostEstimate(
            flops=2 * tall * depth * (columns + rows),
            bytes_accessed=2 * (8 * rows * width + weight.size + tall * columns // 2),
            transcendentals=tall * columns // 2,
        ),
        name="gate_up",
    )(where, code, *pairs, weight, *earlier)


def sum_call(k, where, code, mine, other, weight, capacity):
    rows = code.shape[1]
    depth, wide = weight.shape
    tall, units = mine.shape
    anywhere = pl.BlockSpec(memory_space=pl.ANY)
    return pl.pallas_call(
        functools.partial(sum_kernel, capacity, k),
        in_specs=[
            pl.BlockSpec(memory_space=pltpu.SMEM),
            pl.BlockSpec(memory_space=pltpu.VMEM),
            *[anywhere] * 3,
        ],
        out_specs=[anywhere] * 2,
        out_shape=[jax.ShapeDtypeStruct((2, rows, wide), jnp.bfloat16)] * 2,
        scratch_shapes=[
            pltpu.VMEM((2, tall, units), jnp.bfloat16),
            pltpu.VMEM((depth, wide), jnp.bfloat16),
            pltpu.VMEM((4, rows, wide), jnp.bfloat16),
            pltpu.SemaphoreType.DMA((2 + 3 * (wide // 512),)),
        ],
        compiler_params=pltpu.CompilerParams(vmem_limit_bytes=VMEM),
        cost_estimate=pl.CostEstimate(
            flops=2 * wide * (tall * depth + 4 * rows * capacity),
            bytes_accessed=2 * (2 * mine.size + weight.size + 4 * rows * wide),
            transcendentals=0,
        ),
        name="down",
    )(where, code, mine, other, weight)


def codes_of(expert_ids, numerators, experts):
    rows = expert_ids.shape[0]
    named = expert_ids.T[None] == jnp.arange(experts, dtype=jnp.int32)[:, None, None]
    hits = jnp.any(named, axis=1)
    weight = jnp.sum(jnp.where(named, numerators.T[None], 0), axis=1)
    earlier = jnp.arange(rows)[:, None] < jnp.arange(rows)[None, :]
    rank = jnp.dot(hits.astype(jnp.bfloat16), earlier.astype(jnp.bfloat16), preferred_element_type=jnp.float32)
    return jnp.where(hits, rank.astype(jnp.int32) * 256 + weight, -1)


def shards(tokens, expert_ids, numerators, gate_up_weight, down_weight):
    rows, width = tokens.shape
    experts = lax.axis_size("expert")
    capacity = rows * expert_ids.shape[1] * 5 // (4 * experts)
    chips = experts // 2
    across = [[2 * i + c for i in range(chips)] for c in range(2)]
    pairs = [[2 * i, 2 * i + 1] for i in range(chips)]

    codes = lax.all_gather(codes_of(expert_ids, numerators, experts), "expert", axis=0)
    code = lax.dynamic_index_in_dim(codes, lax.axis_index("expert"), 1, keepdims=False)
    code = code.reshape(chips, 2, rows).swapaxes(0, 1).reshape(experts, rows)

    wide = lax.all_gather(tokens, "section", axis=0)
    half = lax.all_gather(wide, "expert", axis=0, axis_index_groups=across)
    whole = lax.all_gather(half, "expert", axis=0, axis_index_groups=pairs)
    whole = whole.reshape((experts,) + wide.shape)

    hidden = up_call(code, whole, gate_up_weight[0], capacity)
    hidden = lax.all_gather(hidden, "section", axis=0)
    part = down_call(code, hidden, down_weight[0], capacity)

    part = part.reshape(2, chips * rows, width)
    part = lax.psum_scatter(part, "expert", scatter_dimension=0, axis_index_groups=pairs, tiled=False)
    return lax.psum_scatter(part, "expert", scatter_dimension=0, axis_index_groups=across, tiled=True)


def pair_shards(tokens, expert_ids, numerators, gate_up_weight, down_weight):
    rows, width = tokens.shape
    experts = lax.axis_size("expert")
    layers = experts // 4
    capacity = rows * expert_ids.shape[1] * 5 // (4 * experts)
    axes = ("section", "expert")
    ring = [0, *range(1, layers, 2), *reversed(range(2, layers, 2))]
    following = {z: ring[(p + 1) % layers] for p, z in enumerate(ring)}

    def perm(place):
        moves = []
        for x in range(2):
            for z in range(layers):
                for y in range(2):
                    for c in range(2):
                        tx, tz, ty, tc = place(x, z, y, c)
                        moves.append(((x * layers + z) * 4 + y * 2 + c, (tx * layers + tz) * 4 + ty * 2 + tc))
        return moves

    onward = perm(lambda x, z, y, c: (x, following[z], y, c))
    first = perm(lambda x, z, y, c: (x ^ (1 - c), z, y ^ c, c))
    second = perm(lambda x, z, y, c: (x ^ c, z, y ^ (1 - c), c))
    sibling = perm(lambda x, z, y, c: (x, z, y, 1 - c))
    over_x = perm(lambda x, z, y, c: (1 - x, z, y, c))
    over_y = perm(lambda x, z, y, c: (x, z, 1 - y, c))

    def move(value, moves):
        return lax.ppermute(value, axes, moves)

    table = np.zeros((2, layers, 2, 2, layers, 20), np.int32)
    for x, z, y, c, k in np.ndindex(2, layers, 2, 2, layers):
        at = ring[(ring.index(z) - k) % layers] * 4
        row = [at + (y ^ (i & 1)) * 2 + (c ^ (i >> 1)) for i in range(4)]
        for own in (0, 1):
            core, base = c ^ own, 2 * own
            row += [base, x, base + core, x ^ (1 - core), base + 1 - core, x ^ core, base + 1, 1 - x]
        table[x, z, y, c, k] = row
    device = lax.axis_index("section") * experts + lax.axis_index("expert")
    where = lax.dynamic_index_in_dim(jnp.asarray(table.reshape(2 * experts, layers, 20)), device, 0, keepdims=False)
    code = lax.all_to_all(codes_of(expert_ids, numerators, experts), "expert", split_axis=0, concat_axis=0, tiled=True)

    kept, hiddens = [], []
    near = move(tokens, first)
    later = move(tokens, onward)
    near, code, where = lax.optimization_barrier((near, code, where))
    near_later = move(near, onward)
    pair = jnp.stack([tokens, near])
    for k in range(layers):
        if k == 0:
            after = jnp.stack([later, near_later])
        else:
            after = move(pair, onward) if k < layers - 1 else None
        cross = move(pair, second)
        pairs = [pair, cross, move(pair, sibling), move(cross, sibling)]
        earlier = hiddens[-1:] + [keep for keep, _, _ in kept[-2:-1]]
        mine = pick_call(k, where, code, pairs, gate_up_weight[0], earlier, capacity)
        other = move(mine, over_x)
        keep, send = sum_call(k, where, code, mine, other, down_weight[0], capacity)
        got = move(send, sibling)
        away = (keep[1].astype(jnp.float32) + got[1].astype(jnp.float32)).astype(jnp.bfloat16)
        back = move(away, over_y)
        kept.append((keep, got, back))
        hiddens.append(mine)
        pair = after

    total = None
    for k in [*range(1, layers), 0]:
        keep, got, back = kept[k]
        terms = [v.astype(jnp.float32) for v in (keep[0], got[0], back)]
        if total is not None:
            terms.append(move(total, onward).astype(jnp.float32))
        total = functools.reduce(jnp.add, terms).astype(jnp.bfloat16)
    return total


def solution(mesh):
    in_specs = (
        P("expert", "section"),
        P("expert", None),
        P("expert", None),
        P("expert", None, "section"),
        P("expert", None, "section"),
    )
    out_specs = P("expert", "section")
    fits = mesh.shape["section"] == 2 and mesh.shape["expert"] % 4 == 0
    return jax.shard_map(pair_shards if fits else shards, mesh=mesh, in_specs=in_specs, out_specs=out_specs, check_vma=False)
```

```python
import functools

import jax
import jax.numpy as jnp
import numpy as np
from jax import lax
from jax.experimental import pallas as pl
from jax.experimental.pallas import tpu as pltpu
from jax.sharding import PartitionSpec as P

UNITS = 64
SCALE = 1.0 / 256.0
VMEM = 60 * 1024 * 1024


def group_of(capacity):
    count = 2
    while (count * capacity) % 16:
        count *= 2
    return count


def slot_map(code, group, capacity):
    line = jnp.concatenate(
        [code[i : i + 1] + jnp.where(code[i : i + 1] >= 0, i * capacity * 256, 0) for i in range(group)], axis=1
    )
    slot, weight = line >> 8, line & 255
    places = lax.broadcasted_iota(jnp.int32, (group * capacity, line.shape[1]), 0)
    return places == slot, weight


def up_kernel(group, capacity, code_ref, tokens_ref, weight_ref, hidden_ref, rows_ref):
    groups = tokens_ref.shape[0] // group
    sections, rows, width = tokens_ref.shape[1:]
    size = group * capacity
    for g in range(groups):
        onehot, _ = slot_map(code_ref[0, g * group : (g + 1) * group], group, capacity)
        onehot = onehot.astype(jnp.bfloat16)
        for s in range(sections):
            block = jnp.concatenate([tokens_ref[g * group + i, s] for i in range(group)], axis=0)
            picked = jnp.dot(onehot, block, preferred_element_type=jnp.float32)
            rows_ref[g * size : (g + 1) * size, s * width : (s + 1) * width] = picked.astype(jnp.bfloat16)
    columns = weight_ref.shape[1]
    pair = 4 * UNITS

    def products(first, count):
        return jnp.dot(rows_ref[...], weight_ref[:, pl.ds(first, count)], preferred_element_type=jnp.float32)

    def mix(gate, up):
        return (gate / (1.0 + jnp.exp(-gate)) * up).astype(jnp.bfloat16)

    @pl.loop(0, columns // pair)
    def _(p):
        both = products(pl.multiple_of(p * pair, pair), pair)
        one, two = both[:, : 2 * UNITS], both[:, 2 * UNITS :]
        low = lax.broadcasted_iota(jnp.int32, one.shape, 1) < UNITS
        gate = jnp.where(low, one, pltpu.roll(two, UNITS, 1))
        up = jnp.where(low, pltpu.roll(one, UNITS, 1), two)
        hidden_ref[:, pl.ds(pl.multiple_of(p * 2 * UNITS, 2 * UNITS), 2 * UNITS)] = mix(gate, up)

    if columns % pair:
        start = columns // pair * pair
        both = products(start, 2 * UNITS)
        hidden_ref[:, start // 2 :] = mix(both, pltpu.roll(both, UNITS, 1))[:, :UNITS]


def down_kernel(group, capacity, code_ref, hidden_ref, weight_ref, out_ref, result_ref):
    sections, _, units = hidden_ref.shape
    groups = code_ref.shape[1] // group
    size = group * capacity
    wide = weight_ref.shape[1]
    step = min(512, wide)

    @pl.loop(0, wide // step)
    def _(p):
        at = pl.ds(pl.multiple_of(p * step, step), step)
        total = jnp.dot(hidden_ref[0], weight_ref[0:units, at], preferred_element_type=jnp.float32)
        for s in range(1, sections):
            total += jnp.dot(
                hidden_ref[s], weight_ref[s * units : (s + 1) * units, at], preferred_element_type=jnp.float32
            )
        result_ref[...] = total.astype(jnp.bfloat16)
        for g in range(groups):
            onehot, weight = slot_map(code_ref[0, g * group : (g + 1) * group], group, capacity)
            scaled = jnp.where(onehot, weight.astype(jnp.float32) * SCALE, 0.0).astype(jnp.bfloat16)
            mixed = lax.dot_general(
                scaled,
                result_ref[g * size : (g + 1) * size],
                (((0,), (0,)), ((), ())),
                preferred_element_type=jnp.float32,
            )
            tall = scaled.shape[1]
            out_ref[g * tall : (g + 1) * tall, at] = mixed.astype(jnp.bfloat16)


def up_call(code, tokens, weight, capacity):
    blocks, sections, rows, width = tokens.shape
    group = group_of(capacity)
    take = min(blocks, 2 * group)
    depth, columns = weight.shape
    tall = take * capacity
    flops = 2 * blocks * capacity * depth * (columns + group * rows)
    return pl.pallas_call(
        functools.partial(up_kernel, group, capacity),
        grid=(blocks // take,),
        in_specs=[
            pl.BlockSpec((1, take, rows), lambda i: (i, 0, 0)),
            pl.BlockSpec((take, sections, rows, width), lambda i: (i, 0, 0, 0)),
            pl.BlockSpec((depth, columns), lambda i: (0, 0), pipeline_mode=pl.Buffered(1)),
        ],
        out_specs=pl.BlockSpec((tall, columns // 2), lambda i: (i, 0)),
        out_shape=jax.ShapeDtypeStruct((blocks * capacity, columns // 2), jnp.bfloat16),
        scratch_shapes=[pltpu.VMEM((tall, depth), jnp.bfloat16)],
        compiler_params=pltpu.CompilerParams(vmem_limit_bytes=48 * 1024 * 1024),
        cost_estimate=pl.CostEstimate(
            flops=flops, bytes_accessed=2 * (tokens.size + weight.size), transcendentals=blocks * capacity * columns // 2
        ),
        name="gate_up",
    )(code.reshape(blocks // take, take, rows), tokens, weight)


def down_call(code, hidden, weight, capacity):
    blocks, rows = code.shape
    sections, _, units = hidden.shape
    group = group_of(capacity)
    take = min(blocks, 2 * group)
    depth, wide = weight.shape
    tall = take * capacity
    return pl.pallas_call(
        functools.partial(down_kernel, group, capacity),
        grid=(blocks // take,),
        in_specs=[
            pl.BlockSpec((1, take, rows), lambda i: (i, 0, 0)),
            pl.BlockSpec((sections, tall, units), lambda i: (0, i, 0)),
            pl.BlockSpec((depth, wide), lambda i: (0, 0), pipeline_mode=pl.Buffered(1)),
        ],
        out_specs=pl.BlockSpec((take * rows, wide), lambda i: (i, 0)),
        out_shape=jax.ShapeDtypeStruct((blocks * rows, wide), jnp.bfloat16),
        scratch_shapes=[pltpu.VMEM((tall, min(512, wide)), jnp.bfloat16)],
        compiler_params=pltpu.CompilerParams(vmem_limit_bytes=48 * 1024 * 1024),
        cost_estimate=pl.CostEstimate(
            flops=2 * blocks * capacity * wide * (depth + group * rows),
            bytes_accessed=2 * (hidden.size + weight.size + blocks * rows * wide),
            transcendentals=0,
        ),
        name="down",
    )(code.reshape(blocks // take, take, rows), hidden, weight)


def block_codes(k, own, where_ref, code_ref):
    return jnp.concatenate([code_ref[pl.ds(where_ref[k, 2 * own + i], 1), :] for i in range(2)], axis=0)


def pick_kernel(capacity, k, where_ref, code_ref, *refs):
    pairs, weight_hbm = refs[:4], refs[4]
    hidden_ref, pair_ref, weight_ref, rows_ref, sems = refs[-5:]
    rows, width = pairs[0].shape[1:]
    span = 8 * UNITS
    spans = weight_hbm.shape[1] // span
    x, c = where_ref[k, 4], where_ref[k, 5]

    def weight_copy(j):
        at = pl.ds(pl.multiple_of(j * span, span), span)
        return pltpu.make_async_copy(weight_hbm.at[:, at], weight_ref.at[:, at], sems.at[4 + j])

    copies = [pltpu.make_async_copy(v, pair_ref.at[pl.ds(2 * i, 2)], sems.at[i]) for i, v in enumerate(pairs)]
    for copy in copies:
        copy.start()
    for j in range(spans):
        weight_copy(j).start()
    for own in range(2):
        core = c ^ own
        onehot, _ = slot_map(block_codes(k, own, where_ref, code_ref), 2, capacity)
        onehot = onehot.astype(jnp.bfloat16)
        copies[2 * own].wait()
        copies[2 * own + 1].wait()
        for section, near, far in ((x, 0, 2 - core), (1 - x, 1 + core, 3)):
            block = jnp.concatenate([pair_ref[4 * own + near], pair_ref[4 * own + far]], axis=0)
            picked = jnp.dot(onehot, block, preferred_element_type=jnp.float32)
            at = pl.ds(pl.multiple_of(section * width, width), width)
            rows_ref[2 * own * capacity : 2 * (own + 1) * capacity, at] = picked.astype(jnp.bfloat16)

    @pl.loop(0, spans)
    def _(j):
        weight_copy(j).wait()
        at = pl.ds(pl.multiple_of(j * span, span), span)
        both = jnp.dot(rows_ref[...], weight_ref[:, at], preferred_element_type=jnp.float32)
        for p in range(2):
            one, two = both[:, 4 * p * UNITS : (4 * p + 2) * UNITS], both[:, (4 * p + 2) * UNITS : 4 * (p + 1) * UNITS]
            low = lax.broadcasted_iota(jnp.int32, one.shape, 1) < UNITS
            gate = jnp.where(low, one, pltpu.roll(two, UNITS, 1))
            up = jnp.where(low, pltpu.roll(one, UNITS, 1), two)
            half = pl.ds(pl.multiple_of((2 * j + p) * 2 * UNITS, 2 * UNITS), 2 * UNITS)
            hidden_ref[:, half] = (gate / (1.0 + jnp.exp(-gate)) * up).astype(jnp.bfloat16)


def sum_kernel(capacity, k, where_ref, code_ref, *refs):
    mine_hbm, other_hbm, weight_hbm = refs[:3]
    keep_hbm, send_hbm, hidden_ref, weight_ref, out_ref, sems = refs[-6:]
    rows = code_ref.shape[1]
    units = mine_hbm.shape[1]
    span = 512
    spans = weight_hbm.shape[1] // span

    def weight_copy(j):
        at = pl.ds(pl.multiple_of(j * span, span), span)
        return pltpu.make_async_copy(weight_hbm.at[:, at], weight_ref.at[:, at], sems.at[2 + j])

    def out_copy(j, i, to):
        at = pl.ds(pl.multiple_of(j * span, span), span)
        sem = sems.at[2 + spans + 2 * j + i]
        return pltpu.make_async_copy(out_ref.at[pl.ds(2 * i, 2), :, at], to.at[:, :, at], sem)

    copies = [pltpu.make_async_copy(v, hidden_ref.at[i], sems.at[i]) for i, v in enumerate((mine_hbm, other_hbm))]
    for copy in copies:
        copy.start()
    for j in range(spans):
        weight_copy(j).start()
    scaled = []
    for own in range(2):
        onehot, weight = slot_map(block_codes(k, own, where_ref, code_ref), 2, capacity)
        scaled.append(jnp.where(onehot, weight.astype(jnp.float32) * SCALE, 0.0).astype(jnp.bfloat16))
    me = where_ref[k, 4]
    mine_at = pl.ds(pl.multiple_of(me * units, units), units)
    other_at = pl.ds(pl.multiple_of((1 - me) * units, units), units)
    for copy in copies:
        copy.wait()

    @pl.loop(0, spans)
    def _(j):
        weight_copy(j).wait()
        at = pl.ds(pl.multiple_of(j * span, span), span)
        total = jnp.dot(hidden_ref[0], weight_ref[mine_at, at], preferred_element_type=jnp.float32)
        total += jnp.dot(hidden_ref[1], weight_ref[other_at, at], preferred_element_type=jnp.float32)
        result = total.astype(jnp.bfloat16)
        for own in range(2):
            mixed = lax.dot_general(
                scaled[own],
                result[2 * own * capacity : 2 * (own + 1) * capacity],
                (((0,), (0,)), ((), ())),
                preferred_element_type=jnp.float32,
            )
            out_ref[2 * own : 2 * own + 2, :, at] = mixed.astype(jnp.bfloat16).reshape(2, rows, span)
        out_copy(j, 0, keep_hbm).start()
        out_copy(j, 1, send_hbm).start()

    for j in range(spans):
        out_copy(j, 0, keep_hbm).wait()
        out_copy(j, 1, send_hbm).wait()


def pick_call(k, where, code, pairs, weight, earlier, capacity):
    _, rows, width = pairs[0].shape
    depth, columns = weight.shape
    tall = 4 * capacity
    anywhere = pl.BlockSpec(memory_space=pl.ANY)
    return pl.pallas_call(
        functools.partial(pick_kernel, capacity, k),
        in_specs=[
            pl.BlockSpec(memory_space=pltpu.SMEM),
            pl.BlockSpec(memory_space=pltpu.VMEM),
            *[anywhere] * (5 + len(earlier)),
        ],
        out_specs=pl.BlockSpec(memory_space=pltpu.VMEM),
        out_shape=jax.ShapeDtypeStruct((tall, columns // 2), jnp.bfloat16),
        scratch_shapes=[
            pltpu.VMEM((8, rows, width), jnp.bfloat16),
            pltpu.VMEM((depth, columns), jnp.bfloat16),
            pltpu.VMEM((tall, depth), jnp.bfloat16),
            pltpu.SemaphoreType.DMA((4 + columns // (8 * UNITS),)),
        ],
        compiler_params=pltpu.CompilerParams(vmem_limit_bytes=VMEM),
        cost_estimate=pl.CostEstimate(
            flops=2 * tall * depth * (columns + rows),
            bytes_accessed=2 * (8 * rows * width + weight.size + tall * columns // 2),
            transcendentals=tall * columns // 2,
        ),
        name="gate_up",
    )(where, code, *pairs, weight, *earlier)


def sum_call(k, where, code, mine, other, weight, earlier, capacity):
    rows = code.shape[1]
    depth, wide = weight.shape
    tall, units = mine.shape
    anywhere = pl.BlockSpec(memory_space=pl.ANY)
    return pl.pallas_call(
        functools.partial(sum_kernel, capacity, k),
        in_specs=[
            pl.BlockSpec(memory_space=pltpu.SMEM),
            pl.BlockSpec(memory_space=pltpu.VMEM),
            *[anywhere] * (3 + len(earlier)),
        ],
        out_specs=[anywhere] * 2,
        out_shape=[jax.ShapeDtypeStruct((2, rows, wide), jnp.bfloat16)] * 2,
        scratch_shapes=[
            pltpu.VMEM((2, tall, units), jnp.bfloat16),
            pltpu.VMEM((depth, wide), jnp.bfloat16),
            pltpu.VMEM((4, rows, wide), jnp.bfloat16),
            pltpu.SemaphoreType.DMA((2 + 3 * (wide // 512),)),
        ],
        compiler_params=pltpu.CompilerParams(vmem_limit_bytes=VMEM),
        cost_estimate=pl.CostEstimate(
            flops=2 * wide * (tall * depth + 4 * rows * capacity),
            bytes_accessed=2 * (2 * mine.size + weight.size + 4 * rows * wide),
            transcendentals=0,
        ),
        name="down",
    )(where, code, mine, other, weight, *earlier)


def codes_of(expert_ids, numerators, experts):
    rows = expert_ids.shape[0]
    named = expert_ids.T[None] == jnp.arange(experts, dtype=jnp.int32)[:, None, None]
    hits = jnp.any(named, axis=1)
    weight = jnp.sum(jnp.where(named, numerators.T[None], 0), axis=1)
    earlier = jnp.arange(rows)[:, None] < jnp.arange(rows)[None, :]
    rank = jnp.dot(hits.astype(jnp.bfloat16), earlier.astype(jnp.bfloat16), preferred_element_type=jnp.float32)
    return jnp.where(hits, rank.astype(jnp.int32) * 256 + weight, -1)


def shards(tokens, expert_ids, numerators, gate_up_weight, down_weight):
    rows, width = tokens.shape
    experts = lax.axis_size("expert")
    capacity = rows * expert_ids.shape[1] * 5 // (4 * experts)
    chips = experts // 2
    across = [[2 * i + c for i in range(chips)] for c in range(2)]
    pairs = [[2 * i, 2 * i + 1] for i in range(chips)]

    codes = lax.all_gather(codes_of(expert_ids, numerators, experts), "expert", axis=0)
    code = lax.dynamic_index_in_dim(codes, lax.axis_index("expert"), 1, keepdims=False)
    code = code.reshape(chips, 2, rows).swapaxes(0, 1).reshape(experts, rows)

    wide = lax.all_gather(tokens, "section", axis=0)
    half = lax.all_gather(wide, "expert", axis=0, axis_index_groups=across)
    whole = lax.all_gather(half, "expert", axis=0, axis_index_groups=pairs)
    whole = whole.reshape((experts,) + wide.shape)

    hidden = up_call(code, whole, gate_up_weight[0], capacity)
    hidden = lax.all_gather(hidden, "section", axis=0)
    part = down_call(code, hidden, down_weight[0], capacity)

    part = part.reshape(2, chips * rows, width)
    part = lax.psum_scatter(part, "expert", scatter_dimension=0, axis_index_groups=pairs, tiled=False)
    return lax.psum_scatter(part, "expert", scatter_dimension=0, axis_index_groups=across, tiled=True)


def pair_shards(tokens, expert_ids, numerators, gate_up_weight, down_weight):
    rows, width = tokens.shape
    experts = lax.axis_size("expert")
    layers = experts // 4
    capacity = rows * expert_ids.shape[1] * 5 // (4 * experts)
    axes = ("section", "expert")
    ring = [0, *range(1, layers, 2), *reversed(range(2, layers, 2))]
    following = {z: ring[(p + 1) % layers] for p, z in enumerate(ring)}

    def perm(place):
        moves = []
        for x in range(2):
            for z in range(layers):
                for y in range(2):
                    for c in range(2):
                        tx, tz, ty, tc = place(x, z, y, c)
                        moves.append(((x * layers + z) * 4 + y * 2 + c, (tx * layers + tz) * 4 + ty * 2 + tc))
        return moves

    onward = perm(lambda x, z, y, c: (x, following[z], y, c))
    first = perm(lambda x, z, y, c: (x ^ (1 - c), z, y ^ c, c))
    second = perm(lambda x, z, y, c: (x ^ c, z, y ^ (1 - c), c))
    sibling = perm(lambda x, z, y, c: (x, z, y, 1 - c))
    over_x = perm(lambda x, z, y, c: (1 - x, z, y, c))
    over_y = perm(lambda x, z, y, c: (x, z, 1 - y, c))

    def move(value, moves):
        return lax.ppermute(value, axes, moves)

    table = np.zeros((2, layers, 2, 2, layers, 6), np.int32)
    for x, z, y, c, k in np.ndindex(2, layers, 2, 2, layers):
        at = ring[(ring.index(z) - k) % layers] * 4
        table[x, z, y, c, k] = [at + (y ^ (i & 1)) * 2 + (c ^ (i >> 1)) for i in range(4)] + [x, c]
    device = lax.axis_index("section") * experts + lax.axis_index("expert")
    where = lax.dynamic_index_in_dim(jnp.asarray(table.reshape(2 * experts, layers, 6)), device, 0, keepdims=False)
    code = lax.all_to_all(codes_of(expert_ids, numerators, experts), "expert", split_axis=0, concat_axis=0, tiled=True)

    later = move(tokens, onward)
    pairs = [jnp.stack([v, move(v, first)]) for v in (tokens, later)]

    mine, keeps, backs, hops, sums = [], [], [], [], []

    def spread(k):
        nonlocal code, where
        cross = move(pairs[k], second)
        if k == 0:
            cross, code, where = lax.optimization_barrier((cross, code, where))
        return [pairs[k], cross, move(pairs[k], sibling), move(cross, sibling)]

    def gate_up(k, shards_of, *earlier):
        mine.append(pick_call(k, where, code, shards_of, gate_up_weight[0], mine[-1:] + list(earlier), capacity))

    def down(k, *earlier):
        other = move(mine[k], over_x)
        keep, send = sum_call(k, where, code, mine[k], other, down_weight[0], keeps[-1:] + list(earlier), capacity)
        got = move(send, sibling)
        away = (keep[1].astype(jnp.float32) + got[1].astype(jnp.float32)).astype(jnp.bfloat16)
        keeps.append(keep)
        backs.append(move(away, over_y))
        sums.append((keep[0], got[0], backs[-1]))

    def hop(k):
        terms = [v.astype(jnp.float32) for v in [*sums[k], *hops[-1:]]]
        total = functools.reduce(jnp.add, terms).astype(jnp.bfloat16)
        if k:
            hops.append(move(total, onward))
        return total

    for k in range(layers):
        shards_of = spread(k)
        if k + 2 < layers:
            pairs.append(move(pairs[k + 1], onward))
        gate_up(k, shards_of, *keeps[-1:], *pairs[k + 1 : k + 2], *backs[:-1][-1:])
        if k == 0 and layers > 2:
            pairs[2], _ = lax.optimization_barrier((pairs[2], mine[0]))
        if k == 1:
            down(0, mine[1])
            if layers > 3:
                pairs[3], _ = lax.optimization_barrier((pairs[3], keeps[0]))
            down(1)
        if k > 2:
            down(k - 1, mine[k], backs[k - 2])
            hop(k - 2)
    hop(layers - 2)
    down(layers - 1, *hops[:1])
    hop(layers - 1)
    return hop(0)


def solution(mesh):
    in_specs = (
        P("expert", "section"),
        P("expert", None),
        P("expert", None),
        P("expert", None, "section"),
        P("expert", None, "section"),
    )
    out_specs = P("expert", "section")
    fits = mesh.shape["section"] == 2 and mesh.shape["expert"] == 16
    return jax.shard_map(pair_shards if fits else shards, mesh=mesh, in_specs=in_specs, out_specs=out_specs, check_vma=False)
```

```python
import functools

import jax
import jax.numpy as jnp
import numpy as np
from jax import lax
from jax.experimental import pallas as pl
from jax.experimental.pallas import tpu as pltpu
from jax.sharding import PartitionSpec as P

UNITS = 64
SCALE = 1.0 / 256.0
VMEM = 60 * 1024 * 1024


def group_of(capacity):
    count = 2
    while (count * capacity) % 16:
        count *= 2
    return count


def slot_map(code, group, capacity):
    line = jnp.concatenate(
        [code[i : i + 1] + jnp.where(code[i : i + 1] >= 0, i * capacity * 256, 0) for i in range(group)], axis=1
    )
    slot, weight = line >> 8, line & 255
    places = lax.broadcasted_iota(jnp.int32, (group * capacity, line.shape[1]), 0)
    return places == slot, weight


def up_kernel(group, capacity, code_ref, tokens_ref, weight_ref, hidden_ref, rows_ref):
    groups = tokens_ref.shape[0] // group
    sections, rows, width = tokens_ref.shape[1:]
    size = group * capacity
    for g in range(groups):
        onehot, _ = slot_map(code_ref[0, g * group : (g + 1) * group], group, capacity)
        onehot = onehot.astype(jnp.bfloat16)
        for s in range(sections):
            block = jnp.concatenate([tokens_ref[g * group + i, s] for i in range(group)], axis=0)
            picked = jnp.dot(onehot, block, preferred_element_type=jnp.float32)
            rows_ref[g * size : (g + 1) * size, s * width : (s + 1) * width] = picked.astype(jnp.bfloat16)
    columns = weight_ref.shape[1]
    pair = 4 * UNITS

    def products(first, count):
        return jnp.dot(rows_ref[...], weight_ref[:, pl.ds(first, count)], preferred_element_type=jnp.float32)

    def mix(gate, up):
        return (gate / (1.0 + jnp.exp(-gate)) * up).astype(jnp.bfloat16)

    @pl.loop(0, columns // pair)
    def _(p):
        both = products(pl.multiple_of(p * pair, pair), pair)
        one, two = both[:, : 2 * UNITS], both[:, 2 * UNITS :]
        low = lax.broadcasted_iota(jnp.int32, one.shape, 1) < UNITS
        gate = jnp.where(low, one, pltpu.roll(two, UNITS, 1))
        up = jnp.where(low, pltpu.roll(one, UNITS, 1), two)
        hidden_ref[:, pl.ds(pl.multiple_of(p * 2 * UNITS, 2 * UNITS), 2 * UNITS)] = mix(gate, up)

    if columns % pair:
        start = columns // pair * pair
        both = products(start, 2 * UNITS)
        hidden_ref[:, start // 2 :] = mix(both, pltpu.roll(both, UNITS, 1))[:, :UNITS]


def down_kernel(group, capacity, code_ref, hidden_ref, weight_ref, out_ref, result_ref):
    sections, _, units = hidden_ref.shape
    groups = code_ref.shape[1] // group
    size = group * capacity
    wide = weight_ref.shape[1]
    step = min(512, wide)

    @pl.loop(0, wide // step)
    def _(p):
        at = pl.ds(pl.multiple_of(p * step, step), step)
        total = jnp.dot(hidden_ref[0], weight_ref[0:units, at], preferred_element_type=jnp.float32)
        for s in range(1, sections):
            total += jnp.dot(
                hidden_ref[s], weight_ref[s * units : (s + 1) * units, at], preferred_element_type=jnp.float32
            )
        result_ref[...] = total.astype(jnp.bfloat16)
        for g in range(groups):
            onehot, weight = slot_map(code_ref[0, g * group : (g + 1) * group], group, capacity)
            scaled = jnp.where(onehot, weight.astype(jnp.float32) * SCALE, 0.0).astype(jnp.bfloat16)
            mixed = lax.dot_general(
                scaled,
                result_ref[g * size : (g + 1) * size],
                (((0,), (0,)), ((), ())),
                preferred_element_type=jnp.float32,
            )
            tall = scaled.shape[1]
            out_ref[g * tall : (g + 1) * tall, at] = mixed.astype(jnp.bfloat16)


def up_call(code, tokens, weight, capacity):
    blocks, sections, rows, width = tokens.shape
    group = group_of(capacity)
    take = min(blocks, 2 * group)
    depth, columns = weight.shape
    tall = take * capacity
    flops = 2 * blocks * capacity * depth * (columns + group * rows)
    return pl.pallas_call(
        functools.partial(up_kernel, group, capacity),
        grid=(blocks // take,),
        in_specs=[
            pl.BlockSpec((1, take, rows), lambda i: (i, 0, 0)),
            pl.BlockSpec((take, sections, rows, width), lambda i: (i, 0, 0, 0)),
            pl.BlockSpec((depth, columns), lambda i: (0, 0), pipeline_mode=pl.Buffered(1)),
        ],
        out_specs=pl.BlockSpec((tall, columns // 2), lambda i: (i, 0)),
        out_shape=jax.ShapeDtypeStruct((blocks * capacity, columns // 2), jnp.bfloat16),
        scratch_shapes=[pltpu.VMEM((tall, depth), jnp.bfloat16)],
        compiler_params=pltpu.CompilerParams(vmem_limit_bytes=48 * 1024 * 1024),
        cost_estimate=pl.CostEstimate(
            flops=flops, bytes_accessed=2 * (tokens.size + weight.size), transcendentals=blocks * capacity * columns // 2
        ),
        name="gate_up",
    )(code.reshape(blocks // take, take, rows), tokens, weight)


def down_call(code, hidden, weight, capacity):
    blocks, rows = code.shape
    sections, _, units = hidden.shape
    group = group_of(capacity)
    take = min(blocks, 2 * group)
    depth, wide = weight.shape
    tall = take * capacity
    return pl.pallas_call(
        functools.partial(down_kernel, group, capacity),
        grid=(blocks // take,),
        in_specs=[
            pl.BlockSpec((1, take, rows), lambda i: (i, 0, 0)),
            pl.BlockSpec((sections, tall, units), lambda i: (0, i, 0)),
            pl.BlockSpec((depth, wide), lambda i: (0, 0), pipeline_mode=pl.Buffered(1)),
        ],
        out_specs=pl.BlockSpec((take * rows, wide), lambda i: (i, 0)),
        out_shape=jax.ShapeDtypeStruct((blocks * rows, wide), jnp.bfloat16),
        scratch_shapes=[pltpu.VMEM((tall, min(512, wide)), jnp.bfloat16)],
        compiler_params=pltpu.CompilerParams(vmem_limit_bytes=48 * 1024 * 1024),
        cost_estimate=pl.CostEstimate(
            flops=2 * blocks * capacity * wide * (depth + group * rows),
            bytes_accessed=2 * (hidden.size + weight.size + blocks * rows * wide),
            transcendentals=0,
        ),
        name="down",
    )(code.reshape(blocks // take, take, rows), hidden, weight)


def block_codes(k, own, where_ref, code_ref):
    return jnp.concatenate([code_ref[pl.ds(where_ref[k, 2 * own + i], 1), :] for i in range(2)], axis=0)


def pick_kernel(capacity, k, where_ref, code_ref, *refs):
    pairs, weight_hbm = refs[:4], refs[4]
    hidden_ref, pair_ref, weight_ref, rows_ref, sems = refs[-5:]
    rows, width = pairs[0].shape[1:]
    span = 8 * UNITS
    spans = weight_hbm.shape[1] // span
    x, c = where_ref[k, 4], where_ref[k, 5]

    def weight_copy(j):
        at = pl.ds(pl.multiple_of(j * span, span), span)
        return pltpu.make_async_copy(weight_hbm.at[:, at], weight_ref.at[:, at], sems.at[4 + j])

    copies = [pltpu.make_async_copy(v, pair_ref.at[pl.ds(2 * i, 2)], sems.at[i]) for i, v in enumerate(pairs)]
    for copy in copies:
        copy.start()
    for j in range(spans):
        weight_copy(j).start()
    for own in range(2):
        core = c ^ own
        onehot, _ = slot_map(block_codes(k, own, where_ref, code_ref), 2, capacity)
        onehot = onehot.astype(jnp.bfloat16)
        copies[2 * own].wait()
        copies[2 * own + 1].wait()
        for section, near, far in ((x, 0, 2 - core), (1 - x, 1 + core, 3)):
            block = jnp.concatenate([pair_ref[4 * own + near], pair_ref[4 * own + far]], axis=0)
            picked = jnp.dot(onehot, block, preferred_element_type=jnp.float32)
            at = pl.ds(pl.multiple_of(section * width, width), width)
            rows_ref[2 * own * capacity : 2 * (own + 1) * capacity, at] = picked.astype(jnp.bfloat16)

    @pl.loop(0, spans)
    def _(j):
        weight_copy(j).wait()
        at = pl.ds(pl.multiple_of(j * span, span), span)
        both = jnp.dot(rows_ref[...], weight_ref[:, at], preferred_element_type=jnp.float32)
        for p in range(2):
            one, two = both[:, 4 * p * UNITS : (4 * p + 2) * UNITS], both[:, (4 * p + 2) * UNITS : 4 * (p + 1) * UNITS]
            low = lax.broadcasted_iota(jnp.int32, one.shape, 1) < UNITS
            gate = jnp.where(low, one, pltpu.roll(two, UNITS, 1))
            up = jnp.where(low, pltpu.roll(one, UNITS, 1), two)
            half = pl.ds(pl.multiple_of((2 * j + p) * 2 * UNITS, 2 * UNITS), 2 * UNITS)
            hidden_ref[:, half] = (gate / (1.0 + jnp.exp(-gate)) * up).astype(jnp.bfloat16)


def sum_kernel(capacity, k, where_ref, code_ref, *refs):
    mine_hbm, other_hbm, weight_hbm = refs[:3]
    keep_hbm, send_hbm, hidden_ref, weight_ref, out_ref, sems = refs[-6:]
    rows = code_ref.shape[1]
    units = mine_hbm.shape[1]
    span = 512
    spans = weight_hbm.shape[1] // span

    def weight_copy(j):
        at = pl.ds(pl.multiple_of(j * span, span), span)
        return pltpu.make_async_copy(weight_hbm.at[:, at], weight_ref.at[:, at], sems.at[2 + j])

    def out_copy(j, i, to):
        at = pl.ds(pl.multiple_of(j * span, span), span)
        sem = sems.at[2 + spans + 2 * j + i]
        return pltpu.make_async_copy(out_ref.at[pl.ds(2 * i, 2), :, at], to.at[:, :, at], sem)

    copies = [pltpu.make_async_copy(v, hidden_ref.at[i], sems.at[i]) for i, v in enumerate((mine_hbm, other_hbm))]
    for copy in copies:
        copy.start()
    for j in range(spans):
        weight_copy(j).start()
    scaled = []
    for own in range(2):
        onehot, weight = slot_map(block_codes(k, own, where_ref, code_ref), 2, capacity)
        scaled.append(jnp.where(onehot, weight.astype(jnp.float32) * SCALE, 0.0).astype(jnp.bfloat16))
    me = where_ref[k, 4]
    mine_at = pl.ds(pl.multiple_of(me * units, units), units)
    other_at = pl.ds(pl.multiple_of((1 - me) * units, units), units)
    for copy in copies:
        copy.wait()

    @pl.loop(0, spans)
    def _(j):
        weight_copy(j).wait()
        at = pl.ds(pl.multiple_of(j * span, span), span)
        total = jnp.dot(hidden_ref[0], weight_ref[mine_at, at], preferred_element_type=jnp.float32)
        total += jnp.dot(hidden_ref[1], weight_ref[other_at, at], preferred_element_type=jnp.float32)
        result = total.astype(jnp.bfloat16)
        for own in range(2):
            mixed = lax.dot_general(
                scaled[own],
                result[2 * own * capacity : 2 * (own + 1) * capacity],
                (((0,), (0,)), ((), ())),
                preferred_element_type=jnp.float32,
            )
            out_ref[2 * own : 2 * own + 2, :, at] = mixed.astype(jnp.bfloat16).reshape(2, rows, span)
        out_copy(j, 0, keep_hbm).start()
        out_copy(j, 1, send_hbm).start()

    for j in range(spans):
        out_copy(j, 0, keep_hbm).wait()
        out_copy(j, 1, send_hbm).wait()


def pick_call(k, where, code, pairs, weight, earlier, capacity):
    _, rows, width = pairs[0].shape
    depth, columns = weight.shape
    tall = 4 * capacity
    anywhere = pl.BlockSpec(memory_space=pl.ANY)
    return pl.pallas_call(
        functools.partial(pick_kernel, capacity, k),
        in_specs=[
            pl.BlockSpec(memory_space=pltpu.SMEM),
            pl.BlockSpec(memory_space=pltpu.VMEM),
            *[anywhere] * (5 + len(earlier)),
        ],
        out_specs=pl.BlockSpec(memory_space=pltpu.VMEM),
        out_shape=jax.ShapeDtypeStruct((tall, columns // 2), jnp.bfloat16),
        scratch_shapes=[
            pltpu.VMEM((8, rows, width), jnp.bfloat16),
            pltpu.VMEM((depth, columns), jnp.bfloat16),
            pltpu.VMEM((tall, depth), jnp.bfloat16),
            pltpu.SemaphoreType.DMA((4 + columns // (8 * UNITS),)),
        ],
        compiler_params=pltpu.CompilerParams(vmem_limit_bytes=VMEM),
        cost_estimate=pl.CostEstimate(
            flops=2 * tall * depth * (columns + rows),
            bytes_accessed=2 * (8 * rows * width + weight.size + tall * columns // 2),
            transcendentals=tall * columns // 2,
        ),
        name="gate_up",
    )(where, code, *pairs, weight, *earlier)


def sum_call(k, where, code, mine, other, weight, earlier, capacity):
    rows = code.shape[1]
    depth, wide = weight.shape
    tall, units = mine.shape
    anywhere = pl.BlockSpec(memory_space=pl.ANY)
    return pl.pallas_call(
        functools.partial(sum_kernel, capacity, k),
        in_specs=[
            pl.BlockSpec(memory_space=pltpu.SMEM),
            pl.BlockSpec(memory_space=pltpu.VMEM),
            *[anywhere] * (3 + len(earlier)),
        ],
        out_specs=[anywhere] * 2,
        out_shape=[jax.ShapeDtypeStruct((2, rows, wide), jnp.bfloat16)] * 2,
        scratch_shapes=[
            pltpu.VMEM((2, tall, units), jnp.bfloat16),
            pltpu.VMEM((depth, wide), jnp.bfloat16),
            pltpu.VMEM((4, rows, wide), jnp.bfloat16),
            pltpu.SemaphoreType.DMA((2 + 3 * (wide // 512),)),
        ],
        compiler_params=pltpu.CompilerParams(vmem_limit_bytes=VMEM),
        cost_estimate=pl.CostEstimate(
            flops=2 * wide * (tall * depth + 4 * rows * capacity),
            bytes_accessed=2 * (2 * mine.size + weight.size + 4 * rows * wide),
            transcendentals=0,
        ),
        name="down",
    )(where, code, mine, other, weight, *earlier)


def codes_of(expert_ids, numerators, experts):
    rows = expert_ids.shape[0]
    named = expert_ids.T[None] == jnp.arange(experts, dtype=jnp.int32)[:, None, None]
    hits = jnp.any(named, axis=1)
    weight = jnp.sum(jnp.where(named, numerators.T[None], 0), axis=1)
    earlier = jnp.arange(rows)[:, None] < jnp.arange(rows)[None, :]
    rank = jnp.dot(hits.astype(jnp.bfloat16), earlier.astype(jnp.bfloat16), preferred_element_type=jnp.float32)
    return jnp.where(hits, rank.astype(jnp.int32) * 256 + weight, -1)


def shards(tokens, expert_ids, numerators, gate_up_weight, down_weight):
    rows, width = tokens.shape
    experts = lax.axis_size("expert")
    capacity = rows * expert_ids.shape[1] * 5 // (4 * experts)
    chips = experts // 2
    across = [[2 * i + c for i in range(chips)] for c in range(2)]
    pairs = [[2 * i, 2 * i + 1] for i in range(chips)]

    codes = lax.all_gather(codes_of(expert_ids, numerators, experts), "expert", axis=0)
    code = lax.dynamic_index_in_dim(codes, lax.axis_index("expert"), 1, keepdims=False)
    code = code.reshape(chips, 2, rows).swapaxes(0, 1).reshape(experts, rows)

    wide = lax.all_gather(tokens, "section", axis=0)
    half = lax.all_gather(wide, "expert", axis=0, axis_index_groups=across)
    whole = lax.all_gather(half, "expert", axis=0, axis_index_groups=pairs)
    whole = whole.reshape((experts,) + wide.shape)

    hidden = up_call(code, whole, gate_up_weight[0], capacity)
    hidden = lax.all_gather(hidden, "section", axis=0)
    part = down_call(code, hidden, down_weight[0], capacity)

    part = part.reshape(2, chips * rows, width)
    part = lax.psum_scatter(part, "expert", scatter_dimension=0, axis_index_groups=pairs, tiled=False)
    return lax.psum_scatter(part, "expert", scatter_dimension=0, axis_index_groups=across, tiled=True)


def pair_shards(tokens, expert_ids, numerators, gate_up_weight, down_weight):
    rows, width = tokens.shape
    experts = lax.axis_size("expert")
    layers = experts // 4
    capacity = rows * expert_ids.shape[1] * 5 // (4 * experts)
    axes = ("section", "expert")
    ring = [0, *range(1, layers, 2), *reversed(range(2, layers, 2))]
    following = {z: ring[(p + 1) % layers] for p, z in enumerate(ring)}

    def perm(place):
        moves = []
        for x in range(2):
            for z in range(layers):
                for y in range(2):
                    for c in range(2):
                        tx, tz, ty, tc = place(x, z, y, c)
                        moves.append(((x * layers + z) * 4 + y * 2 + c, (tx * layers + tz) * 4 + ty * 2 + tc))
        return moves

    onward = perm(lambda x, z, y, c: (x, following[z], y, c))
    first = perm(lambda x, z, y, c: (x ^ (1 - c), z, y ^ c, c))
    second = perm(lambda x, z, y, c: (x ^ c, z, y ^ (1 - c), c))
    sibling = perm(lambda x, z, y, c: (x, z, y, 1 - c))
    over_x = perm(lambda x, z, y, c: (1 - x, z, y, c))
    over_y = perm(lambda x, z, y, c: (x, z, 1 - y, c))

    def move(value, moves):
        return lax.ppermute(value, axes, moves)

    table = np.zeros((2, layers, 2, 2, layers, 6), np.int32)
    for x, z, y, c, k in np.ndindex(2, layers, 2, 2, layers):
        at = ring[(ring.index(z) - k) % layers] * 4
        table[x, z, y, c, k] = [at + (y ^ (i & 1)) * 2 + (c ^ (i >> 1)) for i in range(4)] + [x, c]
    device = lax.axis_index("section") * experts + lax.axis_index("expert")
    where = lax.dynamic_index_in_dim(jnp.asarray(table.reshape(2 * experts, layers, 6)), device, 0, keepdims=False)
    code = lax.all_to_all(codes_of(expert_ids, numerators, experts), "expert", split_axis=0, concat_axis=0, tiled=True)

    later = move(tokens, onward)
    near = move(tokens, first)
    later, near, code, where = lax.optimization_barrier((later, near, code, where))
    pairs = [jnp.stack([tokens, near]), jnp.stack([later, move(later, first)])]
    pairs.append(move(pairs[1], onward))

    mine, others, keeps, gots, backs, hops = [], [], [], [], [], []

    def after(value, *done):
        return lax.optimization_barrier((value, *done))[0]

    def spread(k, *done):
        cross = move(pairs[k], second)
        return [pairs[k], cross, move(pairs[k], sibling), move(after(cross, *done), sibling)]

    def gate_up(k, shards_of, *earlier):
        mine.append(pick_call(k, where, code, shards_of, gate_up_weight[0], mine[-1:] + list(earlier), capacity))
        others.append(move(mine[k], over_x))

    def down(k, *earlier):
        keep, send = sum_call(k, where, code, mine[k], others[k], down_weight[0], keeps[-1:] + list(earlier), capacity)
        keeps.append(keep)
        gots.append(move(send, sibling))

    def away(k):
        return (keeps[k][1].astype(jnp.float32) + gots[k][1].astype(jnp.float32)).astype(jnp.bfloat16)

    def hop(k):
        terms = [v.astype(jnp.float32) for v in [keeps[k][0], gots[k][0], backs[k], *hops[-1:]]]
        total = functools.reduce(jnp.add, terms).astype(jnp.bfloat16)
        if k:
            hops.append(move(total, onward))
        return total

    gate_up(0, spread(0))
    gate_up(1, spread(1), pairs[2])
    pairs[2] = after(pairs[2], mine[0])
    pairs.append(move(pairs[2], onward))
    down(0, mine[1])
    pairs[3] = after(pairs[3], keeps[0])
    down(1)
    both = move(jnp.stack([away(0), away(1)]), over_y)
    backs += [both[0], both[1]]
    gate_up(2, spread(2), keeps[1], pairs[3])
    gate_up(3, spread(3, mine[2]))
    hop(1)
    down(2, mine[3])
    backs.append(move(away(2), over_y))
    down(3, both)
    backs.append(move(after(away(3), hops[0]), over_y))
    hop(2)
    hop(3)
    return hop(0)


def solution(mesh):
    in_specs = (
        P("expert", "section"),
        P("expert", None),
        P("expert", None),
        P("expert", None, "section"),
        P("expert", None, "section"),
    )
    out_specs = P("expert", "section")
    fits = mesh.shape["section"] == 2 and mesh.shape["expert"] == 16
    return jax.shard_map(pair_shards if fits else shards, mesh=mesh, in_specs=in_specs, out_specs=out_specs, check_vma=False)
```

```python
import functools

import jax
import jax.numpy as jnp
import numpy as np
from jax import lax
from jax.experimental import pallas as pl
from jax.experimental.pallas import tpu as pltpu
from jax.sharding import PartitionSpec as P

UNITS = 64
SCALE = 1.0 / 256.0
VMEM = 40 * 1024 * 1024


def group_of(capacity):
    count = 2
    while (count * capacity) % 16:
        count *= 2
    return count


def slot_map(code, group, capacity):
    line = jnp.concatenate(
        [code[i : i + 1] + jnp.where(code[i : i + 1] >= 0, i * capacity * 256, 0) for i in range(group)], axis=1
    )
    slot, weight = line >> 8, line & 255
    places = lax.broadcasted_iota(jnp.int32, (group * capacity, line.shape[1]), 0)
    return places == slot, weight


def up_kernel(group, capacity, code_ref, tokens_ref, weight_ref, hidden_ref, rows_ref):
    groups = tokens_ref.shape[0] // group
    sections, rows, width = tokens_ref.shape[1:]
    size = group * capacity
    for g in range(groups):
        onehot, _ = slot_map(code_ref[0, g * group : (g + 1) * group], group, capacity)
        onehot = onehot.astype(jnp.bfloat16)
        for s in range(sections):
            block = jnp.concatenate([tokens_ref[g * group + i, s] for i in range(group)], axis=0)
            picked = jnp.dot(onehot, block, preferred_element_type=jnp.float32)
            rows_ref[g * size : (g + 1) * size, s * width : (s + 1) * width] = picked.astype(jnp.bfloat16)
    columns = weight_ref.shape[1]
    pair = 4 * UNITS

    def products(first, count):
        return jnp.dot(rows_ref[...], weight_ref[:, pl.ds(first, count)], preferred_element_type=jnp.float32)

    def mix(gate, up):
        return (gate / (1.0 + jnp.exp(-gate)) * up).astype(jnp.bfloat16)

    @pl.loop(0, columns // pair)
    def _(p):
        both = products(pl.multiple_of(p * pair, pair), pair)
        one, two = both[:, : 2 * UNITS], both[:, 2 * UNITS :]
        low = lax.broadcasted_iota(jnp.int32, one.shape, 1) < UNITS
        gate = jnp.where(low, one, pltpu.roll(two, UNITS, 1))
        up = jnp.where(low, pltpu.roll(one, UNITS, 1), two)
        hidden_ref[:, pl.ds(pl.multiple_of(p * 2 * UNITS, 2 * UNITS), 2 * UNITS)] = mix(gate, up)

    if columns % pair:
        start = columns // pair * pair
        both = products(start, 2 * UNITS)
        hidden_ref[:, start // 2 :] = mix(both, pltpu.roll(both, UNITS, 1))[:, :UNITS]


def down_kernel(group, capacity, code_ref, hidden_ref, weight_ref, out_ref, result_ref):
    sections, _, units = hidden_ref.shape
    groups = code_ref.shape[1] // group
    size = group * capacity
    wide = weight_ref.shape[1]
    step = min(512, wide)

    @pl.loop(0, wide // step)
    def _(p):
        at = pl.ds(pl.multiple_of(p * step, step), step)
        total = jnp.dot(hidden_ref[0], weight_ref[0:units, at], preferred_element_type=jnp.float32)
        for s in range(1, sections):
            total += jnp.dot(
                hidden_ref[s], weight_ref[s * units : (s + 1) * units, at], preferred_element_type=jnp.float32
            )
        result_ref[...] = total.astype(jnp.bfloat16)
        for g in range(groups):
            onehot, weight = slot_map(code_ref[0, g * group : (g + 1) * group], group, capacity)
            scaled = jnp.where(onehot, weight.astype(jnp.float32) * SCALE, 0.0).astype(jnp.bfloat16)
            mixed = lax.dot_general(
                scaled,
                result_ref[g * size : (g + 1) * size],
                (((0,), (0,)), ((), ())),
                preferred_element_type=jnp.float32,
            )
            tall = scaled.shape[1]
            out_ref[g * tall : (g + 1) * tall, at] = mixed.astype(jnp.bfloat16)


def up_call(code, tokens, weight, capacity):
    blocks, sections, rows, width = tokens.shape
    group = group_of(capacity)
    take = min(blocks, 2 * group)
    depth, columns = weight.shape
    tall = take * capacity
    flops = 2 * blocks * capacity * depth * (columns + group * rows)
    return pl.pallas_call(
        functools.partial(up_kernel, group, capacity),
        grid=(blocks // take,),
        in_specs=[
            pl.BlockSpec((1, take, rows), lambda i: (i, 0, 0)),
            pl.BlockSpec((take, sections, rows, width), lambda i: (i, 0, 0, 0)),
            pl.BlockSpec((depth, columns), lambda i: (0, 0), pipeline_mode=pl.Buffered(1)),
        ],
        out_specs=pl.BlockSpec((tall, columns // 2), lambda i: (i, 0)),
        out_shape=jax.ShapeDtypeStruct((blocks * capacity, columns // 2), jnp.bfloat16),
        scratch_shapes=[pltpu.VMEM((tall, depth), jnp.bfloat16)],
        compiler_params=pltpu.CompilerParams(vmem_limit_bytes=48 * 1024 * 1024),
        cost_estimate=pl.CostEstimate(
            flops=flops, bytes_accessed=2 * (tokens.size + weight.size), transcendentals=blocks * capacity * columns // 2
        ),
        name="gate_up",
    )(code.reshape(blocks // take, take, rows), tokens, weight)


def down_call(code, hidden, weight, capacity):
    blocks, rows = code.shape
    sections, _, units = hidden.shape
    group = group_of(capacity)
    take = min(blocks, 2 * group)
    depth, wide = weight.shape
    tall = take * capacity
    return pl.pallas_call(
        functools.partial(down_kernel, group, capacity),
        grid=(blocks // take,),
        in_specs=[
            pl.BlockSpec((1, take, rows), lambda i: (i, 0, 0)),
            pl.BlockSpec((sections, tall, units), lambda i: (0, i, 0)),
            pl.BlockSpec((depth, wide), lambda i: (0, 0), pipeline_mode=pl.Buffered(1)),
        ],
        out_specs=pl.BlockSpec((take * rows, wide), lambda i: (i, 0)),
        out_shape=jax.ShapeDtypeStruct((blocks * rows, wide), jnp.bfloat16),
        scratch_shapes=[pltpu.VMEM((tall, min(512, wide)), jnp.bfloat16)],
        compiler_params=pltpu.CompilerParams(vmem_limit_bytes=48 * 1024 * 1024),
        cost_estimate=pl.CostEstimate(
            flops=2 * blocks * capacity * wide * (depth + group * rows),
            bytes_accessed=2 * (hidden.size + weight.size + blocks * rows * wide),
            transcendentals=0,
        ),
        name="down",
    )(code.reshape(blocks // take, take, rows), hidden, weight)


def block_codes(k, own, where_ref, code_ref):
    return jnp.concatenate([code_ref[pl.ds(where_ref[k, 2 * own + i], 1), :] for i in range(2)], axis=0)


def pick_kernel(capacity, k, where_ref, code_ref, *refs):
    pairs, weight_hbm = refs[:4], refs[4]
    hidden_ref, pair_ref, weight_ref, rows_ref, sems = refs[-5:]
    rows, width = pairs[0].shape[1:]
    span = 8 * UNITS
    spans = weight_hbm.shape[1] // span
    x, c = where_ref[k, 4], where_ref[k, 5]

    def weight_copy(j):
        at = pl.ds(pl.multiple_of(j * span, span), span)
        return pltpu.make_async_copy(weight_hbm.at[:, at], weight_ref.at[:, at], sems.at[4 + j])

    copies = [pltpu.make_async_copy(v, pair_ref.at[pl.ds(2 * i, 2)], sems.at[i]) for i, v in enumerate(pairs)]
    for copy in copies:
        copy.start()
    for j in range(spans):
        weight_copy(j).start()
    for own in range(2):
        core = c ^ own
        onehot, _ = slot_map(block_codes(k, own, where_ref, code_ref), 2, capacity)
        onehot = onehot.astype(jnp.bfloat16)
        copies[2 * own].wait()
        copies[2 * own + 1].wait()
        for section, near, far in ((x, 0, 2 - core), (1 - x, 1 + core, 3)):
            block = jnp.concatenate([pair_ref[4 * own + near], pair_ref[4 * own + far]], axis=0)
            picked = jnp.dot(onehot, block, preferred_element_type=jnp.float32)
            at = pl.ds(pl.multiple_of(section * width, width), width)
            rows_ref[2 * own * capacity : 2 * (own + 1) * capacity, at] = picked.astype(jnp.bfloat16)

    @pl.loop(0, spans)
    def _(j):
        weight_copy(j).wait()
        at = pl.ds(pl.multiple_of(j * span, span), span)
        both = jnp.dot(rows_ref[...], weight_ref[:, at], preferred_element_type=jnp.float32)
        for p in range(2):
            one, two = both[:, 4 * p * UNITS : (4 * p + 2) * UNITS], both[:, (4 * p + 2) * UNITS : 4 * (p + 1) * UNITS]
            low = lax.broadcasted_iota(jnp.int32, one.shape, 1) < UNITS
            gate = jnp.where(low, one, pltpu.roll(two, UNITS, 1))
            up = jnp.where(low, pltpu.roll(one, UNITS, 1), two)
            half = pl.ds(pl.multiple_of((2 * j + p) * 2 * UNITS, 2 * UNITS), 2 * UNITS)
            hidden_ref[:, half] = (gate / (1.0 + jnp.exp(-gate)) * up).astype(jnp.bfloat16)


def sum_kernel(capacity, k, where_ref, code_ref, *refs):
    mine_hbm, other_hbm, weight_hbm = refs[:3]
    keep_hbm, send_hbm, hidden_ref, weight_ref, out_ref, sems = refs[-6:]
    rows = code_ref.shape[1]
    units = mine_hbm.shape[1]
    span = 512
    spans = weight_hbm.shape[1] // span

    def weight_copy(j):
        at = pl.ds(pl.multiple_of(j * span, span), span)
        return pltpu.make_async_copy(weight_hbm.at[:, at], weight_ref.at[:, at], sems.at[2 + j])

    def out_copy(j, i, to):
        at = pl.ds(pl.multiple_of(j * span, span), span)
        sem = sems.at[2 + spans + 2 * j + i]
        return pltpu.make_async_copy(out_ref.at[pl.ds(2 * i, 2), :, at], to.at[:, :, at], sem)

    copies = [pltpu.make_async_copy(v, hidden_ref.at[i], sems.at[i]) for i, v in enumerate((mine_hbm, other_hbm))]
    for copy in copies:
        copy.start()
    for j in range(spans):
        weight_copy(j).start()
    scaled = []
    for own in range(2):
        onehot, weight = slot_map(block_codes(k, own, where_ref, code_ref), 2, capacity)
        scaled.append(jnp.where(onehot, weight.astype(jnp.float32) * SCALE, 0.0).astype(jnp.bfloat16))
    me = where_ref[k, 4]
    mine_at = pl.ds(pl.multiple_of(me * units, units), units)
    other_at = pl.ds(pl.multiple_of((1 - me) * units, units), units)
    for copy in copies:
        copy.wait()

    @pl.loop(0, spans)
    def _(j):
        weight_copy(j).wait()
        at = pl.ds(pl.multiple_of(j * span, span), span)
        total = jnp.dot(hidden_ref[0], weight_ref[mine_at, at], preferred_element_type=jnp.float32)
        total += jnp.dot(hidden_ref[1], weight_ref[other_at, at], preferred_element_type=jnp.float32)
        result = total.astype(jnp.bfloat16)
        for own in range(2):
            mixed = lax.dot_general(
                scaled[own],
                result[2 * own * capacity : 2 * (own + 1) * capacity],
                (((0,), (0,)), ((), ())),
                preferred_element_type=jnp.float32,
            )
            out_ref[2 * own : 2 * own + 2, :, at] = mixed.astype(jnp.bfloat16).reshape(2, rows, span)
        out_copy(j, 0, keep_hbm).start()
        out_copy(j, 1, send_hbm).start()

    for j in range(spans):
        out_copy(j, 0, keep_hbm).wait()
        out_copy(j, 1, send_hbm).wait()


def pick_call(k, where, code, pairs, weight, earlier, capacity):
    _, rows, width = pairs[0].shape
    depth, columns = weight.shape
    tall = 4 * capacity
    anywhere = pl.BlockSpec(memory_space=pl.ANY)
    return pl.pallas_call(
        functools.partial(pick_kernel, capacity, k),
        in_specs=[
            pl.BlockSpec(memory_space=pltpu.SMEM),
            pl.BlockSpec(memory_space=pltpu.VMEM),
            *[anywhere] * (5 + len(earlier)),
        ],
        out_specs=pl.BlockSpec(memory_space=pltpu.VMEM),
        out_shape=jax.ShapeDtypeStruct((tall, columns // 2), jnp.bfloat16),
        scratch_shapes=[
            pltpu.VMEM((8, rows, width), jnp.bfloat16),
            pltpu.VMEM((depth, columns), jnp.bfloat16),
            pltpu.VMEM((tall, depth), jnp.bfloat16),
            pltpu.SemaphoreType.DMA((4 + columns // (8 * UNITS),)),
        ],
        compiler_params=pltpu.CompilerParams(vmem_limit_bytes=VMEM),
        cost_estimate=pl.CostEstimate(
            flops=2 * tall * depth * (columns + rows),
            bytes_accessed=2 * (8 * rows * width + weight.size + tall * columns // 2),
            transcendentals=tall * columns // 2,
        ),
        name="gate_up",
    )(where, code, *pairs, weight, *earlier)


def sum_call(k, where, code, mine, other, weight, earlier, capacity):
    rows = code.shape[1]
    depth, wide = weight.shape
    tall, units = mine.shape
    anywhere = pl.BlockSpec(memory_space=pl.ANY)
    return pl.pallas_call(
        functools.partial(sum_kernel, capacity, k),
        in_specs=[
            pl.BlockSpec(memory_space=pltpu.SMEM),
            pl.BlockSpec(memory_space=pltpu.VMEM),
            *[anywhere] * (3 + len(earlier)),
        ],
        out_specs=[anywhere] * 2,
        out_shape=[jax.ShapeDtypeStruct((2, rows, wide), jnp.bfloat16)] * 2,
        scratch_shapes=[
            pltpu.VMEM((2, tall, units), jnp.bfloat16),
            pltpu.VMEM((depth, wide), jnp.bfloat16),
            pltpu.VMEM((4, rows, wide), jnp.bfloat16),
            pltpu.SemaphoreType.DMA((2 + 3 * (wide // 512),)),
        ],
        compiler_params=pltpu.CompilerParams(vmem_limit_bytes=VMEM),
        cost_estimate=pl.CostEstimate(
            flops=2 * wide * (tall * depth + 4 * rows * capacity),
            bytes_accessed=2 * (2 * mine.size + weight.size + 4 * rows * wide),
            transcendentals=0,
        ),
        name="down",
    )(where, code, mine, other, weight, *earlier)


def codes_of(expert_ids, numerators, experts):
    rows = expert_ids.shape[0]
    named = expert_ids.T[None] == jnp.arange(experts, dtype=jnp.int32)[:, None, None]
    hits = jnp.any(named, axis=1)
    weight = jnp.sum(jnp.where(named, numerators.T[None], 0), axis=1)
    earlier = jnp.arange(rows)[:, None] < jnp.arange(rows)[None, :]
    rank = jnp.dot(hits.astype(jnp.bfloat16), earlier.astype(jnp.bfloat16), preferred_element_type=jnp.float32)
    return jnp.where(hits, rank.astype(jnp.int32) * 256 + weight, -1)


def shards(tokens, expert_ids, numerators, gate_up_weight, down_weight):
    rows, width = tokens.shape
    experts = lax.axis_size("expert")
    capacity = rows * expert_ids.shape[1] * 5 // (4 * experts)
    chips = experts // 2
    across = [[2 * i + c for i in range(chips)] for c in range(2)]
    pairs = [[2 * i, 2 * i + 1] for i in range(chips)]

    codes = lax.all_gather(codes_of(expert_ids, numerators, experts), "expert", axis=0)
    code = lax.dynamic_index_in_dim(codes, lax.axis_index("expert"), 1, keepdims=False)
    code = code.reshape(chips, 2, rows).swapaxes(0, 1).reshape(experts, rows)

    wide = lax.all_gather(tokens, "section", axis=0)
    half = lax.all_gather(wide, "expert", axis=0, axis_index_groups=across)
    whole = lax.all_gather(half, "expert", axis=0, axis_index_groups=pairs)
    whole = whole.reshape((experts,) + wide.shape)

    hidden = up_call(code, whole, gate_up_weight[0], capacity)
    hidden = lax.all_gather(hidden, "section", axis=0)
    part = down_call(code, hidden, down_weight[0], capacity)

    part = part.reshape(2, chips * rows, width)
    part = lax.psum_scatter(part, "expert", scatter_dimension=0, axis_index_groups=pairs, tiled=False)
    return lax.psum_scatter(part, "expert", scatter_dimension=0, axis_index_groups=across, tiled=True)


def pair_shards(tokens, expert_ids, numerators, gate_up_weight, down_weight):
    rows, width = tokens.shape
    experts = lax.axis_size("expert")
    layers = experts // 4
    capacity = rows * expert_ids.shape[1] * 5 // (4 * experts)
    axes = ("section", "expert")
    ring = [0, *range(1, layers, 2), *reversed(range(2, layers, 2))]
    following = {z: ring[(p + 1) % layers] for p, z in enumerate(ring)}

    def perm(place):
        moves = []
        for x in range(2):
            for z in range(layers):
                for y in range(2):
                    for c in range(2):
                        tx, tz, ty, tc = place(x, z, y, c)
                        moves.append(((x * layers + z) * 4 + y * 2 + c, (tx * layers + tz) * 4 + ty * 2 + tc))
        return moves

    onward = perm(lambda x, z, y, c: (x, following[z], y, c))
    backward = [(to, source) for source, to in onward]
    first = perm(lambda x, z, y, c: (x ^ (1 - c), z, y ^ c, c))
    second = perm(lambda x, z, y, c: (x ^ c, z, y ^ (1 - c), c))
    sibling = perm(lambda x, z, y, c: (x, z, y, 1 - c))
    over_x = perm(lambda x, z, y, c: (1 - x, z, y, c))
    over_y = perm(lambda x, z, y, c: (x, z, 1 - y, c))

    def move(value, moves):
        return lax.ppermute(value, axes, moves)

    table = np.zeros((2, layers, 2, 2, layers, 6), np.int32)
    for x, z, y, c, k in np.ndindex(2, layers, 2, 2, layers):
        at = ring[(ring.index(z) - k) % layers] * 4
        table[x, z, y, c, k] = [at + (y ^ (i & 1)) * 2 + (c ^ (i >> 1)) for i in range(4)] + [x, c]
    device = lax.axis_index("section") * experts + lax.axis_index("expert")
    where = lax.dynamic_index_in_dim(jnp.asarray(table.reshape(2 * experts, layers, 6)), device, 0, keepdims=False)
    code = lax.all_to_all(codes_of(expert_ids, numerators, experts), "expert", split_axis=0, concat_axis=0, tiled=True)

    near = move(tokens, first)
    later = move(tokens, onward)
    last = move(later, onward)
    later, near, code, where = lax.optimization_barrier((later, near, code, where))
    pairs = [jnp.stack([tokens, near])] + [jnp.stack([v, move(v, first)]) for v in (later, last)]
    pairs.append(move(pairs[2], onward))

    def after(value, *done):
        return lax.optimization_barrier((value, *done))[0]

    def spread(k, *done):
        cross = move(pairs[k], second)
        return [pairs[k], cross, move(pairs[k], sibling), move(after(cross, *done), sibling)]

    def gate_up(k, shards_of, *earlier):
        mine = pick_call(k, where, code, shards_of, gate_up_weight[0], earlier, capacity)
        return mine, move(mine, over_x)

    def down(k, hidden, *earlier):
        keep, send = sum_call(k, where, code, *hidden, down_weight[0], earlier, capacity)
        return keep, move(send, sibling)

    def away(part):
        keep, got = part
        return (keep[1].astype(jnp.float32) + got[1].astype(jnp.float32)).astype(jnp.bfloat16)

    def total(part, back, *hop):
        terms = [v.astype(jnp.float32) for v in (part[0][0], part[1][0], back, *hop)]
        return functools.reduce(jnp.add, terms).astype(jnp.bfloat16)

    hidden0 = gate_up(0, spread(0))
    pairs[3] = after(pairs[3], hidden0[0])
    shards2 = spread(2, hidden0[0])
    hidden1 = gate_up(1, spread(1, hidden0[0]), pairs[3], shards2[1])
    part0 = down(0, hidden0, hidden1[0])
    hidden2 = gate_up(2, shards2, part0[0])
    back0 = move(away(part0), over_y)
    hidden3 = gate_up(3, spread(3, hidden1[0]), hidden2[0])
    part1 = down(1, hidden1, hidden3[0], back0)
    back1 = move(away(part1), over_y)
    part2 = down(2, hidden2, part1[0], hidden3[1])
    part3 = down(3, hidden3, part2[0], back1)
    from_next = move(total(part1, back1), backward)
    from_far = move(total(part2, move(away(part2), over_y)), onward)
    from_last = move(total(part3, move(away(part3), over_y), after(from_far, from_next)), onward)
    return total(part0, back0, from_next, from_last)


def solution(mesh):
    in_specs = (
        P("expert", "section"),
        P("expert", None),
        P("expert", None),
        P("expert", None, "section"),
        P("expert", None, "section"),
    )
    out_specs = P("expert", "section")
    fits = mesh.shape["section"] == 2 and mesh.shape["expert"] == 16
    return jax.shard_map(pair_shards if fits else shards, mesh=mesh, in_specs=in_specs, out_specs=out_specs, check_vma=False)
```

```python
import functools

import jax
import jax.numpy as jnp
import numpy as np
from jax import lax
from jax.experimental import pallas as pl
from jax.experimental.pallas import tpu as pltpu
from jax.sharding import PartitionSpec as P

UNITS = 64
SCALE = 1.0 / 256.0
VMEM = 40 * 1024 * 1024


def group_of(capacity):
    count = 2
    while (count * capacity) % 16:
        count *= 2
    return count


def slot_map(code, group, capacity):
    line = jnp.concatenate(
        [code[i : i + 1] + jnp.where(code[i : i + 1] >= 0, i * capacity * 256, 0) for i in range(group)], axis=1
    )
    slot, weight = line >> 8, line & 255
    places = lax.broadcasted_iota(jnp.int32, (group * capacity, line.shape[1]), 0)
    return places == slot, weight


def up_kernel(group, capacity, code_ref, tokens_ref, weight_ref, hidden_ref, rows_ref):
    groups = tokens_ref.shape[0] // group
    sections, rows, width = tokens_ref.shape[1:]
    size = group * capacity
    for g in range(groups):
        onehot, _ = slot_map(code_ref[0, g * group : (g + 1) * group], group, capacity)
        onehot = onehot.astype(jnp.bfloat16)
        for s in range(sections):
            block = jnp.concatenate([tokens_ref[g * group + i, s] for i in range(group)], axis=0)
            picked = jnp.dot(onehot, block, preferred_element_type=jnp.float32)
            rows_ref[g * size : (g + 1) * size, s * width : (s + 1) * width] = picked.astype(jnp.bfloat16)
    columns = weight_ref.shape[1]
    pair = 4 * UNITS

    def products(first, count):
        return jnp.dot(rows_ref[...], weight_ref[:, pl.ds(first, count)], preferred_element_type=jnp.float32)

    def mix(gate, up):
        return (gate / (1.0 + jnp.exp(-gate)) * up).astype(jnp.bfloat16)

    @pl.loop(0, columns // pair)
    def _(p):
        both = products(pl.multiple_of(p * pair, pair), pair)
        one, two = both[:, : 2 * UNITS], both[:, 2 * UNITS :]
        low = lax.broadcasted_iota(jnp.int32, one.shape, 1) < UNITS
        gate = jnp.where(low, one, pltpu.roll(two, UNITS, 1))
        up = jnp.where(low, pltpu.roll(one, UNITS, 1), two)
        hidden_ref[:, pl.ds(pl.multiple_of(p * 2 * UNITS, 2 * UNITS), 2 * UNITS)] = mix(gate, up)

    if columns % pair:
        start = columns // pair * pair
        both = products(start, 2 * UNITS)
        hidden_ref[:, start // 2 :] = mix(both, pltpu.roll(both, UNITS, 1))[:, :UNITS]


def down_kernel(group, capacity, code_ref, hidden_ref, weight_ref, out_ref, result_ref):
    sections, _, units = hidden_ref.shape
    groups = code_ref.shape[1] // group
    size = group * capacity
    wide = weight_ref.shape[1]
    step = min(512, wide)

    @pl.loop(0, wide // step)
    def _(p):
        at = pl.ds(pl.multiple_of(p * step, step), step)
        total = jnp.dot(hidden_ref[0], weight_ref[0:units, at], preferred_element_type=jnp.float32)
        for s in range(1, sections):
            total += jnp.dot(
                hidden_ref[s], weight_ref[s * units : (s + 1) * units, at], preferred_element_type=jnp.float32
            )
        result_ref[...] = total.astype(jnp.bfloat16)
        for g in range(groups):
            onehot, weight = slot_map(code_ref[0, g * group : (g + 1) * group], group, capacity)
            scaled = jnp.where(onehot, weight.astype(jnp.float32) * SCALE, 0.0).astype(jnp.bfloat16)
            mixed = lax.dot_general(
                scaled,
                result_ref[g * size : (g + 1) * size],
                (((0,), (0,)), ((), ())),
                preferred_element_type=jnp.float32,
            )
            tall = scaled.shape[1]
            out_ref[g * tall : (g + 1) * tall, at] = mixed.astype(jnp.bfloat16)


def up_call(code, tokens, weight, capacity):
    blocks, sections, rows, width = tokens.shape
    group = group_of(capacity)
    take = min(blocks, 2 * group)
    depth, columns = weight.shape
    tall = take * capacity
    flops = 2 * blocks * capacity * depth * (columns + group * rows)
    return pl.pallas_call(
        functools.partial(up_kernel, group, capacity),
        grid=(blocks // take,),
        in_specs=[
            pl.BlockSpec((1, take, rows), lambda i: (i, 0, 0)),
            pl.BlockSpec((take, sections, rows, width), lambda i: (i, 0, 0, 0)),
            pl.BlockSpec((depth, columns), lambda i: (0, 0), pipeline_mode=pl.Buffered(1)),
        ],
        out_specs=pl.BlockSpec((tall, columns // 2), lambda i: (i, 0)),
        out_shape=jax.ShapeDtypeStruct((blocks * capacity, columns // 2), jnp.bfloat16),
        scratch_shapes=[pltpu.VMEM((tall, depth), jnp.bfloat16)],
        compiler_params=pltpu.CompilerParams(vmem_limit_bytes=48 * 1024 * 1024),
        cost_estimate=pl.CostEstimate(
            flops=flops, bytes_accessed=2 * (tokens.size + weight.size), transcendentals=blocks * capacity * columns // 2
        ),
        name="gate_up",
    )(code.reshape(blocks // take, take, rows), tokens, weight)


def down_call(code, hidden, weight, capacity):
    blocks, rows = code.shape
    sections, _, units = hidden.shape
    group = group_of(capacity)
    take = min(blocks, 2 * group)
    depth, wide = weight.shape
    tall = take * capacity
    return pl.pallas_call(
        functools.partial(down_kernel, group, capacity),
        grid=(blocks // take,),
        in_specs=[
            pl.BlockSpec((1, take, rows), lambda i: (i, 0, 0)),
            pl.BlockSpec((sections, tall, units), lambda i: (0, i, 0)),
            pl.BlockSpec((depth, wide), lambda i: (0, 0), pipeline_mode=pl.Buffered(1)),
        ],
        out_specs=pl.BlockSpec((take * rows, wide), lambda i: (i, 0)),
        out_shape=jax.ShapeDtypeStruct((blocks * rows, wide), jnp.bfloat16),
        scratch_shapes=[pltpu.VMEM((tall, min(512, wide)), jnp.bfloat16)],
        compiler_params=pltpu.CompilerParams(vmem_limit_bytes=48 * 1024 * 1024),
        cost_estimate=pl.CostEstimate(
            flops=2 * blocks * capacity * wide * (depth + group * rows),
            bytes_accessed=2 * (hidden.size + weight.size + blocks * rows * wide),
            transcendentals=0,
        ),
        name="down",
    )(code.reshape(blocks // take, take, rows), hidden, weight)


def block_codes(k, own, where_ref, code_ref):
    return jnp.concatenate([code_ref[pl.ds(where_ref[k, 2 * own + i], 1), :] for i in range(2)], axis=0)


def pick_kernel(capacity, k, where_ref, code_ref, *refs):
    pairs, weight_hbm = refs[:4], refs[4]
    hidden_ref, pair_ref, weight_ref, rows_ref, sems = refs[-5:]
    rows, width = pairs[0].shape[1:]
    span = 8 * UNITS
    spans = weight_hbm.shape[1] // span
    x, c = where_ref[k, 4], where_ref[k, 5]

    def weight_copy(j):
        at = pl.ds(pl.multiple_of(j * span, span), span)
        return pltpu.make_async_copy(weight_hbm.at[:, at], weight_ref.at[:, at], sems.at[4 + j])

    copies = [pltpu.make_async_copy(v, pair_ref.at[pl.ds(2 * i, 2)], sems.at[i]) for i, v in enumerate(pairs)]
    for copy in copies:
        copy.start()
    for j in range(spans):
        weight_copy(j).start()
    for own in range(2):
        core = c ^ own
        onehot, _ = slot_map(block_codes(k, own, where_ref, code_ref), 2, capacity)
        onehot = onehot.astype(jnp.bfloat16)
        copies[2 * own].wait()
        copies[2 * own + 1].wait()
        for section, near, far in ((x, 0, 2 - core), (1 - x, 1 + core, 3)):
            block = jnp.concatenate([pair_ref[4 * own + near], pair_ref[4 * own + far]], axis=0)
            picked = jnp.dot(onehot, block, preferred_element_type=jnp.float32)
            at = pl.ds(pl.multiple_of(section * width, width), width)
            rows_ref[2 * own * capacity : 2 * (own + 1) * capacity, at] = picked.astype(jnp.bfloat16)

    @pl.loop(0, spans)
    def _(j):
        weight_copy(j).wait()
        at = pl.ds(pl.multiple_of(j * span, span), span)
        both = jnp.dot(rows_ref[...], weight_ref[:, at], preferred_element_type=jnp.float32)
        for p in range(2):
            one, two = both[:, 4 * p * UNITS : (4 * p + 2) * UNITS], both[:, (4 * p + 2) * UNITS : 4 * (p + 1) * UNITS]
            low = lax.broadcasted_iota(jnp.int32, one.shape, 1) < UNITS
            gate = jnp.where(low, one, pltpu.roll(two, UNITS, 1))
            up = jnp.where(low, pltpu.roll(one, UNITS, 1), two)
            half = pl.ds(pl.multiple_of((2 * j + p) * 2 * UNITS, 2 * UNITS), 2 * UNITS)
            hidden_ref[:, half] = (gate / (1.0 + jnp.exp(-gate)) * up).astype(jnp.bfloat16)


def sum_kernel(capacity, k, where_ref, code_ref, *refs):
    mine_hbm, other_hbm, weight_hbm = refs[:3]
    keep_hbm, send_hbm, hidden_ref, weight_ref, out_ref, sems = refs[-6:]
    rows = code_ref.shape[1]
    units = mine_hbm.shape[1]
    span = 512
    spans = weight_hbm.shape[1] // span

    def weight_copy(j):
        at = pl.ds(pl.multiple_of(j * span, span), span)
        return pltpu.make_async_copy(weight_hbm.at[:, at], weight_ref.at[:, at], sems.at[2 + j])

    def out_copy(j, i, to):
        at = pl.ds(pl.multiple_of(j * span, span), span)
        sem = sems.at[2 + spans + 2 * j + i]
        return pltpu.make_async_copy(out_ref.at[pl.ds(2 * i, 2), :, at], to.at[:, :, at], sem)

    copies = [pltpu.make_async_copy(v, hidden_ref.at[i], sems.at[i]) for i, v in enumerate((mine_hbm, other_hbm))]
    for copy in copies:
        copy.start()
    for j in range(spans):
        weight_copy(j).start()
    scaled = []
    for own in range(2):
        onehot, weight = slot_map(block_codes(k, own, where_ref, code_ref), 2, capacity)
        scaled.append(jnp.where(onehot, weight.astype(jnp.float32) * SCALE, 0.0).astype(jnp.bfloat16))
    me = where_ref[k, 4]
    mine_at = pl.ds(pl.multiple_of(me * units, units), units)
    other_at = pl.ds(pl.multiple_of((1 - me) * units, units), units)
    for copy in copies:
        copy.wait()

    @pl.loop(0, spans)
    def _(j):
        weight_copy(j).wait()
        at = pl.ds(pl.multiple_of(j * span, span), span)
        total = jnp.dot(hidden_ref[0], weight_ref[mine_at, at], preferred_element_type=jnp.float32)
        total += jnp.dot(hidden_ref[1], weight_ref[other_at, at], preferred_element_type=jnp.float32)
        result = total.astype(jnp.bfloat16)
        for own in range(2):
            mixed = lax.dot_general(
                scaled[own],
                result[2 * own * capacity : 2 * (own + 1) * capacity],
                (((0,), (0,)), ((), ())),
                preferred_element_type=jnp.float32,
            )
            out_ref[2 * own : 2 * own + 2, :, at] = mixed.astype(jnp.bfloat16).reshape(2, rows, span)
        out_copy(j, 0, keep_hbm).start()
        out_copy(j, 1, send_hbm).start()

    for j in range(spans):
        out_copy(j, 0, keep_hbm).wait()
        out_copy(j, 1, send_hbm).wait()


def pick_call(k, where, code, pairs, weight, earlier, capacity):
    _, rows, width = pairs[0].shape
    depth, columns = weight.shape
    tall = 4 * capacity
    anywhere = pl.BlockSpec(memory_space=pl.ANY)
    return pl.pallas_call(
        functools.partial(pick_kernel, capacity, k),
        in_specs=[
            pl.BlockSpec(memory_space=pltpu.SMEM),
            pl.BlockSpec(memory_space=pltpu.VMEM),
            *[anywhere] * (5 + len(earlier)),
        ],
        out_specs=pl.BlockSpec(memory_space=pltpu.VMEM),
        out_shape=jax.ShapeDtypeStruct((tall, columns // 2), jnp.bfloat16),
        scratch_shapes=[
            pltpu.VMEM((8, rows, width), jnp.bfloat16),
            pltpu.VMEM((depth, columns), jnp.bfloat16),
            pltpu.VMEM((tall, depth), jnp.bfloat16),
            pltpu.SemaphoreType.DMA((4 + columns // (8 * UNITS),)),
        ],
        compiler_params=pltpu.CompilerParams(vmem_limit_bytes=VMEM),
        cost_estimate=pl.CostEstimate(
            flops=2 * tall * depth * (columns + rows),
            bytes_accessed=2 * (8 * rows * width + weight.size + tall * columns // 2),
            transcendentals=tall * columns // 2,
        ),
        name="gate_up",
    )(where, code, *pairs, weight, *earlier)


def sum_call(k, where, code, mine, other, weight, earlier, capacity):
    rows = code.shape[1]
    depth, wide = weight.shape
    tall, units = mine.shape
    anywhere = pl.BlockSpec(memory_space=pl.ANY)
    return pl.pallas_call(
        functools.partial(sum_kernel, capacity, k),
        in_specs=[
            pl.BlockSpec(memory_space=pltpu.SMEM),
            pl.BlockSpec(memory_space=pltpu.VMEM),
            *[anywhere] * (3 + len(earlier)),
        ],
        out_specs=[anywhere] * 2,
        out_shape=[jax.ShapeDtypeStruct((2, rows, wide), jnp.bfloat16)] * 2,
        scratch_shapes=[
            pltpu.VMEM((2, tall, units), jnp.bfloat16),
            pltpu.VMEM((depth, wide), jnp.bfloat16),
            pltpu.VMEM((4, rows, wide), jnp.bfloat16),
            pltpu.SemaphoreType.DMA((2 + 3 * (wide // 512),)),
        ],
        compiler_params=pltpu.CompilerParams(vmem_limit_bytes=VMEM),
        cost_estimate=pl.CostEstimate(
            flops=2 * wide * (tall * depth + 4 * rows * capacity),
            bytes_accessed=2 * (2 * mine.size + weight.size + 4 * rows * wide),
            transcendentals=0,
        ),
        name="down",
    )(where, code, mine, other, weight, *earlier)


def codes_of(expert_ids, numerators, experts):
    rows = expert_ids.shape[0]
    named = expert_ids.T[None] == jnp.arange(experts, dtype=jnp.int32)[:, None, None]
    hits = jnp.any(named, axis=1)
    weight = jnp.sum(jnp.where(named, numerators.T[None], 0), axis=1)
    earlier = jnp.arange(rows)[:, None] < jnp.arange(rows)[None, :]
    rank = jnp.dot(hits.astype(jnp.bfloat16), earlier.astype(jnp.bfloat16), preferred_element_type=jnp.float32)
    return jnp.where(hits, rank.astype(jnp.int32) * 256 + weight, -1)


def shards(tokens, expert_ids, numerators, gate_up_weight, down_weight):
    rows, width = tokens.shape
    experts = lax.axis_size("expert")
    capacity = rows * expert_ids.shape[1] * 5 // (4 * experts)
    chips = experts // 2
    across = [[2 * i + c for i in range(chips)] for c in range(2)]
    pairs = [[2 * i, 2 * i + 1] for i in range(chips)]

    codes = lax.all_gather(codes_of(expert_ids, numerators, experts), "expert", axis=0)
    code = lax.dynamic_index_in_dim(codes, lax.axis_index("expert"), 1, keepdims=False)
    code = code.reshape(chips, 2, rows).swapaxes(0, 1).reshape(experts, rows)

    wide = lax.all_gather(tokens, "section", axis=0)
    half = lax.all_gather(wide, "expert", axis=0, axis_index_groups=across)
    whole = lax.all_gather(half, "expert", axis=0, axis_index_groups=pairs)
    whole = whole.reshape((experts,) + wide.shape)

    hidden = up_call(code, whole, gate_up_weight[0], capacity)
    hidden = lax.all_gather(hidden, "section", axis=0)
    part = down_call(code, hidden, down_weight[0], capacity)

    part = part.reshape(2, chips * rows, width)
    part = lax.psum_scatter(part, "expert", scatter_dimension=0, axis_index_groups=pairs, tiled=False)
    return lax.psum_scatter(part, "expert", scatter_dimension=0, axis_index_groups=across, tiled=True)


def pair_shards(tokens, expert_ids, numerators, gate_up_weight, down_weight):
    rows, width = tokens.shape
    experts = lax.axis_size("expert")
    layers = experts // 4
    capacity = rows * expert_ids.shape[1] * 5 // (4 * experts)
    axes = ("section", "expert")
    ring = [0, *range(1, layers, 2), *reversed(range(2, layers, 2))]
    following = {z: ring[(p + 1) % layers] for p, z in enumerate(ring)}

    def perm(place):
        moves = []
        for x in range(2):
            for z in range(layers):
                for y in range(2):
                    for c in range(2):
                        tx, tz, ty, tc = place(x, z, y, c)
                        moves.append(((x * layers + z) * 4 + y * 2 + c, (tx * layers + tz) * 4 + ty * 2 + tc))
        return moves

    onward = perm(lambda x, z, y, c: (x, following[z], y, c))
    backward = [(to, source) for source, to in onward]
    first = perm(lambda x, z, y, c: (x ^ (1 - c), z, y ^ c, c))
    second = perm(lambda x, z, y, c: (x ^ c, z, y ^ (1 - c), c))
    sibling = perm(lambda x, z, y, c: (x, z, y, 1 - c))
    over_x = perm(lambda x, z, y, c: (1 - x, z, y, c))
    over_y = perm(lambda x, z, y, c: (x, z, 1 - y, c))

    def move(value, moves):
        return lax.ppermute(value, axes, moves)

    table = np.zeros((2, layers, 2, 2, layers, 6), np.int32)
    for x, z, y, c, k in np.ndindex(2, layers, 2, 2, layers):
        at = ring[(ring.index(z) - k) % layers] * 4
        table[x, z, y, c, k] = [at + (y ^ (i & 1)) * 2 + (c ^ (i >> 1)) for i in range(4)] + [x, c]
    device = lax.axis_index("section") * experts + lax.axis_index("expert")
    where = lax.dynamic_index_in_dim(jnp.asarray(table.reshape(2 * experts, layers, 6)), device, 0, keepdims=False)
    def after(value, *done):
        return lax.optimization_barrier((value, *done))[0]

    near = move(tokens, first)
    later = move(tokens, onward)
    near_later = move(later, first)
    last = move(later, onward)
    named = codes_of(after(expert_ids, last), numerators, experts)
    code = lax.all_to_all(named, "expert", split_axis=0, concat_axis=0, tiled=True)
    pairs = [jnp.stack([tokens, near]), jnp.stack([later, near_later])]
    crosses = [move(pairs[0], second)]
    near_last = move(after(last, near_later, crosses[0]), first)
    pairs.append(jnp.stack([after(last, code), near_last]))
    pairs.append(move(pairs[2], onward))
    crosses.append(move(after(pairs[1], pairs[2]), second))
    crosses.append(move(pairs[2], second))

    def spread(k, *done):
        return [pairs[k], crosses[k], move(pairs[k], sibling), move(after(crosses[k], *done), sibling)]

    def gate_up(k, shards_of, *earlier):
        mine = pick_call(k, where, code, shards_of, gate_up_weight[0], earlier, capacity)
        return mine, move(mine, over_x)

    def down(k, hidden, *earlier):
        keep, send = sum_call(k, where, code, *hidden, down_weight[0], earlier, capacity)
        return keep, move(send, sibling)

    def away(part):
        keep, got = part
        return (keep[1].astype(jnp.float32) + got[1].astype(jnp.float32)).astype(jnp.bfloat16)

    def total(part, back, *hop):
        terms = [v.astype(jnp.float32) for v in (part[0][0], part[1][0], back, *hop)]
        return functools.reduce(jnp.add, terms).astype(jnp.bfloat16)

    hidden0 = gate_up(0, spread(0))
    crosses.append(move(after(pairs[3], hidden0[1]), second))
    hidden1 = gate_up(1, spread(1, hidden0[0]), hidden0[0], pairs[3])
    hidden2 = gate_up(2, spread(2, hidden0[0]), hidden1[0])
    shards3 = spread(3, hidden1[0])
    part1 = down(1, hidden1, hidden2[0], shards3[3])
    back1 = move(away(part1), over_y)
    hidden3 = gate_up(3, shards3, part1[0])
    part2 = down(2, hidden2, hidden3[0], back1)
    part0 = down(0, hidden0, part2[0])
    part3 = down(3, hidden3, part0[0])
    from_next = move(total(part1, back1), backward)
    from_far = move(after(total(part2, move(away(part2), over_y)), from_next), onward)
    back3 = move(away(part3), over_y)
    from_last = move(total(part3, back3, from_far), onward)
    back0 = move(after(away(part0), back3), over_y)
    return total(part0, back0, from_next, from_last)


def solution(mesh):
    in_specs = (
        P("expert", "section"),
        P("expert", None),
        P("expert", None),
        P("expert", None, "section"),
        P("expert", None, "section"),
    )
    out_specs = P("expert", "section")
    fits = mesh.shape["section"] == 2 and mesh.shape["expert"] == 16
    return jax.shard_map(pair_shards if fits else shards, mesh=mesh, in_specs=in_specs, out_specs=out_specs, check_vma=False)
```

```python
import functools

import jax
import jax.numpy as jnp
import numpy as np
from jax import lax
from jax.experimental import pallas as pl
from jax.experimental.pallas import tpu as pltpu
from jax.sharding import PartitionSpec as P

UNITS = 64
SCALE = 1.0 / 256.0
VMEM = 40 * 1024 * 1024


def group_of(capacity):
    count = 2
    while (count * capacity) % 16:
        count *= 2
    return count


def slot_map(code, group, capacity):
    line = jnp.concatenate(
        [code[i : i + 1] + jnp.where(code[i : i + 1] >= 0, i * capacity * 256, 0) for i in range(group)], axis=1
    )
    slot, weight = line >> 8, line & 255
    places = lax.broadcasted_iota(jnp.int32, (group * capacity, line.shape[1]), 0)
    return places == slot, weight


def up_kernel(group, capacity, code_ref, tokens_ref, weight_ref, hidden_ref, rows_ref):
    groups = tokens_ref.shape[0] // group
    sections, rows, width = tokens_ref.shape[1:]
    size = group * capacity
    for g in range(groups):
        onehot, _ = slot_map(code_ref[0, g * group : (g + 1) * group], group, capacity)
        onehot = onehot.astype(jnp.bfloat16)
        for s in range(sections):
            block = jnp.concatenate([tokens_ref[g * group + i, s] for i in range(group)], axis=0)
            picked = jnp.dot(onehot, block, preferred_element_type=jnp.float32)
            rows_ref[g * size : (g + 1) * size, s * width : (s + 1) * width] = picked.astype(jnp.bfloat16)
    columns = weight_ref.shape[1]
    pair = 4 * UNITS

    def products(first, count):
        return jnp.dot(rows_ref[...], weight_ref[:, pl.ds(first, count)], preferred_element_type=jnp.float32)

    def mix(gate, up):
        return (gate / (1.0 + jnp.exp(-gate)) * up).astype(jnp.bfloat16)

    @pl.loop(0, columns // pair)
    def _(p):
        both = products(pl.multiple_of(p * pair, pair), pair)
        one, two = both[:, : 2 * UNITS], both[:, 2 * UNITS :]
        low = lax.broadcasted_iota(jnp.int32, one.shape, 1) < UNITS
        gate = jnp.where(low, one, pltpu.roll(two, UNITS, 1))
        up = jnp.where(low, pltpu.roll(one, UNITS, 1), two)
        hidden_ref[:, pl.ds(pl.multiple_of(p * 2 * UNITS, 2 * UNITS), 2 * UNITS)] = mix(gate, up)

    if columns % pair:
        start = columns // pair * pair
        both = products(start, 2 * UNITS)
        hidden_ref[:, start // 2 :] = mix(both, pltpu.roll(both, UNITS, 1))[:, :UNITS]


def down_kernel(group, capacity, code_ref, hidden_ref, weight_ref, out_ref, result_ref):
    sections, _, units = hidden_ref.shape
    groups = code_ref.shape[1] // group
    size = group * capacity
    wide = weight_ref.shape[1]
    step = min(512, wide)

    @pl.loop(0, wide // step)
    def _(p):
        at = pl.ds(pl.multiple_of(p * step, step), step)
        total = jnp.dot(hidden_ref[0], weight_ref[0:units, at], preferred_element_type=jnp.float32)
        for s in range(1, sections):
            total += jnp.dot(
                hidden_ref[s], weight_ref[s * units : (s + 1) * units, at], preferred_element_type=jnp.float32
            )
        result_ref[...] = total.astype(jnp.bfloat16)
        for g in range(groups):
            onehot, weight = slot_map(code_ref[0, g * group : (g + 1) * group], group, capacity)
            scaled = jnp.where(onehot, weight.astype(jnp.float32) * SCALE, 0.0).astype(jnp.bfloat16)
            mixed = lax.dot_general(
                scaled,
                result_ref[g * size : (g + 1) * size],
                (((0,), (0,)), ((), ())),
                preferred_element_type=jnp.float32,
            )
            tall = scaled.shape[1]
            out_ref[g * tall : (g + 1) * tall, at] = mixed.astype(jnp.bfloat16)


def up_call(code, tokens, weight, capacity):
    blocks, sections, rows, width = tokens.shape
    group = group_of(capacity)
    take = min(blocks, 2 * group)
    depth, columns = weight.shape
    tall = take * capacity
    flops = 2 * blocks * capacity * depth * (columns + group * rows)
    return pl.pallas_call(
        functools.partial(up_kernel, group, capacity),
        grid=(blocks // take,),
        in_specs=[
            pl.BlockSpec((1, take, rows), lambda i: (i, 0, 0)),
            pl.BlockSpec((take, sections, rows, width), lambda i: (i, 0, 0, 0)),
            pl.BlockSpec((depth, columns), lambda i: (0, 0), pipeline_mode=pl.Buffered(1)),
        ],
        out_specs=pl.BlockSpec((tall, columns // 2), lambda i: (i, 0)),
        out_shape=jax.ShapeDtypeStruct((blocks * capacity, columns // 2), jnp.bfloat16),
        scratch_shapes=[pltpu.VMEM((tall, depth), jnp.bfloat16)],
        compiler_params=pltpu.CompilerParams(vmem_limit_bytes=48 * 1024 * 1024),
        cost_estimate=pl.CostEstimate(
            flops=flops, bytes_accessed=2 * (tokens.size + weight.size), transcendentals=blocks * capacity * columns // 2
        ),
        name="gate_up",
    )(code.reshape(blocks // take, take, rows), tokens, weight)


def down_call(code, hidden, weight, capacity):
    blocks, rows = code.shape
    sections, _, units = hidden.shape
    group = group_of(capacity)
    take = min(blocks, 2 * group)
    depth, wide = weight.shape
    tall = take * capacity
    return pl.pallas_call(
        functools.partial(down_kernel, group, capacity),
        grid=(blocks // take,),
        in_specs=[
            pl.BlockSpec((1, take, rows), lambda i: (i, 0, 0)),
            pl.BlockSpec((sections, tall, units), lambda i: (0, i, 0)),
            pl.BlockSpec((depth, wide), lambda i: (0, 0), pipeline_mode=pl.Buffered(1)),
        ],
        out_specs=pl.BlockSpec((take * rows, wide), lambda i: (i, 0)),
        out_shape=jax.ShapeDtypeStruct((blocks * rows, wide), jnp.bfloat16),
        scratch_shapes=[pltpu.VMEM((tall, min(512, wide)), jnp.bfloat16)],
        compiler_params=pltpu.CompilerParams(vmem_limit_bytes=48 * 1024 * 1024),
        cost_estimate=pl.CostEstimate(
            flops=2 * blocks * capacity * wide * (depth + group * rows),
            bytes_accessed=2 * (hidden.size + weight.size + blocks * rows * wide),
            transcendentals=0,
        ),
        name="down",
    )(code.reshape(blocks // take, take, rows), hidden, weight)


def block_codes(k, own, where_ref, code_ref):
    return jnp.concatenate([code_ref[pl.ds(where_ref[k, 2 * own + i], 1), :] for i in range(2)], axis=0)


def pick_kernel(capacity, k, where_ref, code_ref, *refs):
    pairs, weight_hbm = refs[:4], refs[4]
    hidden_ref, pair_ref, weight_ref, rows_ref, sems = refs[-5:]
    rows, width = pairs[0].shape[1:]
    span = 8 * UNITS
    spans = weight_hbm.shape[1] // span
    x, c = where_ref[k, 4], where_ref[k, 5]

    def weight_copy(j):
        at = pl.ds(pl.multiple_of(j * span, span), span)
        return pltpu.make_async_copy(weight_hbm.at[:, at], weight_ref.at[:, at], sems.at[4 + j])

    copies = [pltpu.make_async_copy(v, pair_ref.at[pl.ds(2 * i, 2)], sems.at[i]) for i, v in enumerate(pairs)]
    for copy in copies:
        copy.start()
    for j in range(spans):
        weight_copy(j).start()
    for own in range(2):
        core = c ^ own
        onehot, _ = slot_map(block_codes(k, own, where_ref, code_ref), 2, capacity)
        onehot = onehot.astype(jnp.bfloat16)
        copies[2 * own].wait()
        copies[2 * own + 1].wait()
        for section, near, far in ((x, 0, 2 - core), (1 - x, 1 + core, 3)):
            block = jnp.concatenate([pair_ref[4 * own + near], pair_ref[4 * own + far]], axis=0)
            picked = jnp.dot(onehot, block, preferred_element_type=jnp.float32)
            at = pl.ds(pl.multiple_of(section * width, width), width)
            rows_ref[2 * own * capacity : 2 * (own + 1) * capacity, at] = picked.astype(jnp.bfloat16)

    @pl.loop(0, spans)
    def _(j):
        weight_copy(j).wait()
        at = pl.ds(pl.multiple_of(j * span, span), span)
        both = jnp.dot(rows_ref[...], weight_ref[:, at], preferred_element_type=jnp.float32)
        for p in range(2):
            one, two = both[:, 4 * p * UNITS : (4 * p + 2) * UNITS], both[:, (4 * p + 2) * UNITS : 4 * (p + 1) * UNITS]
            low = lax.broadcasted_iota(jnp.int32, one.shape, 1) < UNITS
            gate = jnp.where(low, one, pltpu.roll(two, UNITS, 1))
            up = jnp.where(low, pltpu.roll(one, UNITS, 1), two)
            half = pl.ds(pl.multiple_of((2 * j + p) * 2 * UNITS, 2 * UNITS), 2 * UNITS)
            hidden_ref[:, half] = (gate / (1.0 + jnp.exp(-gate)) * up).astype(jnp.bfloat16)


def sum_kernel(capacity, k, where_ref, code_ref, *refs):
    mine_hbm, other_hbm, weight_hbm = refs[:3]
    keep_hbm, send_hbm, hidden_ref, weight_ref, out_ref, sems = refs[-6:]
    rows = code_ref.shape[1]
    units = mine_hbm.shape[1]
    span = 512
    spans = weight_hbm.shape[1] // span

    def weight_copy(j):
        at = pl.ds(pl.multiple_of(j * span, span), span)
        return pltpu.make_async_copy(weight_hbm.at[:, at], weight_ref.at[:, at], sems.at[2 + j])

    def out_copy(j, i, to):
        at = pl.ds(pl.multiple_of(j * span, span), span)
        sem = sems.at[2 + spans + 2 * j + i]
        return pltpu.make_async_copy(out_ref.at[pl.ds(2 * i, 2), :, at], to.at[:, :, at], sem)

    copies = [pltpu.make_async_copy(v, hidden_ref.at[i], sems.at[i]) for i, v in enumerate((mine_hbm, other_hbm))]
    for copy in copies:
        copy.start()
    for j in range(spans):
        weight_copy(j).start()
    scaled = []
    for own in range(2):
        onehot, weight = slot_map(block_codes(k, own, where_ref, code_ref), 2, capacity)
        scaled.append(jnp.where(onehot, weight.astype(jnp.float32) * SCALE, 0.0).astype(jnp.bfloat16))
    me = where_ref[k, 4]
    mine_at = pl.ds(pl.multiple_of(me * units, units), units)
    other_at = pl.ds(pl.multiple_of((1 - me) * units, units), units)
    for copy in copies:
        copy.wait()

    @pl.loop(0, spans)
    def _(j):
        weight_copy(j).wait()
        at = pl.ds(pl.multiple_of(j * span, span), span)
        total = jnp.dot(hidden_ref[0], weight_ref[mine_at, at], preferred_element_type=jnp.float32)
        total += jnp.dot(hidden_ref[1], weight_ref[other_at, at], preferred_element_type=jnp.float32)
        result = total.astype(jnp.bfloat16)
        for own in range(2):
            mixed = lax.dot_general(
                scaled[own],
                result[2 * own * capacity : 2 * (own + 1) * capacity],
                (((0,), (0,)), ((), ())),
                preferred_element_type=jnp.float32,
            )
            out_ref[2 * own : 2 * own + 2, :, at] = mixed.astype(jnp.bfloat16).reshape(2, rows, span)
        out_copy(j, 0, keep_hbm).start()
        out_copy(j, 1, send_hbm).start()

    for j in range(spans):
        out_copy(j, 0, keep_hbm).wait()
        out_copy(j, 1, send_hbm).wait()


def pick_call(k, where, code, pairs, weight, earlier, capacity):
    _, rows, width = pairs[0].shape
    depth, columns = weight.shape
    tall = 4 * capacity
    anywhere = pl.BlockSpec(memory_space=pl.ANY)
    return pl.pallas_call(
        functools.partial(pick_kernel, capacity, k),
        in_specs=[
            pl.BlockSpec(memory_space=pltpu.SMEM),
            pl.BlockSpec(memory_space=pltpu.VMEM),
            *[anywhere] * (5 + len(earlier)),
        ],
        out_specs=pl.BlockSpec(memory_space=pltpu.VMEM),
        out_shape=jax.ShapeDtypeStruct((tall, columns // 2), jnp.bfloat16),
        scratch_shapes=[
            pltpu.VMEM((8, rows, width), jnp.bfloat16),
            pltpu.VMEM((depth, columns), jnp.bfloat16),
            pltpu.VMEM((tall, depth), jnp.bfloat16),
            pltpu.SemaphoreType.DMA((4 + columns // (8 * UNITS),)),
        ],
        compiler_params=pltpu.CompilerParams(vmem_limit_bytes=VMEM),
        cost_estimate=pl.CostEstimate(
            flops=2 * tall * depth * (columns + rows),
            bytes_accessed=2 * (8 * rows * width + weight.size + tall * columns // 2),
            transcendentals=tall * columns // 2,
        ),
        name="gate_up",
    )(where, code, *pairs, weight, *earlier)


def sum_call(k, where, code, mine, other, weight, earlier, capacity):
    rows = code.shape[1]
    depth, wide = weight.shape
    tall, units = mine.shape
    anywhere = pl.BlockSpec(memory_space=pl.ANY)
    return pl.pallas_call(
        functools.partial(sum_kernel, capacity, k),
        in_specs=[
            pl.BlockSpec(memory_space=pltpu.SMEM),
            pl.BlockSpec(memory_space=pltpu.VMEM),
            *[anywhere] * (3 + len(earlier)),
        ],
        out_specs=[anywhere] * 2,
        out_shape=[jax.ShapeDtypeStruct((2, rows, wide), jnp.bfloat16)] * 2,
        scratch_shapes=[
            pltpu.VMEM((2, tall, units), jnp.bfloat16),
            pltpu.VMEM((depth, wide), jnp.bfloat16),
            pltpu.VMEM((4, rows, wide), jnp.bfloat16),
            pltpu.SemaphoreType.DMA((2 + 3 * (wide // 512),)),
        ],
        compiler_params=pltpu.CompilerParams(vmem_limit_bytes=VMEM),
        cost_estimate=pl.CostEstimate(
            flops=2 * wide * (tall * depth + 4 * rows * capacity),
            bytes_accessed=2 * (2 * mine.size + weight.size + 4 * rows * wide),
            transcendentals=0,
        ),
        name="down",
    )(where, code, mine, other, weight, *earlier)


def codes_of(expert_ids, numerators, experts):
    rows = expert_ids.shape[0]
    named = expert_ids.T[None] == jnp.arange(experts, dtype=jnp.int32)[:, None, None]
    hits = jnp.any(named, axis=1)
    weight = jnp.sum(jnp.where(named, numerators.T[None], 0), axis=1)
    earlier = jnp.arange(rows)[:, None] < jnp.arange(rows)[None, :]
    rank = jnp.dot(hits.astype(jnp.bfloat16), earlier.astype(jnp.bfloat16), preferred_element_type=jnp.float32)
    return jnp.where(hits, rank.astype(jnp.int32) * 256 + weight, -1)


def shards(tokens, expert_ids, numerators, gate_up_weight, down_weight):
    rows, width = tokens.shape
    experts = lax.axis_size("expert")
    capacity = rows * expert_ids.shape[1] * 5 // (4 * experts)
    chips = experts // 2
    across = [[2 * i + c for i in range(chips)] for c in range(2)]
    pairs = [[2 * i, 2 * i + 1] for i in range(chips)]

    codes = lax.all_gather(codes_of(expert_ids, numerators, experts), "expert", axis=0)
    code = lax.dynamic_index_in_dim(codes, lax.axis_index("expert"), 1, keepdims=False)
    code = code.reshape(chips, 2, rows).swapaxes(0, 1).reshape(experts, rows)

    wide = lax.all_gather(tokens, "section", axis=0)
    half = lax.all_gather(wide, "expert", axis=0, axis_index_groups=across)
    whole = lax.all_gather(half, "expert", axis=0, axis_index_groups=pairs)
    whole = whole.reshape((experts,) + wide.shape)

    hidden = up_call(code, whole, gate_up_weight[0], capacity)
    hidden = lax.all_gather(hidden, "section", axis=0)
    part = down_call(code, hidden, down_weight[0], capacity)

    part = part.reshape(2, chips * rows, width)
    part = lax.psum_scatter(part, "expert", scatter_dimension=0, axis_index_groups=pairs, tiled=False)
    return lax.psum_scatter(part, "expert", scatter_dimension=0, axis_index_groups=across, tiled=True)


def pair_shards(tokens, expert_ids, numerators, gate_up_weight, down_weight):
    rows, width = tokens.shape
    experts = lax.axis_size("expert")
    layers = experts // 4
    capacity = rows * expert_ids.shape[1] * 5 // (4 * experts)
    axes = ("section", "expert")
    ring = [0, *range(1, layers, 2), *reversed(range(2, layers, 2))]
    following = {z: ring[(p + 1) % layers] for p, z in enumerate(ring)}

    def perm(place):
        moves = []
        for x in range(2):
            for z in range(layers):
                for y in range(2):
                    for c in range(2):
                        tx, tz, ty, tc = place(x, z, y, c)
                        moves.append(((x * layers + z) * 4 + y * 2 + c, (tx * layers + tz) * 4 + ty * 2 + tc))
        return moves

    onward = perm(lambda x, z, y, c: (x, following[z], y, c))
    backward = [(to, source) for source, to in onward]
    first = perm(lambda x, z, y, c: (x ^ (1 - c), z, y ^ c, c))
    second = perm(lambda x, z, y, c: (x ^ c, z, y ^ (1 - c), c))
    sibling = perm(lambda x, z, y, c: (x, z, y, 1 - c))
    over_x = perm(lambda x, z, y, c: (1 - x, z, y, c))
    over_y = perm(lambda x, z, y, c: (x, z, 1 - y, c))

    def move(value, moves):
        return lax.ppermute(value, axes, moves)

    table = np.zeros((2, layers, 2, 2, layers, 6), np.int32)
    for x, z, y, c, k in np.ndindex(2, layers, 2, 2, layers):
        at = ring[(ring.index(z) - k) % layers] * 4
        table[x, z, y, c, k] = [at + (y ^ (i & 1)) * 2 + (c ^ (i >> 1)) for i in range(4)] + [x, c]
    device = lax.axis_index("section") * experts + lax.axis_index("expert")
    where = lax.dynamic_index_in_dim(jnp.asarray(table.reshape(2 * experts, layers, 6)), device, 0, keepdims=False)
    def after(value, *done):
        return lax.optimization_barrier((value, *done))[0]

    near = move(tokens, first)
    later = move(tokens, onward)
    near_later = move(later, first)
    last = move(later, onward)
    named = codes_of(after(expert_ids, later), numerators, experts)
    code = lax.all_to_all(named, "expert", split_axis=0, concat_axis=0, tiled=True)
    pairs = [jnp.stack([tokens, near]), jnp.stack([later, near_later])]
    crosses = [move(pairs[0], second)]
    near_last = move(after(last, near_later, crosses[0], code), first)
    pairs.append(jnp.stack([last, near_last]))
    pairs.append(move(pairs[2], onward))
    crosses.append(move(after(pairs[1], pairs[2]), second))
    crosses.append(move(pairs[2], second))

    def spread(k, *done):
        return [pairs[k], crosses[k], move(pairs[k], sibling), move(after(crosses[k], *done), sibling)]

    def gate_up(k, shards_of, *earlier):
        mine = pick_call(k, where, code, shards_of, gate_up_weight[0], earlier, capacity)
        return mine, move(mine, over_x)

    def down(k, hidden, *earlier):
        return sum_call(k, where, code, *hidden, down_weight[0], earlier, capacity)

    def give(part, *done):
        return part[0], move(after(part[1], *done), sibling)

    def away(part):
        keep, got = part
        return (keep[1].astype(jnp.float32) + got[1].astype(jnp.float32)).astype(jnp.bfloat16)

    def total(part, back, *hop):
        terms = [v.astype(jnp.float32) for v in (part[0][0], part[1][0], back, *hop)]
        return functools.reduce(jnp.add, terms).astype(jnp.bfloat16)

    hidden0 = gate_up(0, spread(0))
    crosses.append(move(after(pairs[3], hidden0[1]), second))
    hidden1 = gate_up(1, spread(1, hidden0[0]), hidden0[0], pairs[3])
    hidden2 = gate_up(2, spread(2, hidden0[0]), hidden1[0])
    shards3 = spread(3, hidden1[0])
    part1 = down(1, hidden1, hidden2[0], *shards3[2:])
    part2 = down(2, hidden2, part1[0])
    part1 = give(part1, part2[0])
    part2 = give(part2)
    back1 = move(away(part1), over_y)
    hidden3 = gate_up(3, shards3, part2[0])
    part0 = give(down(0, hidden0, hidden3[0], back1))
    back2 = move(after(away(part2), back1, hidden3[0]), over_y)
    from_next = move(total(part1, after(back1, hidden3[0])), backward)
    part3 = give(down(3, hidden3, part0[0], back2, from_next))
    from_far = move(total(part2, back2), onward)
    back3 = move(away(part3), over_y)
    from_last = move(total(part3, back3, from_far), onward)
    back0 = move(after(away(part0), back3), over_y)
    return total(part0, back0, from_next, from_last)


def solution(mesh):
    in_specs = (
        P("expert", "section"),
        P("expert", None),
        P("expert", None),
        P("expert", None, "section"),
        P("expert", None, "section"),
    )
    out_specs = P("expert", "section")
    fits = mesh.shape["section"] == 2 and mesh.shape["expert"] == 16
    return jax.shard_map(pair_shards if fits else shards, mesh=mesh, in_specs=in_specs, out_specs=out_specs, check_vma=False)
```

```python
import functools

import jax
import jax.numpy as jnp
import numpy as np
from jax import lax
from jax.experimental import pallas as pl
from jax.experimental.pallas import tpu as pltpu
from jax.sharding import PartitionSpec as P

UNITS = 64
SCALE = 1.0 / 256.0
VMEM = 40 * 1024 * 1024


def group_of(capacity):
    count = 2
    while (count * capacity) % 16:
        count *= 2
    return count


def slot_map(code, group, capacity):
    line = jnp.concatenate(
        [code[i : i + 1] + jnp.where(code[i : i + 1] >= 0, i * capacity * 256, 0) for i in range(group)], axis=1
    )
    slot, weight = line >> 8, line & 255
    places = lax.broadcasted_iota(jnp.int32, (group * capacity, line.shape[1]), 0)
    return places == slot, weight


def up_kernel(group, capacity, code_ref, tokens_ref, weight_ref, hidden_ref, rows_ref):
    groups = tokens_ref.shape[0] // group
    sections, rows, width = tokens_ref.shape[1:]
    size = group * capacity
    for g in range(groups):
        onehot, _ = slot_map(code_ref[0, g * group : (g + 1) * group], group, capacity)
        onehot = onehot.astype(jnp.bfloat16)
        for s in range(sections):
            block = jnp.concatenate([tokens_ref[g * group + i, s] for i in range(group)], axis=0)
            picked = jnp.dot(onehot, block, preferred_element_type=jnp.float32)
            rows_ref[g * size : (g + 1) * size, s * width : (s + 1) * width] = picked.astype(jnp.bfloat16)
    columns = weight_ref.shape[1]
    pair = 4 * UNITS

    def products(first, count):
        return jnp.dot(rows_ref[...], weight_ref[:, pl.ds(first, count)], preferred_element_type=jnp.float32)

    def mix(gate, up):
        return (gate / (1.0 + jnp.exp(-gate)) * up).astype(jnp.bfloat16)

    @pl.loop(0, columns // pair)
    def _(p):
        both = products(pl.multiple_of(p * pair, pair), pair)
        one, two = both[:, : 2 * UNITS], both[:, 2 * UNITS :]
        low = lax.broadcasted_iota(jnp.int32, one.shape, 1) < UNITS
        gate = jnp.where(low, one, pltpu.roll(two, UNITS, 1))
        up = jnp.where(low, pltpu.roll(one, UNITS, 1), two)
        hidden_ref[:, pl.ds(pl.multiple_of(p * 2 * UNITS, 2 * UNITS), 2 * UNITS)] = mix(gate, up)

    if columns % pair:
        start = columns // pair * pair
        both = products(start, 2 * UNITS)
        hidden_ref[:, start // 2 :] = mix(both, pltpu.roll(both, UNITS, 1))[:, :UNITS]


def down_kernel(group, capacity, code_ref, hidden_ref, weight_ref, out_ref, result_ref):
    sections, _, units = hidden_ref.shape
    groups = code_ref.shape[1] // group
    size = group * capacity
    wide = weight_ref.shape[1]
    step = min(512, wide)

    @pl.loop(0, wide // step)
    def _(p):
        at = pl.ds(pl.multiple_of(p * step, step), step)
        total = jnp.dot(hidden_ref[0], weight_ref[0:units, at], preferred_element_type=jnp.float32)
        for s in range(1, sections):
            total += jnp.dot(
                hidden_ref[s], weight_ref[s * units : (s + 1) * units, at], preferred_element_type=jnp.float32
            )
        result_ref[...] = total.astype(jnp.bfloat16)
        for g in range(groups):
            onehot, weight = slot_map(code_ref[0, g * group : (g + 1) * group], group, capacity)
            scaled = jnp.where(onehot, weight.astype(jnp.float32) * SCALE, 0.0).astype(jnp.bfloat16)
            mixed = lax.dot_general(
                scaled,
                result_ref[g * size : (g + 1) * size],
                (((0,), (0,)), ((), ())),
                preferred_element_type=jnp.float32,
            )
            tall = scaled.shape[1]
            out_ref[g * tall : (g + 1) * tall, at] = mixed.astype(jnp.bfloat16)


def up_call(code, tokens, weight, capacity):
    blocks, sections, rows, width = tokens.shape
    group = group_of(capacity)
    take = min(blocks, 2 * group)
    depth, columns = weight.shape
    tall = take * capacity
    flops = 2 * blocks * capacity * depth * (columns + group * rows)
    return pl.pallas_call(
        functools.partial(up_kernel, group, capacity),
        grid=(blocks // take,),
        in_specs=[
            pl.BlockSpec((1, take, rows), lambda i: (i, 0, 0)),
            pl.BlockSpec((take, sections, rows, width), lambda i: (i, 0, 0, 0)),
            pl.BlockSpec((depth, columns), lambda i: (0, 0), pipeline_mode=pl.Buffered(1)),
        ],
        out_specs=pl.BlockSpec((tall, columns // 2), lambda i: (i, 0)),
        out_shape=jax.ShapeDtypeStruct((blocks * capacity, columns // 2), jnp.bfloat16),
        scratch_shapes=[pltpu.VMEM((tall, depth), jnp.bfloat16)],
        compiler_params=pltpu.CompilerParams(vmem_limit_bytes=48 * 1024 * 1024),
        cost_estimate=pl.CostEstimate(
            flops=flops, bytes_accessed=2 * (tokens.size + weight.size), transcendentals=blocks * capacity * columns // 2
        ),
        name="gate_up",
    )(code.reshape(blocks // take, take, rows), tokens, weight)


def down_call(code, hidden, weight, capacity):
    blocks, rows = code.shape
    sections, _, units = hidden.shape
    group = group_of(capacity)
    take = min(blocks, 2 * group)
    depth, wide = weight.shape
    tall = take * capacity
    return pl.pallas_call(
        functools.partial(down_kernel, group, capacity),
        grid=(blocks // take,),
        in_specs=[
            pl.BlockSpec((1, take, rows), lambda i: (i, 0, 0)),
            pl.BlockSpec((sections, tall, units), lambda i: (0, i, 0)),
            pl.BlockSpec((depth, wide), lambda i: (0, 0), pipeline_mode=pl.Buffered(1)),
        ],
        out_specs=pl.BlockSpec((take * rows, wide), lambda i: (i, 0)),
        out_shape=jax.ShapeDtypeStruct((blocks * rows, wide), jnp.bfloat16),
        scratch_shapes=[pltpu.VMEM((tall, min(512, wide)), jnp.bfloat16)],
        compiler_params=pltpu.CompilerParams(vmem_limit_bytes=48 * 1024 * 1024),
        cost_estimate=pl.CostEstimate(
            flops=2 * blocks * capacity * wide * (depth + group * rows),
            bytes_accessed=2 * (hidden.size + weight.size + blocks * rows * wide),
            transcendentals=0,
        ),
        name="down",
    )(code.reshape(blocks // take, take, rows), hidden, weight)


def block_codes(k, own, where_ref, code_ref):
    return jnp.concatenate([code_ref[pl.ds(where_ref[k, 2 * own + i], 1), :] for i in range(2)], axis=0)


def pick_kernel(capacity, k, where_ref, code_ref, *refs):
    pairs, weight_hbm = refs[:4], refs[4]
    hidden_ref, pair_ref, weight_ref, rows_ref, sems = refs[-5:]
    rows, width = pairs[0].shape[1:]
    span = 8 * UNITS
    spans = weight_hbm.shape[1] // span
    x, c = where_ref[k, 4], where_ref[k, 5]

    def weight_copy(j):
        at = pl.ds(pl.multiple_of(j * span, span), span)
        return pltpu.make_async_copy(weight_hbm.at[:, at], weight_ref.at[:, at], sems.at[4 + j])

    copies = [pltpu.make_async_copy(v, pair_ref.at[pl.ds(2 * i, 2)], sems.at[i]) for i, v in enumerate(pairs)]
    for copy in copies:
        copy.start()
    for j in range(spans):
        weight_copy(j).start()
    for own in range(2):
        core = c ^ own
        onehot, _ = slot_map(block_codes(k, own, where_ref, code_ref), 2, capacity)
        onehot = onehot.astype(jnp.bfloat16)
        copies[2 * own].wait()
        copies[2 * own + 1].wait()
        for section, near, far in ((x, 0, 2 - core), (1 - x, 1 + core, 3)):
            block = jnp.concatenate([pair_ref[4 * own + near], pair_ref[4 * own + far]], axis=0)
            picked = jnp.dot(onehot, block, preferred_element_type=jnp.float32)
            at = pl.ds(pl.multiple_of(section * width, width), width)
            rows_ref[2 * own * capacity : 2 * (own + 1) * capacity, at] = picked.astype(jnp.bfloat16)

    @pl.loop(0, spans)
    def _(j):
        weight_copy(j).wait()
        at = pl.ds(pl.multiple_of(j * span, span), span)
        both = jnp.dot(rows_ref[...], weight_ref[:, at], preferred_element_type=jnp.float32)
        for p in range(2):
            one, two = both[:, 4 * p * UNITS : (4 * p + 2) * UNITS], both[:, (4 * p + 2) * UNITS : 4 * (p + 1) * UNITS]
            low = lax.broadcasted_iota(jnp.int32, one.shape, 1) < UNITS
            gate = jnp.where(low, one, pltpu.roll(two, UNITS, 1))
            up = jnp.where(low, pltpu.roll(one, UNITS, 1), two)
            half = pl.ds(pl.multiple_of((2 * j + p) * 2 * UNITS, 2 * UNITS), 2 * UNITS)
            hidden_ref[:, half] = (gate / (1.0 + jnp.exp(-gate)) * up).astype(jnp.bfloat16)


def sum_kernel(capacity, k, where_ref, code_ref, *refs):
    mine_hbm, other_hbm, weight_hbm = refs[:3]
    keep_hbm, send_hbm, hidden_ref, weight_ref, out_ref, sems = refs[-6:]
    rows = code_ref.shape[1]
    units = mine_hbm.shape[1]
    span = 512
    spans = weight_hbm.shape[1] // span

    def weight_copy(j):
        at = pl.ds(pl.multiple_of(j * span, span), span)
        return pltpu.make_async_copy(weight_hbm.at[:, at], weight_ref.at[:, at], sems.at[2 + j])

    def out_copy(j, i, to):
        at = pl.ds(pl.multiple_of(j * span, span), span)
        sem = sems.at[2 + spans + 2 * j + i]
        return pltpu.make_async_copy(out_ref.at[pl.ds(2 * i, 2), :, at], to.at[:, :, at], sem)

    copies = [pltpu.make_async_copy(v, hidden_ref.at[i], sems.at[i]) for i, v in enumerate((mine_hbm, other_hbm))]
    for copy in copies:
        copy.start()
    for j in range(spans):
        weight_copy(j).start()
    scaled = []
    for own in range(2):
        onehot, weight = slot_map(block_codes(k, own, where_ref, code_ref), 2, capacity)
        scaled.append(jnp.where(onehot, weight.astype(jnp.float32) * SCALE, 0.0).astype(jnp.bfloat16))
    me = where_ref[k, 4]
    mine_at = pl.ds(pl.multiple_of(me * units, units), units)
    other_at = pl.ds(pl.multiple_of((1 - me) * units, units), units)
    for copy in copies:
        copy.wait()

    @pl.loop(0, spans)
    def _(j):
        weight_copy(j).wait()
        at = pl.ds(pl.multiple_of(j * span, span), span)
        total = jnp.dot(hidden_ref[0], weight_ref[mine_at, at], preferred_element_type=jnp.float32)
        total += jnp.dot(hidden_ref[1], weight_ref[other_at, at], preferred_element_type=jnp.float32)
        result = total.astype(jnp.bfloat16)
        for own in range(2):
            mixed = lax.dot_general(
                scaled[own],
                result[2 * own * capacity : 2 * (own + 1) * capacity],
                (((0,), (0,)), ((), ())),
                preferred_element_type=jnp.float32,
            )
            out_ref[2 * own : 2 * own + 2, :, at] = mixed.astype(jnp.bfloat16).reshape(2, rows, span)
        out_copy(j, 0, keep_hbm).start()
        out_copy(j, 1, send_hbm).start()

    for j in range(spans):
        out_copy(j, 0, keep_hbm).wait()
        out_copy(j, 1, send_hbm).wait()


def pick_call(k, where, code, pairs, weight, earlier, capacity):
    _, rows, width = pairs[0].shape
    depth, columns = weight.shape
    tall = 4 * capacity
    anywhere = pl.BlockSpec(memory_space=pl.ANY)
    return pl.pallas_call(
        functools.partial(pick_kernel, capacity, k),
        in_specs=[
            pl.BlockSpec(memory_space=pltpu.SMEM),
            pl.BlockSpec(memory_space=pltpu.VMEM),
            *[anywhere] * (5 + len(earlier)),
        ],
        out_specs=pl.BlockSpec(memory_space=pltpu.VMEM),
        out_shape=jax.ShapeDtypeStruct((tall, columns // 2), jnp.bfloat16),
        scratch_shapes=[
            pltpu.VMEM((8, rows, width), jnp.bfloat16),
            pltpu.VMEM((depth, columns), jnp.bfloat16),
            pltpu.VMEM((tall, depth), jnp.bfloat16),
            pltpu.SemaphoreType.DMA((4 + columns // (8 * UNITS),)),
        ],
        compiler_params=pltpu.CompilerParams(vmem_limit_bytes=VMEM),
        cost_estimate=pl.CostEstimate(
            flops=2 * tall * depth * (columns + rows),
            bytes_accessed=2 * (8 * rows * width + weight.size + tall * columns // 2),
            transcendentals=tall * columns // 2,
        ),
        name="gate_up",
    )(where, code, *pairs, weight, *earlier)


def sum_call(k, where, code, mine, other, weight, earlier, capacity):
    rows = code.shape[1]
    depth, wide = weight.shape
    tall, units = mine.shape
    anywhere = pl.BlockSpec(memory_space=pl.ANY)
    return pl.pallas_call(
        functools.partial(sum_kernel, capacity, k),
        in_specs=[
            pl.BlockSpec(memory_space=pltpu.SMEM),
            pl.BlockSpec(memory_space=pltpu.VMEM),
            *[anywhere] * (3 + len(earlier)),
        ],
        out_specs=[anywhere] * 2,
        out_shape=[jax.ShapeDtypeStruct((2, rows, wide), jnp.bfloat16)] * 2,
        scratch_shapes=[
            pltpu.VMEM((2, tall, units), jnp.bfloat16),
            pltpu.VMEM((depth, wide), jnp.bfloat16),
            pltpu.VMEM((4, rows, wide), jnp.bfloat16),
            pltpu.SemaphoreType.DMA((2 + 3 * (wide // 512),)),
        ],
        compiler_params=pltpu.CompilerParams(vmem_limit_bytes=VMEM),
        cost_estimate=pl.CostEstimate(
            flops=2 * wide * (tall * depth + 4 * rows * capacity),
            bytes_accessed=2 * (2 * mine.size + weight.size + 4 * rows * wide),
            transcendentals=0,
        ),
        name="down",
    )(where, code, mine, other, weight, *earlier)


def codes_of(expert_ids, numerators, experts):
    rows = expert_ids.shape[0]
    named = expert_ids.T[None] == jnp.arange(experts, dtype=jnp.int32)[:, None, None]
    hits = jnp.any(named, axis=1)
    weight = jnp.sum(jnp.where(named, numerators.T[None], 0), axis=1)
    earlier = jnp.arange(rows)[:, None] < jnp.arange(rows)[None, :]
    rank = jnp.dot(hits.astype(jnp.bfloat16), earlier.astype(jnp.bfloat16), preferred_element_type=jnp.float32)
    return jnp.where(hits, rank.astype(jnp.int32) * 256 + weight, -1)


def shards(tokens, expert_ids, numerators, gate_up_weight, down_weight):
    rows, width = tokens.shape
    experts = lax.axis_size("expert")
    capacity = rows * expert_ids.shape[1] * 5 // (4 * experts)
    chips = experts // 2
    across = [[2 * i + c for i in range(chips)] for c in range(2)]
    pairs = [[2 * i, 2 * i + 1] for i in range(chips)]

    codes = lax.all_gather(codes_of(expert_ids, numerators, experts), "expert", axis=0)
    code = lax.dynamic_index_in_dim(codes, lax.axis_index("expert"), 1, keepdims=False)
    code = code.reshape(chips, 2, rows).swapaxes(0, 1).reshape(experts, rows)

    wide = lax.all_gather(tokens, "section", axis=0)
    half = lax.all_gather(wide, "expert", axis=0, axis_index_groups=across)
    whole = lax.all_gather(half, "expert", axis=0, axis_index_groups=pairs)
    whole = whole.reshape((experts,) + wide.shape)

    hidden = up_call(code, whole, gate_up_weight[0], capacity)
    hidden = lax.all_gather(hidden, "section", axis=0)
    part = down_call(code, hidden, down_weight[0], capacity)

    part = part.reshape(2, chips * rows, width)
    part = lax.psum_scatter(part, "expert", scatter_dimension=0, axis_index_groups=pairs, tiled=False)
    return lax.psum_scatter(part, "expert", scatter_dimension=0, axis_index_groups=across, tiled=True)


def pair_shards(tokens, expert_ids, numerators, gate_up_weight, down_weight):
    rows, width = tokens.shape
    experts = lax.axis_size("expert")
    layers = experts // 4
    capacity = rows * expert_ids.shape[1] * 5 // (4 * experts)
    axes = ("section", "expert")
    ring = [0, *range(1, layers, 2), *reversed(range(2, layers, 2))]
    following = {z: ring[(p + 1) % layers] for p, z in enumerate(ring)}

    def perm(place):
        moves = []
        for x in range(2):
            for z in range(layers):
                for y in range(2):
                    for c in range(2):
                        tx, tz, ty, tc = place(x, z, y, c)
                        moves.append(((x * layers + z) * 4 + y * 2 + c, (tx * layers + tz) * 4 + ty * 2 + tc))
        return moves

    onward = perm(lambda x, z, y, c: (x, following[z], y, c))
    backward = [(to, source) for source, to in onward]
    first = perm(lambda x, z, y, c: (x ^ (1 - c), z, y ^ c, c))
    second = perm(lambda x, z, y, c: (x ^ c, z, y ^ (1 - c), c))
    sibling = perm(lambda x, z, y, c: (x, z, y, 1 - c))
    over_x = perm(lambda x, z, y, c: (1 - x, z, y, c))
    over_y = perm(lambda x, z, y, c: (x, z, 1 - y, c))

    def move(value, moves):
        return lax.ppermute(value, axes, moves)

    table = np.zeros((2, layers, 2, 2, layers, 6), np.int32)
    for x, z, y, c, k in np.ndindex(2, layers, 2, 2, layers):
        at = ring[(ring.index(z) - k) % layers] * 4
        table[x, z, y, c, k] = [at + (y ^ (i & 1)) * 2 + (c ^ (i >> 1)) for i in range(4)] + [x, c]
    device = lax.axis_index("section") * experts + lax.axis_index("expert")
    where = lax.dynamic_index_in_dim(jnp.asarray(table.reshape(2 * experts, layers, 6)), device, 0, keepdims=False)
    def after(value, *done):
        return lax.optimization_barrier((value, *done))[0]

    near = move(tokens, first)
    later = move(tokens, onward)
    near_later = move(later, first)
    last = move(later, onward)
    named = codes_of(after(expert_ids, later), numerators, experts)
    code = lax.all_to_all(named, "expert", split_axis=0, concat_axis=0, tiled=True)
    pairs = [jnp.stack([tokens, near]), jnp.stack([later, near_later])]
    crosses = [move(pairs[0], second)]
    near_last = move(after(last, near_later, crosses[0], code), first)
    pairs.append(jnp.stack([last, near_last]))
    pairs.append(move(pairs[2], onward))
    crosses.append(move(after(pairs[1], pairs[2]), second))

    def spread(k, *done):
        return [pairs[k], crosses[k], move(pairs[k], sibling), move(after(crosses[k], *done), sibling)]

    def gate_up(k, shards_of, *earlier):
        return pick_call(k, where, code, shards_of, gate_up_weight[0], earlier, capacity)

    def swap(mine, *done):
        return mine, move(after(mine, *done), over_x)

    def down(k, hidden, *earlier):
        return sum_call(k, where, code, *hidden, down_weight[0], earlier, capacity)

    def give(part, *done):
        return part[0], move(after(part[1], *done), sibling)

    def away(part):
        keep, got = part
        return (keep[1].astype(jnp.float32) + got[1].astype(jnp.float32)).astype(jnp.bfloat16)

    def total(part, back, *hop):
        terms = [v.astype(jnp.float32) for v in (part[0][0], part[1][0], back, *hop)]
        return functools.reduce(jnp.add, terms).astype(jnp.bfloat16)

    hidden0 = swap(gate_up(0, spread(0)))
    crosses.append(move(after(pairs[2], hidden0[0]), second))
    hidden1 = swap(gate_up(1, spread(1, hidden0[0]), *hidden0))
    pairs[3] = after(pairs[3], hidden1[0])
    crosses.append(move(pairs[3], second))
    hidden2 = swap(gate_up(2, spread(2, hidden1[0]), hidden1[0], pairs[3]))
    part0 = give(down(0, hidden0, hidden2[0]))
    part1 = down(1, hidden1, part0[0], crosses[3])
    shards3 = spread(3, part1[0])
    part1 = give(part1)
    back1 = move(away(part1), over_y)
    hidden3 = swap(gate_up(3, shards3, part1[0]))
    part2 = give(down(2, hidden2, hidden3[0], back1), hidden3[1])
    from_next = move(total(part1, after(back1, hidden3[0])), backward)
    back2 = move(away(part2), over_y)
    part3 = give(down(3, hidden3, part2[0]), from_next, back2)
    from_far = move(total(part2, back2), onward)
    back3 = move(away(part3), over_y)
    from_last = move(total(part3, back3, from_far), onward)
    back0 = move(after(away(part0), back3), over_y)
    return total(part0, back0, from_next, from_last)


def solution(mesh):
    in_specs = (
        P("expert", "section"),
        P("expert", None),
        P("expert", None),
        P("expert", None, "section"),
        P("expert", None, "section"),
    )
    out_specs = P("expert", "section")
    fits = mesh.shape["section"] == 2 and mesh.shape["expert"] == 16
    return jax.shard_map(pair_shards if fits else shards, mesh=mesh, in_specs=in_specs, out_specs=out_specs, check_vma=False)
```

```python
import functools

import jax
import jax.numpy as jnp
import numpy as np
from jax import lax
from jax.experimental import pallas as pl
from jax.experimental.pallas import tpu as pltpu
from jax.sharding import PartitionSpec as P

UNITS = 64
SCALE = 1.0 / 256.0
VMEM = 40 * 1024 * 1024


def group_of(capacity):
    count = 2
    while (count * capacity) % 16:
        count *= 2
    return count


def slot_map(code, group, capacity):
    line = jnp.concatenate(
        [code[i : i + 1] + jnp.where(code[i : i + 1] >= 0, i * capacity * 256, 0) for i in range(group)], axis=1
    )
    slot, weight = line >> 8, line & 255
    places = lax.broadcasted_iota(jnp.int32, (group * capacity, line.shape[1]), 0)
    return places == slot, weight


def up_kernel(group, capacity, code_ref, tokens_ref, weight_ref, hidden_ref, rows_ref):
    groups = tokens_ref.shape[0] // group
    sections, rows, width = tokens_ref.shape[1:]
    size = group * capacity
    for g in range(groups):
        onehot, _ = slot_map(code_ref[0, g * group : (g + 1) * group], group, capacity)
        onehot = onehot.astype(jnp.bfloat16)
        for s in range(sections):
            block = jnp.concatenate([tokens_ref[g * group + i, s] for i in range(group)], axis=0)
            picked = jnp.dot(onehot, block, preferred_element_type=jnp.float32)
            rows_ref[g * size : (g + 1) * size, s * width : (s + 1) * width] = picked.astype(jnp.bfloat16)
    columns = weight_ref.shape[1]
    pair = 4 * UNITS

    def products(first, count):
        return jnp.dot(rows_ref[...], weight_ref[:, pl.ds(first, count)], preferred_element_type=jnp.float32)

    def mix(gate, up):
        return (gate / (1.0 + jnp.exp(-gate)) * up).astype(jnp.bfloat16)

    @pl.loop(0, columns // pair)
    def _(p):
        both = products(pl.multiple_of(p * pair, pair), pair)
        one, two = both[:, : 2 * UNITS], both[:, 2 * UNITS :]
        low = lax.broadcasted_iota(jnp.int32, one.shape, 1) < UNITS
        gate = jnp.where(low, one, pltpu.roll(two, UNITS, 1))
        up = jnp.where(low, pltpu.roll(one, UNITS, 1), two)
        hidden_ref[:, pl.ds(pl.multiple_of(p * 2 * UNITS, 2 * UNITS), 2 * UNITS)] = mix(gate, up)

    if columns % pair:
        start = columns // pair * pair
        both = products(start, 2 * UNITS)
        hidden_ref[:, start // 2 :] = mix(both, pltpu.roll(both, UNITS, 1))[:, :UNITS]


def down_kernel(group, capacity, code_ref, hidden_ref, weight_ref, out_ref, result_ref):
    sections, _, units = hidden_ref.shape
    groups = code_ref.shape[1] // group
    size = group * capacity
    wide = weight_ref.shape[1]
    step = min(512, wide)

    @pl.loop(0, wide // step)
    def _(p):
        at = pl.ds(pl.multiple_of(p * step, step), step)
        total = jnp.dot(hidden_ref[0], weight_ref[0:units, at], preferred_element_type=jnp.float32)
        for s in range(1, sections):
            total += jnp.dot(
                hidden_ref[s], weight_ref[s * units : (s + 1) * units, at], preferred_element_type=jnp.float32
            )
        result_ref[...] = total.astype(jnp.bfloat16)
        for g in range(groups):
            onehot, weight = slot_map(code_ref[0, g * group : (g + 1) * group], group, capacity)
            scaled = jnp.where(onehot, weight.astype(jnp.float32) * SCALE, 0.0).astype(jnp.bfloat16)
            mixed = lax.dot_general(
                scaled,
                result_ref[g * size : (g + 1) * size],
                (((0,), (0,)), ((), ())),
                preferred_element_type=jnp.float32,
            )
            tall = scaled.shape[1]
            out_ref[g * tall : (g + 1) * tall, at] = mixed.astype(jnp.bfloat16)


def up_call(code, tokens, weight, capacity):
    blocks, sections, rows, width = tokens.shape
    group = group_of(capacity)
    take = min(blocks, 2 * group)
    depth, columns = weight.shape
    tall = take * capacity
    flops = 2 * blocks * capacity * depth * (columns + group * rows)
    return pl.pallas_call(
        functools.partial(up_kernel, group, capacity),
        grid=(blocks // take,),
        in_specs=[
            pl.BlockSpec((1, take, rows), lambda i: (i, 0, 0)),
            pl.BlockSpec((take, sections, rows, width), lambda i: (i, 0, 0, 0)),
            pl.BlockSpec((depth, columns), lambda i: (0, 0), pipeline_mode=pl.Buffered(1)),
        ],
        out_specs=pl.BlockSpec((tall, columns // 2), lambda i: (i, 0)),
        out_shape=jax.ShapeDtypeStruct((blocks * capacity, columns // 2), jnp.bfloat16),
        scratch_shapes=[pltpu.VMEM((tall, depth), jnp.bfloat16)],
        compiler_params=pltpu.CompilerParams(vmem_limit_bytes=48 * 1024 * 1024),
        cost_estimate=pl.CostEstimate(
            flops=flops, bytes_accessed=2 * (tokens.size + weight.size), transcendentals=blocks * capacity * columns // 2
        ),
        name="gate_up",
    )(code.reshape(blocks // take, take, rows), tokens, weight)


def down_call(code, hidden, weight, capacity):
    blocks, rows = code.shape
    sections, _, units = hidden.shape
    group = group_of(capacity)
    take = min(blocks, 2 * group)
    depth, wide = weight.shape
    tall = take * capacity
    return pl.pallas_call(
        functools.partial(down_kernel, group, capacity),
        grid=(blocks // take,),
        in_specs=[
            pl.BlockSpec((1, take, rows), lambda i: (i, 0, 0)),
            pl.BlockSpec((sections, tall, units), lambda i: (0, i, 0)),
            pl.BlockSpec((depth, wide), lambda i: (0, 0), pipeline_mode=pl.Buffered(1)),
        ],
        out_specs=pl.BlockSpec((take * rows, wide), lambda i: (i, 0)),
        out_shape=jax.ShapeDtypeStruct((blocks * rows, wide), jnp.bfloat16),
        scratch_shapes=[pltpu.VMEM((tall, min(512, wide)), jnp.bfloat16)],
        compiler_params=pltpu.CompilerParams(vmem_limit_bytes=48 * 1024 * 1024),
        cost_estimate=pl.CostEstimate(
            flops=2 * blocks * capacity * wide * (depth + group * rows),
            bytes_accessed=2 * (hidden.size + weight.size + blocks * rows * wide),
            transcendentals=0,
        ),
        name="down",
    )(code.reshape(blocks // take, take, rows), hidden, weight)


def block_codes(k, own, where_ref, code_ref):
    return jnp.concatenate([code_ref[pl.ds(where_ref[k, 2 * own + i], 1), :] for i in range(2)], axis=0)


def pick_kernel(capacity, k, where_ref, code_ref, *refs):
    pairs, weight_hbm = refs[:4], refs[4]
    hidden_ref, pair_ref, weight_ref, rows_ref, sems = refs[-5:]
    rows, width = pairs[0].shape[1:]
    span = 8 * UNITS
    spans = weight_hbm.shape[1] // span
    x, c = where_ref[k, 4], where_ref[k, 5]

    def weight_copy(j):
        at = pl.ds(pl.multiple_of(j * span, span), span)
        return pltpu.make_async_copy(weight_hbm.at[:, at], weight_ref.at[:, at], sems.at[4 + j])

    copies = [pltpu.make_async_copy(v, pair_ref.at[pl.ds(2 * i, 2)], sems.at[i]) for i, v in enumerate(pairs)]
    for copy in copies:
        copy.start()
    for j in range(spans):
        weight_copy(j).start()
    for own in range(2):
        core = c ^ own
        onehot, _ = slot_map(block_codes(k, own, where_ref, code_ref), 2, capacity)
        onehot = onehot.astype(jnp.bfloat16)
        copies[2 * own].wait()
        copies[2 * own + 1].wait()
        for section, near, far in ((x, 0, 2 - core), (1 - x, 1 + core, 3)):
            block = jnp.concatenate([pair_ref[4 * own + near], pair_ref[4 * own + far]], axis=0)
            picked = jnp.dot(onehot, block, preferred_element_type=jnp.float32)
            at = pl.ds(pl.multiple_of(section * width, width), width)
            rows_ref[2 * own * capacity : 2 * (own + 1) * capacity, at] = picked.astype(jnp.bfloat16)

    @pl.loop(0, spans)
    def _(j):
        weight_copy(j).wait()
        at = pl.ds(pl.multiple_of(j * span, span), span)
        both = jnp.dot(rows_ref[...], weight_ref[:, at], preferred_element_type=jnp.float32)
        for p in range(2):
            one, two = both[:, 4 * p * UNITS : (4 * p + 2) * UNITS], both[:, (4 * p + 2) * UNITS : 4 * (p + 1) * UNITS]
            low = lax.broadcasted_iota(jnp.int32, one.shape, 1) < UNITS
            gate = jnp.where(low, one, pltpu.roll(two, UNITS, 1))
            up = jnp.where(low, pltpu.roll(one, UNITS, 1), two)
            half = pl.ds(pl.multiple_of((2 * j + p) * 2 * UNITS, 2 * UNITS), 2 * UNITS)
            hidden_ref[:, half] = (gate / (1.0 + jnp.exp(-gate)) * up).astype(jnp.bfloat16)


def sum_kernel(capacity, k, where_ref, code_ref, *refs):
    mine_hbm, other_hbm, weight_hbm = refs[:3]
    keep_hbm, send_hbm, hidden_ref, weight_ref, out_ref, sems = refs[-6:]
    rows = code_ref.shape[1]
    units = mine_hbm.shape[1]
    span = 512
    spans = weight_hbm.shape[1] // span

    def weight_copy(j):
        at = pl.ds(pl.multiple_of(j * span, span), span)
        return pltpu.make_async_copy(weight_hbm.at[:, at], weight_ref.at[:, at], sems.at[2 + j])

    def out_copy(j, i, to):
        at = pl.ds(pl.multiple_of(j * span, span), span)
        sem = sems.at[2 + spans + 2 * j + i]
        return pltpu.make_async_copy(out_ref.at[pl.ds(2 * i, 2), :, at], to.at[:, :, at], sem)

    copies = [pltpu.make_async_copy(v, hidden_ref.at[i], sems.at[i]) for i, v in enumerate((mine_hbm, other_hbm))]
    for copy in copies:
        copy.start()
    for j in range(spans):
        weight_copy(j).start()
    scaled = []
    for own in range(2):
        onehot, weight = slot_map(block_codes(k, own, where_ref, code_ref), 2, capacity)
        scaled.append(jnp.where(onehot, weight.astype(jnp.float32) * SCALE, 0.0).astype(jnp.bfloat16))
    me = where_ref[k, 4]
    mine_at = pl.ds(pl.multiple_of(me * units, units), units)
    other_at = pl.ds(pl.multiple_of((1 - me) * units, units), units)
    for copy in copies:
        copy.wait()

    @pl.loop(0, spans)
    def _(j):
        weight_copy(j).wait()
        at = pl.ds(pl.multiple_of(j * span, span), span)
        total = jnp.dot(hidden_ref[0], weight_ref[mine_at, at], preferred_element_type=jnp.float32)
        total += jnp.dot(hidden_ref[1], weight_ref[other_at, at], preferred_element_type=jnp.float32)
        result = total.astype(jnp.bfloat16)
        for own in range(2):
            mixed = lax.dot_general(
                scaled[own],
                result[2 * own * capacity : 2 * (own + 1) * capacity],
                (((0,), (0,)), ((), ())),
                preferred_element_type=jnp.float32,
            )
            out_ref[2 * own : 2 * own + 2, :, at] = mixed.astype(jnp.bfloat16).reshape(2, rows, span)
        out_copy(j, 0, keep_hbm).start()
        out_copy(j, 1, send_hbm).start()

    for j in range(spans):
        out_copy(j, 0, keep_hbm).wait()
        out_copy(j, 1, send_hbm).wait()


def pick_call(k, where, code, pairs, weight, earlier, capacity):
    _, rows, width = pairs[0].shape
    depth, columns = weight.shape
    tall = 4 * capacity
    anywhere = pl.BlockSpec(memory_space=pl.ANY)
    return pl.pallas_call(
        functools.partial(pick_kernel, capacity, k),
        in_specs=[
            pl.BlockSpec(memory_space=pltpu.SMEM),
            pl.BlockSpec(memory_space=pltpu.VMEM),
            *[anywhere] * (5 + len(earlier)),
        ],
        out_specs=pl.BlockSpec(memory_space=pltpu.VMEM),
        out_shape=jax.ShapeDtypeStruct((tall, columns // 2), jnp.bfloat16),
        scratch_shapes=[
            pltpu.VMEM((8, rows, width), jnp.bfloat16),
            pltpu.VMEM((depth, columns), jnp.bfloat16),
            pltpu.VMEM((tall, depth), jnp.bfloat16),
            pltpu.SemaphoreType.DMA((4 + columns // (8 * UNITS),)),
        ],
        compiler_params=pltpu.CompilerParams(vmem_limit_bytes=VMEM),
        cost_estimate=pl.CostEstimate(
            flops=2 * tall * depth * (columns + rows),
            bytes_accessed=2 * (8 * rows * width + weight.size + tall * columns // 2),
            transcendentals=tall * columns // 2,
        ),
        name="gate_up",
    )(where, code, *pairs, weight, *earlier)


def sum_call(k, where, code, mine, other, weight, earlier, capacity):
    rows = code.shape[1]
    depth, wide = weight.shape
    tall, units = mine.shape
    anywhere = pl.BlockSpec(memory_space=pl.ANY)
    return pl.pallas_call(
        functools.partial(sum_kernel, capacity, k),
        in_specs=[
            pl.BlockSpec(memory_space=pltpu.SMEM),
            pl.BlockSpec(memory_space=pltpu.VMEM),
            *[anywhere] * (3 + len(earlier)),
        ],
        out_specs=[anywhere] * 2,
        out_shape=[jax.ShapeDtypeStruct((2, rows, wide), jnp.bfloat16)] * 2,
        scratch_shapes=[
            pltpu.VMEM((2, tall, units), jnp.bfloat16),
            pltpu.VMEM((depth, wide), jnp.bfloat16),
            pltpu.VMEM((4, rows, wide), jnp.bfloat16),
            pltpu.SemaphoreType.DMA((2 + 3 * (wide // 512),)),
        ],
        compiler_params=pltpu.CompilerParams(vmem_limit_bytes=VMEM),
        cost_estimate=pl.CostEstimate(
            flops=2 * wide * (tall * depth + 4 * rows * capacity),
            bytes_accessed=2 * (2 * mine.size + weight.size + 4 * rows * wide),
            transcendentals=0,
        ),
        name="down",
    )(where, code, mine, other, weight, *earlier)


def codes_of(expert_ids, numerators, experts):
    rows = expert_ids.shape[0]
    named = expert_ids.T[None] == jnp.arange(experts, dtype=jnp.int32)[:, None, None]
    hits = jnp.any(named, axis=1)
    weight = jnp.sum(jnp.where(named, numerators.T[None], 0), axis=1)
    earlier = jnp.arange(rows)[:, None] < jnp.arange(rows)[None, :]
    rank = jnp.dot(hits.astype(jnp.bfloat16), earlier.astype(jnp.bfloat16), preferred_element_type=jnp.float32)
    return jnp.where(hits, rank.astype(jnp.int32) * 256 + weight, -1)


def shards(tokens, expert_ids, numerators, gate_up_weight, down_weight):
    rows, width = tokens.shape
    experts = lax.axis_size("expert")
    capacity = rows * expert_ids.shape[1] * 5 // (4 * experts)
    chips = experts // 2
    across = [[2 * i + c for i in range(chips)] for c in range(2)]
    pairs = [[2 * i, 2 * i + 1] for i in range(chips)]

    codes = lax.all_gather(codes_of(expert_ids, numerators, experts), "expert", axis=0)
    code = lax.dynamic_index_in_dim(codes, lax.axis_index("expert"), 1, keepdims=False)
    code = code.reshape(chips, 2, rows).swapaxes(0, 1).reshape(experts, rows)

    wide = lax.all_gather(tokens, "section", axis=0)
    half = lax.all_gather(wide, "expert", axis=0, axis_index_groups=across)
    whole = lax.all_gather(half, "expert", axis=0, axis_index_groups=pairs)
    whole = whole.reshape((experts,) + wide.shape)

    hidden = up_call(code, whole, gate_up_weight[0], capacity)
    hidden = lax.all_gather(hidden, "section", axis=0)
    part = down_call(code, hidden, down_weight[0], capacity)

    part = part.reshape(2, chips * rows, width)
    part = lax.psum_scatter(part, "expert", scatter_dimension=0, axis_index_groups=pairs, tiled=False)
    return lax.psum_scatter(part, "expert", scatter_dimension=0, axis_index_groups=across, tiled=True)


def pair_shards(tokens, expert_ids, numerators, gate_up_weight, down_weight):
    rows, width = tokens.shape
    experts = lax.axis_size("expert")
    layers = experts // 4
    capacity = rows * expert_ids.shape[1] * 5 // (4 * experts)
    axes = ("section", "expert")
    ring = [0, *range(1, layers, 2), *reversed(range(2, layers, 2))]
    following = {z: ring[(p + 1) % layers] for p, z in enumerate(ring)}

    def perm(place):
        moves = []
        for x in range(2):
            for z in range(layers):
                for y in range(2):
                    for c in range(2):
                        tx, tz, ty, tc = place(x, z, y, c)
                        moves.append(((x * layers + z) * 4 + y * 2 + c, (tx * layers + tz) * 4 + ty * 2 + tc))
        return moves

    onward = perm(lambda x, z, y, c: (x, following[z], y, c))
    backward = [(to, source) for source, to in onward]
    first = perm(lambda x, z, y, c: (x ^ (1 - c), z, y ^ c, c))
    second = perm(lambda x, z, y, c: (x ^ c, z, y ^ (1 - c), c))
    sibling = perm(lambda x, z, y, c: (x, z, y, 1 - c))
    over_x = perm(lambda x, z, y, c: (1 - x, z, y, c))
    over_y = perm(lambda x, z, y, c: (x, z, 1 - y, c))

    def move(value, moves):
        return lax.ppermute(value, axes, moves)

    table = np.zeros((2, layers, 2, 2, layers, 6), np.int32)
    for x, z, y, c, k in np.ndindex(2, layers, 2, 2, layers):
        at = ring[(ring.index(z) - k) % layers] * 4
        table[x, z, y, c, k] = [at + (y ^ (i & 1)) * 2 + (c ^ (i >> 1)) for i in range(4)] + [x, c]
    device = lax.axis_index("section") * experts + lax.axis_index("expert")
    where = lax.dynamic_index_in_dim(jnp.asarray(table.reshape(2 * experts, layers, 6)), device, 0, keepdims=False)
    def after(value, *done):
        return lax.optimization_barrier((value, *done))[0]

    near = move(tokens, first)
    later = move(tokens, onward)
    near_later = move(later, first)
    last = move(later, onward)
    named = codes_of(after(expert_ids, later), numerators, experts)
    code = lax.all_to_all(named, "expert", split_axis=0, concat_axis=0, tiled=True)
    pairs = [jnp.stack([tokens, near]), jnp.stack([later, near_later])]
    crosses = [move(pairs[0], second)]
    near_last = move(after(last, near_later, crosses[0], code), first)
    pairs.append(jnp.stack([last, near_last]))
    pairs.append(move(pairs[2], onward))
    crosses.append(move(after(pairs[1], pairs[2]), second))

    def spread(k, *done):
        return [pairs[k], crosses[k], move(pairs[k], sibling), move(after(crosses[k], *done), sibling)]

    def gate_up(k, shards_of, *earlier):
        return pick_call(k, where, code, shards_of, gate_up_weight[0], earlier, capacity)

    def swap(mine, *done):
        return mine, move(after(mine, *done), over_x)

    def down(k, hidden, *earlier):
        return sum_call(k, where, code, *hidden, down_weight[0], earlier, capacity)

    def give(part, *done):
        return part[0], move(after(part[1], *done), sibling)

    def away(part):
        keep, got = part
        return (keep[1].astype(jnp.float32) + got[1].astype(jnp.float32)).astype(jnp.bfloat16)

    def total(part, back, *hop):
        terms = [v.astype(jnp.float32) for v in (part[0][0], part[1][0], back, *hop)]
        return functools.reduce(jnp.add, terms).astype(jnp.bfloat16)

    mine0 = gate_up(0, spread(0))
    crosses.append(move(after(pairs[2], mine0), second))
    hidden1 = swap(gate_up(1, spread(1, mine0), mine0))
    pairs[3] = after(pairs[3], hidden1[0])
    crosses.append(move(after(pairs[3], hidden1[1]), second))
    hidden2 = swap(gate_up(2, spread(2, hidden1[0]), hidden1[0], pairs[3]))
    part1 = down(1, hidden1, hidden2[0], crosses[3])
    shards3 = spread(3, part1[0])
    part1 = give(part1)
    back1 = move(away(part1), over_y)
    hidden3 = swap(gate_up(3, shards3, part1[0]))
    part2 = give(down(2, hidden2, hidden3[0], back1), hidden3[1])
    hidden0 = swap(mine0, hidden3[1])
    from_next = move(total(part1, after(back1, hidden3[0])), backward)
    back2 = move(away(part2), over_y)
    part3 = down(3, hidden3, part2[0])
    part0 = give(down(0, hidden0, part3[0]))
    part3 = give(part3, from_next, back2, part0[0])
    from_far = move(total(part2, back2), onward)
    back3 = move(away(part3), over_y)
    from_last = move(total(part3, back3, from_far), onward)
    back0 = move(after(away(part0), back3), over_y)
    return total(part0, back0, from_next, from_last)


def solution(mesh):
    in_specs = (
        P("expert", "section"),
        P("expert", None),
        P("expert", None),
        P("expert", None, "section"),
        P("expert", None, "section"),
    )
    out_specs = P("expert", "section")
    fits = mesh.shape["section"] == 2 and mesh.shape["expert"] == 16
    return jax.shard_map(pair_shards if fits else shards, mesh=mesh, in_specs=in_specs, out_specs=out_specs, check_vma=False)
```

```python
import functools

import jax
import jax.numpy as jnp
import numpy as np
from jax import lax
from jax.experimental import pallas as pl
from jax.experimental.pallas import tpu as pltpu
from jax.sharding import PartitionSpec as P

UNITS = 64
SCALE = 1.0 / 256.0
VMEM = 40 * 1024 * 1024


def group_of(capacity):
    count = 2
    while (count * capacity) % 16:
        count *= 2
    return count


def slot_map(code, group, capacity):
    line = jnp.concatenate(
        [code[i : i + 1] + jnp.where(code[i : i + 1] >= 0, i * capacity * 256, 0) for i in range(group)], axis=1
    )
    slot, weight = line >> 8, line & 255
    places = lax.broadcasted_iota(jnp.int32, (group * capacity, line.shape[1]), 0)
    return places == slot, weight


def up_kernel(group, capacity, code_ref, tokens_ref, weight_ref, hidden_ref, rows_ref):
    groups = tokens_ref.shape[0] // group
    sections, rows, width = tokens_ref.shape[1:]
    size = group * capacity
    for g in range(groups):
        onehot, _ = slot_map(code_ref[0, g * group : (g + 1) * group], group, capacity)
        onehot = onehot.astype(jnp.bfloat16)
        for s in range(sections):
            block = jnp.concatenate([tokens_ref[g * group + i, s] for i in range(group)], axis=0)
            picked = jnp.dot(onehot, block, preferred_element_type=jnp.float32)
            rows_ref[g * size : (g + 1) * size, s * width : (s + 1) * width] = picked.astype(jnp.bfloat16)
    columns = weight_ref.shape[1]
    pair = 4 * UNITS

    def products(first, count):
        return jnp.dot(rows_ref[...], weight_ref[:, pl.ds(first, count)], preferred_element_type=jnp.float32)

    def mix(gate, up):
        return (gate / (1.0 + jnp.exp(-gate)) * up).astype(jnp.bfloat16)

    @pl.loop(0, columns // pair)
    def _(p):
        both = products(pl.multiple_of(p * pair, pair), pair)
        one, two = both[:, : 2 * UNITS], both[:, 2 * UNITS :]
        low = lax.broadcasted_iota(jnp.int32, one.shape, 1) < UNITS
        gate = jnp.where(low, one, pltpu.roll(two, UNITS, 1))
        up = jnp.where(low, pltpu.roll(one, UNITS, 1), two)
        hidden_ref[:, pl.ds(pl.multiple_of(p * 2 * UNITS, 2 * UNITS), 2 * UNITS)] = mix(gate, up)

    if columns % pair:
        start = columns // pair * pair
        both = products(start, 2 * UNITS)
        hidden_ref[:, start // 2 :] = mix(both, pltpu.roll(both, UNITS, 1))[:, :UNITS]


def down_kernel(group, capacity, code_ref, hidden_ref, weight_ref, out_ref, result_ref):
    sections, _, units = hidden_ref.shape
    groups = code_ref.shape[1] // group
    size = group * capacity
    wide = weight_ref.shape[1]
    step = min(512, wide)

    @pl.loop(0, wide // step)
    def _(p):
        at = pl.ds(pl.multiple_of(p * step, step), step)
        total = jnp.dot(hidden_ref[0], weight_ref[0:units, at], preferred_element_type=jnp.float32)
        for s in range(1, sections):
            total += jnp.dot(
                hidden_ref[s], weight_ref[s * units : (s + 1) * units, at], preferred_element_type=jnp.float32
            )
        result_ref[...] = total.astype(jnp.bfloat16)
        for g in range(groups):
            onehot, weight = slot_map(code_ref[0, g * group : (g + 1) * group], group, capacity)
            scaled = jnp.where(onehot, weight.astype(jnp.float32) * SCALE, 0.0).astype(jnp.bfloat16)
            mixed = lax.dot_general(
                scaled,
                result_ref[g * size : (g + 1) * size],
                (((0,), (0,)), ((), ())),
                preferred_element_type=jnp.float32,
            )
            tall = scaled.shape[1]
            out_ref[g * tall : (g + 1) * tall, at] = mixed.astype(jnp.bfloat16)


def up_call(code, tokens, weight, capacity):
    blocks, sections, rows, width = tokens.shape
    group = group_of(capacity)
    take = min(blocks, 2 * group)
    depth, columns = weight.shape
    tall = take * capacity
    flops = 2 * blocks * capacity * depth * (columns + group * rows)
    return pl.pallas_call(
        functools.partial(up_kernel, group, capacity),
        grid=(blocks // take,),
        in_specs=[
            pl.BlockSpec((1, take, rows), lambda i: (i, 0, 0)),
            pl.BlockSpec((take, sections, rows, width), lambda i: (i, 0, 0, 0)),
            pl.BlockSpec((depth, columns), lambda i: (0, 0), pipeline_mode=pl.Buffered(1)),
        ],
        out_specs=pl.BlockSpec((tall, columns // 2), lambda i: (i, 0)),
        out_shape=jax.ShapeDtypeStruct((blocks * capacity, columns // 2), jnp.bfloat16),
        scratch_shapes=[pltpu.VMEM((tall, depth), jnp.bfloat16)],
        compiler_params=pltpu.CompilerParams(vmem_limit_bytes=48 * 1024 * 1024),
        cost_estimate=pl.CostEstimate(
            flops=flops, bytes_accessed=2 * (tokens.size + weight.size), transcendentals=blocks * capacity * columns // 2
        ),
        name="gate_up",
    )(code.reshape(blocks // take, take, rows), tokens, weight)


def down_call(code, hidden, weight, capacity):
    blocks, rows = code.shape
    sections, _, units = hidden.shape
    group = group_of(capacity)
    take = min(blocks, 2 * group)
    depth, wide = weight.shape
    tall = take * capacity
    return pl.pallas_call(
        functools.partial(down_kernel, group, capacity),
        grid=(blocks // take,),
        in_specs=[
            pl.BlockSpec((1, take, rows), lambda i: (i, 0, 0)),
            pl.BlockSpec((sections, tall, units), lambda i: (0, i, 0)),
            pl.BlockSpec((depth, wide), lambda i: (0, 0), pipeline_mode=pl.Buffered(1)),
        ],
        out_specs=pl.BlockSpec((take * rows, wide), lambda i: (i, 0)),
        out_shape=jax.ShapeDtypeStruct((blocks * rows, wide), jnp.bfloat16),
        scratch_shapes=[pltpu.VMEM((tall, min(512, wide)), jnp.bfloat16)],
        compiler_params=pltpu.CompilerParams(vmem_limit_bytes=48 * 1024 * 1024),
        cost_estimate=pl.CostEstimate(
            flops=2 * blocks * capacity * wide * (depth + group * rows),
            bytes_accessed=2 * (hidden.size + weight.size + blocks * rows * wide),
            transcendentals=0,
        ),
        name="down",
    )(code.reshape(blocks // take, take, rows), hidden, weight)


def block_codes(k, own, where_ref, code_ref):
    return jnp.concatenate([code_ref[pl.ds(where_ref[k, 2 * own + i], 1), :] for i in range(2)], axis=0)


def pick_kernel(capacity, k, where_ref, code_ref, *refs):
    pairs, weight_hbm = refs[:4], refs[4]
    hidden_ref, pair_ref, weight_ref, rows_ref, sems = refs[-5:]
    rows, width = pairs[0].shape[1:]
    span = 8 * UNITS
    spans = weight_hbm.shape[1] // span
    x, c = where_ref[k, 4], where_ref[k, 5]

    def weight_copy(j):
        at = pl.ds(pl.multiple_of(j * span, span), span)
        return pltpu.make_async_copy(weight_hbm.at[:, at], weight_ref.at[:, at], sems.at[4 + j])

    copies = [pltpu.make_async_copy(v, pair_ref.at[pl.ds(2 * i, 2)], sems.at[i]) for i, v in enumerate(pairs)]
    for copy in copies:
        copy.start()
    for j in range(spans):
        weight_copy(j).start()
    for own in range(2):
        core = c ^ own
        onehot, _ = slot_map(block_codes(k, own, where_ref, code_ref), 2, capacity)
        onehot = onehot.astype(jnp.bfloat16)
        copies[2 * own].wait()
        copies[2 * own + 1].wait()
        for section, near, far in ((x, 0, 2 - core), (1 - x, 1 + core, 3)):
            block = jnp.concatenate([pair_ref[4 * own + near], pair_ref[4 * own + far]], axis=0)
            picked = jnp.dot(onehot, block, preferred_element_type=jnp.float32)
            at = pl.ds(pl.multiple_of(section * width, width), width)
            rows_ref[2 * own * capacity : 2 * (own + 1) * capacity, at] = picked.astype(jnp.bfloat16)

    @pl.loop(0, spans)
    def _(j):
        weight_copy(j).wait()
        at = pl.ds(pl.multiple_of(j * span, span), span)
        both = jnp.dot(rows_ref[...], weight_ref[:, at], preferred_element_type=jnp.float32)
        for p in range(2):
            one, two = both[:, 4 * p * UNITS : (4 * p + 2) * UNITS], both[:, (4 * p + 2) * UNITS : 4 * (p + 1) * UNITS]
            low = lax.broadcasted_iota(jnp.int32, one.shape, 1) < UNITS
            gate = jnp.where(low, one, pltpu.roll(two, UNITS, 1))
            up = jnp.where(low, pltpu.roll(one, UNITS, 1), two)
            half = pl.ds(pl.multiple_of((2 * j + p) * 2 * UNITS, 2 * UNITS), 2 * UNITS)
            hidden_ref[:, half] = (gate / (1.0 + jnp.exp(-gate)) * up).astype(jnp.bfloat16)


def sum_kernel(capacity, k, where_ref, code_ref, *refs):
    mine_hbm, other_hbm, weight_hbm = refs[:3]
    keep_hbm, send_hbm, hidden_ref, weight_ref, out_ref, sems = refs[-6:]
    rows = code_ref.shape[1]
    units = mine_hbm.shape[1]
    span = 512
    spans = weight_hbm.shape[1] // span

    def weight_copy(j):
        at = pl.ds(pl.multiple_of(j * span, span), span)
        return pltpu.make_async_copy(weight_hbm.at[:, at], weight_ref.at[:, at], sems.at[2 + j])

    def out_copy(j, i, to):
        at = pl.ds(pl.multiple_of(j * span, span), span)
        sem = sems.at[2 + spans + 2 * j + i]
        return pltpu.make_async_copy(out_ref.at[pl.ds(2 * i, 2), :, at], to.at[:, :, at], sem)

    copies = [pltpu.make_async_copy(v, hidden_ref.at[i], sems.at[i]) for i, v in enumerate((mine_hbm, other_hbm))]
    for copy in copies:
        copy.start()
    for j in range(spans):
        weight_copy(j).start()
    scaled = []
    for own in range(2):
        onehot, weight = slot_map(block_codes(k, own, where_ref, code_ref), 2, capacity)
        scaled.append(jnp.where(onehot, weight.astype(jnp.float32) * SCALE, 0.0).astype(jnp.bfloat16))
    me = where_ref[k, 4]
    mine_at = pl.ds(pl.multiple_of(me * units, units), units)
    other_at = pl.ds(pl.multiple_of((1 - me) * units, units), units)
    for copy in copies:
        copy.wait()

    @pl.loop(0, spans)
    def _(j):
        weight_copy(j).wait()
        at = pl.ds(pl.multiple_of(j * span, span), span)
        total = jnp.dot(hidden_ref[0], weight_ref[mine_at, at], preferred_element_type=jnp.float32)
        total += jnp.dot(hidden_ref[1], weight_ref[other_at, at], preferred_element_type=jnp.float32)
        result = total.astype(jnp.bfloat16)
        for own in range(2):
            mixed = lax.dot_general(
                scaled[own],
                result[2 * own * capacity : 2 * (own + 1) * capacity],
                (((0,), (0,)), ((), ())),
                preferred_element_type=jnp.float32,
            )
            out_ref[2 * own : 2 * own + 2, :, at] = mixed.astype(jnp.bfloat16).reshape(2, rows, span)
        out_copy(j, 0, keep_hbm).start()
        out_copy(j, 1, send_hbm).start()

    for j in range(spans):
        out_copy(j, 0, keep_hbm).wait()
        out_copy(j, 1, send_hbm).wait()


def pick_call(k, where, code, pairs, weight, earlier, capacity):
    _, rows, width = pairs[0].shape
    depth, columns = weight.shape
    tall = 4 * capacity
    anywhere = pl.BlockSpec(memory_space=pl.ANY)
    return pl.pallas_call(
        functools.partial(pick_kernel, capacity, k),
        in_specs=[
            pl.BlockSpec(memory_space=pltpu.SMEM),
            pl.BlockSpec(memory_space=pltpu.VMEM),
            *[anywhere] * (5 + len(earlier)),
        ],
        out_specs=pl.BlockSpec(memory_space=pltpu.VMEM),
        out_shape=jax.ShapeDtypeStruct((tall, columns // 2), jnp.bfloat16),
        scratch_shapes=[
            pltpu.VMEM((8, rows, width), jnp.bfloat16),
            pltpu.VMEM((depth, columns), jnp.bfloat16),
            pltpu.VMEM((tall, depth), jnp.bfloat16),
            pltpu.SemaphoreType.DMA((4 + columns // (8 * UNITS),)),
        ],
        compiler_params=pltpu.CompilerParams(vmem_limit_bytes=VMEM),
        cost_estimate=pl.CostEstimate(
            flops=2 * tall * depth * (columns + rows),
            bytes_accessed=2 * (8 * rows * width + weight.size + tall * columns // 2),
            transcendentals=tall * columns // 2,
        ),
        name="gate_up",
    )(where, code, *pairs, weight, *earlier)


def sum_call(k, where, code, mine, other, weight, earlier, capacity):
    rows = code.shape[1]
    depth, wide = weight.shape
    tall, units = mine.shape
    anywhere = pl.BlockSpec(memory_space=pl.ANY)
    return pl.pallas_call(
        functools.partial(sum_kernel, capacity, k),
        in_specs=[
            pl.BlockSpec(memory_space=pltpu.SMEM),
            pl.BlockSpec(memory_space=pltpu.VMEM),
            *[anywhere] * (3 + len(earlier)),
        ],
        out_specs=[anywhere] * 2,
        out_shape=[jax.ShapeDtypeStruct((2, rows, wide), jnp.bfloat16)] * 2,
        scratch_shapes=[
            pltpu.VMEM((2, tall, units), jnp.bfloat16),
            pltpu.VMEM((depth, wide), jnp.bfloat16),
            pltpu.VMEM((4, rows, wide), jnp.bfloat16),
            pltpu.SemaphoreType.DMA((2 + 3 * (wide // 512),)),
        ],
        compiler_params=pltpu.CompilerParams(vmem_limit_bytes=VMEM),
        cost_estimate=pl.CostEstimate(
            flops=2 * wide * (tall * depth + 4 * rows * capacity),
            bytes_accessed=2 * (2 * mine.size + weight.size + 4 * rows * wide),
            transcendentals=0,
        ),
        name="down",
    )(where, code, mine, other, weight, *earlier)


def codes_of(expert_ids, numerators, experts):
    rows = expert_ids.shape[0]
    named = expert_ids.T[None] == jnp.arange(experts, dtype=jnp.int32)[:, None, None]
    hits = jnp.any(named, axis=1)
    weight = jnp.sum(jnp.where(named, numerators.T[None], 0), axis=1)
    earlier = jnp.arange(rows)[:, None] < jnp.arange(rows)[None, :]
    rank = jnp.dot(hits.astype(jnp.bfloat16), earlier.astype(jnp.bfloat16), preferred_element_type=jnp.float32)
    return jnp.where(hits, rank.astype(jnp.int32) * 256 + weight, -1)


def shards(tokens, expert_ids, numerators, gate_up_weight, down_weight):
    rows, width = tokens.shape
    experts = lax.axis_size("expert")
    capacity = rows * expert_ids.shape[1] * 5 // (4 * experts)
    chips = experts // 2
    across = [[2 * i + c for i in range(chips)] for c in range(2)]
    pairs = [[2 * i, 2 * i + 1] for i in range(chips)]

    codes = lax.all_gather(codes_of(expert_ids, numerators, experts), "expert", axis=0)
    code = lax.dynamic_index_in_dim(codes, lax.axis_index("expert"), 1, keepdims=False)
    code = code.reshape(chips, 2, rows).swapaxes(0, 1).reshape(experts, rows)

    wide = lax.all_gather(tokens, "section", axis=0)
    half = lax.all_gather(wide, "expert", axis=0, axis_index_groups=across)
    whole = lax.all_gather(half, "expert", axis=0, axis_index_groups=pairs)
    whole = whole.reshape((experts,) + wide.shape)

    hidden = up_call(code, whole, gate_up_weight[0], capacity)
    hidden = lax.all_gather(hidden, "section", axis=0)
    part = down_call(code, hidden, down_weight[0], capacity)

    part = part.reshape(2, chips * rows, width)
    part = lax.psum_scatter(part, "expert", scatter_dimension=0, axis_index_groups=pairs, tiled=False)
    return lax.psum_scatter(part, "expert", scatter_dimension=0, axis_index_groups=across, tiled=True)


def pair_shards(tokens, expert_ids, numerators, gate_up_weight, down_weight):
    rows, width = tokens.shape
    experts = lax.axis_size("expert")
    layers = experts // 4
    capacity = rows * expert_ids.shape[1] * 5 // (4 * experts)
    axes = ("section", "expert")
    ring = [0, *range(1, layers, 2), *reversed(range(2, layers, 2))]
    following = {z: ring[(p + 1) % layers] for p, z in enumerate(ring)}

    def perm(place):
        moves = []
        for x in range(2):
            for z in range(layers):
                for y in range(2):
                    for c in range(2):
                        tx, tz, ty, tc = place(x, z, y, c)
                        moves.append(((x * layers + z) * 4 + y * 2 + c, (tx * layers + tz) * 4 + ty * 2 + tc))
        return moves

    onward = perm(lambda x, z, y, c: (x, following[z], y, c))
    backward = [(to, source) for source, to in onward]
    first = perm(lambda x, z, y, c: (x ^ (1 - c), z, y ^ c, c))
    second = perm(lambda x, z, y, c: (x ^ c, z, y ^ (1 - c), c))
    sibling = perm(lambda x, z, y, c: (x, z, y, 1 - c))
    over_x = perm(lambda x, z, y, c: (1 - x, z, y, c))
    over_y = perm(lambda x, z, y, c: (x, z, 1 - y, c))

    def move(value, moves):
        return lax.ppermute(value, axes, moves)

    table = np.zeros((2, layers, 2, 2, layers, 6), np.int32)
    for x, z, y, c, k in np.ndindex(2, layers, 2, 2, layers):
        at = ring[(ring.index(z) - k) % layers] * 4
        table[x, z, y, c, k] = [at + (y ^ (i & 1)) * 2 + (c ^ (i >> 1)) for i in range(4)] + [x, c]
    device = lax.axis_index("section") * experts + lax.axis_index("expert")
    where = lax.dynamic_index_in_dim(jnp.asarray(table.reshape(2 * experts, layers, 6)), device, 0, keepdims=False)
    def after(value, *done):
        return lax.optimization_barrier((value, *done))[0]

    near = move(tokens, first)
    later = move(tokens, onward)
    near_later = move(later, first)
    last = move(later, onward)
    named = codes_of(after(expert_ids, later), numerators, experts)
    code = lax.all_to_all(named, "expert", split_axis=0, concat_axis=0, tiled=True)
    pairs = [jnp.stack([tokens, near]), jnp.stack([later, near_later])]
    crosses = [move(pairs[0], second)]
    near_last = move(after(last, near_later, crosses[0], code), first)
    pairs.append(jnp.stack([last, near_last]))
    third = move(last, onward)
    pairs.append(jnp.stack([third, move(near_last, onward)]))
    crosses.append(move(after(pairs[1], pairs[2], third), second))

    def spread(k, *done):
        return [pairs[k], crosses[k], move(pairs[k], sibling), move(after(crosses[k], *done), sibling)]

    def gate_up(k, shards_of, *earlier):
        return pick_call(k, where, code, shards_of, gate_up_weight[0], earlier, capacity)

    def swap(mine, *done):
        return mine, move(after(mine, *done), over_x)

    def down(k, hidden, *earlier):
        return sum_call(k, where, code, *hidden, down_weight[0], earlier, capacity)

    def give(part, *done):
        return part[0], move(after(part[1], *done), sibling)

    def away(part):
        keep, got = part
        return (keep[1].astype(jnp.float32) + got[1].astype(jnp.float32)).astype(jnp.bfloat16)

    def total(part, back, *hop):
        terms = [v.astype(jnp.float32) for v in (part[0][0], part[1][0], back, *hop)]
        return functools.reduce(jnp.add, terms).astype(jnp.bfloat16)

    mine0 = gate_up(0, spread(0))
    crosses.append(move(after(pairs[2], mine0), second))
    hidden1 = swap(gate_up(1, spread(1, mine0), mine0))
    pairs[3] = after(pairs[3], hidden1[0])
    crosses.append(move(after(pairs[3], hidden1[1]), second))
    hidden2 = swap(gate_up(2, spread(2, hidden1[0]), hidden1[0], pairs[3]))
    part1 = down(1, hidden1, hidden2[0], crosses[3])
    shards3 = spread(3, hidden2[0])
    part1 = give(part1)
    back1 = move(away(part1), over_y)
    hidden3 = swap(gate_up(3, shards3, part1[0]))
    part2 = give(down(2, hidden2, hidden3[0]), hidden3[1], back1)
    hidden0 = swap(mine0, hidden3[1])
    from_next = move(total(part1, after(back1, hidden3[0])), backward)
    back2 = move(away(part2), over_y)
    part3 = down(3, hidden3, part2[0])
    part0 = give(down(0, hidden0, part3[0]))
    part3 = give(part3, from_next, back2, part0[0])
    from_far = move(total(part2, back2), onward)
    back3 = move(away(part3), over_y)
    from_last = move(total(part3, back3, from_far), onward)
    back0 = move(after(away(part0), back3), over_y)
    return total(part0, back0, from_next, from_last)


def solution(mesh):
    in_specs = (
        P("expert", "section"),
        P("expert", None),
        P("expert", None),
        P("expert", None, "section"),
        P("expert", None, "section"),
    )
    out_specs = P("expert", "section")
    fits = mesh.shape["section"] == 2 and mesh.shape["expert"] == 16
    return jax.shard_map(pair_shards if fits else shards, mesh=mesh, in_specs=in_specs, out_specs=out_specs, check_vma=False)
```

```python
import functools

import jax
import jax.numpy as jnp
import numpy as np
from jax import lax
from jax.experimental import pallas as pl
from jax.experimental.pallas import tpu as pltpu
from jax.sharding import PartitionSpec as P

UNITS = 64
SCALE = 1.0 / 256.0
VMEM = 40 * 1024 * 1024


def group_of(capacity):
    count = 2
    while (count * capacity) % 16:
        count *= 2
    return count


def slot_map(code, group, capacity):
    line = jnp.concatenate(
        [code[i : i + 1] + jnp.where(code[i : i + 1] >= 0, i * capacity * 256, 0) for i in range(group)], axis=1
    )
    slot, weight = line >> 8, line & 255
    places = lax.broadcasted_iota(jnp.int32, (group * capacity, line.shape[1]), 0)
    return places == slot, weight


def up_kernel(group, capacity, code_ref, tokens_ref, weight_ref, hidden_ref, rows_ref):
    groups = tokens_ref.shape[0] // group
    sections, rows, width = tokens_ref.shape[1:]
    size = group * capacity
    for g in range(groups):
        onehot, _ = slot_map(code_ref[0, g * group : (g + 1) * group], group, capacity)
        onehot = onehot.astype(jnp.bfloat16)
        for s in range(sections):
            block = jnp.concatenate([tokens_ref[g * group + i, s] for i in range(group)], axis=0)
            picked = jnp.dot(onehot, block, preferred_element_type=jnp.float32)
            rows_ref[g * size : (g + 1) * size, s * width : (s + 1) * width] = picked.astype(jnp.bfloat16)
    columns = weight_ref.shape[1]
    pair = 4 * UNITS

    def products(first, count):
        return jnp.dot(rows_ref[...], weight_ref[:, pl.ds(first, count)], preferred_element_type=jnp.float32)

    def mix(gate, up):
        return (gate / (1.0 + jnp.exp(-gate)) * up).astype(jnp.bfloat16)

    @pl.loop(0, columns // pair)
    def _(p):
        both = products(pl.multiple_of(p * pair, pair), pair)
        one, two = both[:, : 2 * UNITS], both[:, 2 * UNITS :]
        low = lax.broadcasted_iota(jnp.int32, one.shape, 1) < UNITS
        gate = jnp.where(low, one, pltpu.roll(two, UNITS, 1))
        up = jnp.where(low, pltpu.roll(one, UNITS, 1), two)
        hidden_ref[:, pl.ds(pl.multiple_of(p * 2 * UNITS, 2 * UNITS), 2 * UNITS)] = mix(gate, up)

    if columns % pair:
        start = columns // pair * pair
        both = products(start, 2 * UNITS)
        hidden_ref[:, start // 2 :] = mix(both, pltpu.roll(both, UNITS, 1))[:, :UNITS]


def down_kernel(group, capacity, code_ref, hidden_ref, weight_ref, out_ref, result_ref):
    sections, _, units = hidden_ref.shape
    groups = code_ref.shape[1] // group
    size = group * capacity
    wide = weight_ref.shape[1]
    step = min(512, wide)

    @pl.loop(0, wide // step)
    def _(p):
        at = pl.ds(pl.multiple_of(p * step, step), step)
        total = jnp.dot(hidden_ref[0], weight_ref[0:units, at], preferred_element_type=jnp.float32)
        for s in range(1, sections):
            total += jnp.dot(
                hidden_ref[s], weight_ref[s * units : (s + 1) * units, at], preferred_element_type=jnp.float32
            )
        result_ref[...] = total.astype(jnp.bfloat16)
        for g in range(groups):
            onehot, weight = slot_map(code_ref[0, g * group : (g + 1) * group], group, capacity)
            scaled = jnp.where(onehot, weight.astype(jnp.float32) * SCALE, 0.0).astype(jnp.bfloat16)
            mixed = lax.dot_general(
                scaled,
                result_ref[g * size : (g + 1) * size],
                (((0,), (0,)), ((), ())),
                preferred_element_type=jnp.float32,
            )
            tall = scaled.shape[1]
            out_ref[g * tall : (g + 1) * tall, at] = mixed.astype(jnp.bfloat16)


def up_call(code, tokens, weight, capacity):
    blocks, sections, rows, width = tokens.shape
    group = group_of(capacity)
    take = min(blocks, 2 * group)
    depth, columns = weight.shape
    tall = take * capacity
    flops = 2 * blocks * capacity * depth * (columns + group * rows)
    return pl.pallas_call(
        functools.partial(up_kernel, group, capacity),
        grid=(blocks // take,),
        in_specs=[
            pl.BlockSpec((1, take, rows), lambda i: (i, 0, 0)),
            pl.BlockSpec((take, sections, rows, width), lambda i: (i, 0, 0, 0)),
            pl.BlockSpec((depth, columns), lambda i: (0, 0), pipeline_mode=pl.Buffered(1)),
        ],
        out_specs=pl.BlockSpec((tall, columns // 2), lambda i: (i, 0)),
        out_shape=jax.ShapeDtypeStruct((blocks * capacity, columns // 2), jnp.bfloat16),
        scratch_shapes=[pltpu.VMEM((tall, depth), jnp.bfloat16)],
        compiler_params=pltpu.CompilerParams(vmem_limit_bytes=48 * 1024 * 1024),
        cost_estimate=pl.CostEstimate(
            flops=flops, bytes_accessed=2 * (tokens.size + weight.size), transcendentals=blocks * capacity * columns // 2
        ),
        name="gate_up",
    )(code.reshape(blocks // take, take, rows), tokens, weight)


def down_call(code, hidden, weight, capacity):
    blocks, rows = code.shape
    sections, _, units = hidden.shape
    group = group_of(capacity)
    take = min(blocks, 2 * group)
    depth, wide = weight.shape
    tall = take * capacity
    return pl.pallas_call(
        functools.partial(down_kernel, group, capacity),
        grid=(blocks // take,),
        in_specs=[
            pl.BlockSpec((1, take, rows), lambda i: (i, 0, 0)),
            pl.BlockSpec((sections, tall, units), lambda i: (0, i, 0)),
            pl.BlockSpec((depth, wide), lambda i: (0, 0), pipeline_mode=pl.Buffered(1)),
        ],
        out_specs=pl.BlockSpec((take * rows, wide), lambda i: (i, 0)),
        out_shape=jax.ShapeDtypeStruct((blocks * rows, wide), jnp.bfloat16),
        scratch_shapes=[pltpu.VMEM((tall, min(512, wide)), jnp.bfloat16)],
        compiler_params=pltpu.CompilerParams(vmem_limit_bytes=48 * 1024 * 1024),
        cost_estimate=pl.CostEstimate(
            flops=2 * blocks * capacity * wide * (depth + group * rows),
            bytes_accessed=2 * (hidden.size + weight.size + blocks * rows * wide),
            transcendentals=0,
        ),
        name="down",
    )(code.reshape(blocks // take, take, rows), hidden, weight)


def block_codes(k, own, where_ref, code_ref):
    return jnp.concatenate([code_ref[pl.ds(where_ref[k, 2 * own + i], 1), :] for i in range(2)], axis=0)


def pick_kernel(capacity, k, where_ref, code_ref, *refs):
    pairs, weight_hbm = refs[:4], refs[4]
    hidden_ref, pair_ref, weight_ref, rows_ref, sems = refs[-5:]
    rows, width = pairs[0].shape[1:]
    span = 8 * UNITS
    spans = weight_hbm.shape[1] // span
    x, c = where_ref[k, 4], where_ref[k, 5]

    def weight_copy(j):
        at = pl.ds(pl.multiple_of(j * span, span), span)
        return pltpu.make_async_copy(weight_hbm.at[:, at], weight_ref.at[:, at], sems.at[4 + j])

    copies = [pltpu.make_async_copy(v, pair_ref.at[pl.ds(2 * i, 2)], sems.at[i]) for i, v in enumerate(pairs)]
    for copy in copies:
        copy.start()
    for j in range(spans):
        weight_copy(j).start()
    for own in range(2):
        core = c ^ own
        onehot, _ = slot_map(block_codes(k, own, where_ref, code_ref), 2, capacity)
        onehot = onehot.astype(jnp.bfloat16)
        copies[2 * own].wait()
        copies[2 * own + 1].wait()
        for section, near, far in ((x, 0, 2 - core), (1 - x, 1 + core, 3)):
            block = jnp.concatenate([pair_ref[4 * own + near], pair_ref[4 * own + far]], axis=0)
            picked = jnp.dot(onehot, block, preferred_element_type=jnp.float32)
            at = pl.ds(pl.multiple_of(section * width, width), width)
            rows_ref[2 * own * capacity : 2 * (own + 1) * capacity, at] = picked.astype(jnp.bfloat16)

    @pl.loop(0, spans)
    def _(j):
        weight_copy(j).wait()
        at = pl.ds(pl.multiple_of(j * span, span), span)
        both = jnp.dot(rows_ref[...], weight_ref[:, at], preferred_element_type=jnp.float32)
        for p in range(2):
            one, two = both[:, 4 * p * UNITS : (4 * p + 2) * UNITS], both[:, (4 * p + 2) * UNITS : 4 * (p + 1) * UNITS]
            low = lax.broadcasted_iota(jnp.int32, one.shape, 1) < UNITS
            gate = jnp.where(low, one, pltpu.roll(two, UNITS, 1))
            up = jnp.where(low, pltpu.roll(one, UNITS, 1), two)
            half = pl.ds(pl.multiple_of((2 * j + p) * 2 * UNITS, 2 * UNITS), 2 * UNITS)
            hidden_ref[:, half] = (gate / (1.0 + jnp.exp(-gate)) * up).astype(jnp.bfloat16)


def sum_kernel(capacity, k, where_ref, code_ref, *refs):
    mine_hbm, other_hbm, weight_hbm = refs[:3]
    keep_hbm, send_hbm, hidden_ref, weight_ref, out_ref, sems = refs[-6:]
    rows = code_ref.shape[1]
    units = mine_hbm.shape[1]
    span = 512
    spans = weight_hbm.shape[1] // span

    def weight_copy(j):
        at = pl.ds(pl.multiple_of(j * span, span), span)
        return pltpu.make_async_copy(weight_hbm.at[:, at], weight_ref.at[:, at], sems.at[2 + j])

    def out_copy(j, i, to):
        at = pl.ds(pl.multiple_of(j * span, span), span)
        sem = sems.at[2 + spans + 2 * j + i]
        return pltpu.make_async_copy(out_ref.at[pl.ds(2 * i, 2), :, at], to.at[:, :, at], sem)

    copies = [pltpu.make_async_copy(v, hidden_ref.at[i], sems.at[i]) for i, v in enumerate((mine_hbm, other_hbm))]
    for copy in copies:
        copy.start()
    for j in range(spans):
        weight_copy(j).start()
    scaled = []
    for own in range(2):
        onehot, weight = slot_map(block_codes(k, own, where_ref, code_ref), 2, capacity)
        scaled.append(jnp.where(onehot, weight.astype(jnp.float32) * SCALE, 0.0).astype(jnp.bfloat16))
    me = where_ref[k, 4]
    mine_at = pl.ds(pl.multiple_of(me * units, units), units)
    other_at = pl.ds(pl.multiple_of((1 - me) * units, units), units)
    for copy in copies:
        copy.wait()

    @pl.loop(0, spans)
    def _(j):
        weight_copy(j).wait()
        at = pl.ds(pl.multiple_of(j * span, span), span)
        total = jnp.dot(hidden_ref[0], weight_ref[mine_at, at], preferred_element_type=jnp.float32)
        total += jnp.dot(hidden_ref[1], weight_ref[other_at, at], preferred_element_type=jnp.float32)
        result = total.astype(jnp.bfloat16)
        for own in range(2):
            mixed = lax.dot_general(
                scaled[own],
                result[2 * own * capacity : 2 * (own + 1) * capacity],
                (((0,), (0,)), ((), ())),
                preferred_element_type=jnp.float32,
            )
            out_ref[2 * own : 2 * own + 2, :, at] = mixed.astype(jnp.bfloat16).reshape(2, rows, span)
        out_copy(j, 0, keep_hbm).start()
        out_copy(j, 1, send_hbm).start()

    for j in range(spans):
        out_copy(j, 0, keep_hbm).wait()
        out_copy(j, 1, send_hbm).wait()


def pick_call(k, where, code, pairs, weight, earlier, capacity):
    _, rows, width = pairs[0].shape
    depth, columns = weight.shape
    tall = 4 * capacity
    anywhere = pl.BlockSpec(memory_space=pl.ANY)
    return pl.pallas_call(
        functools.partial(pick_kernel, capacity, k),
        in_specs=[
            pl.BlockSpec(memory_space=pltpu.SMEM),
            pl.BlockSpec(memory_space=pltpu.VMEM),
            *[anywhere] * (5 + len(earlier)),
        ],
        out_specs=pl.BlockSpec(memory_space=pltpu.VMEM),
        out_shape=jax.ShapeDtypeStruct((tall, columns // 2), jnp.bfloat16),
        scratch_shapes=[
            pltpu.VMEM((8, rows, width), jnp.bfloat16),
            pltpu.VMEM((depth, columns), jnp.bfloat16),
            pltpu.VMEM((tall, depth), jnp.bfloat16),
            pltpu.SemaphoreType.DMA((4 + columns // (8 * UNITS),)),
        ],
        compiler_params=pltpu.CompilerParams(vmem_limit_bytes=VMEM),
        cost_estimate=pl.CostEstimate(
            flops=2 * tall * depth * (columns + rows),
            bytes_accessed=2 * (8 * rows * width + weight.size + tall * columns // 2),
            transcendentals=tall * columns // 2,
        ),
        name="gate_up",
    )(where, code, *pairs, weight, *earlier)


def sum_call(k, where, code, mine, other, weight, earlier, capacity):
    rows = code.shape[1]
    depth, wide = weight.shape
    tall, units = mine.shape
    anywhere = pl.BlockSpec(memory_space=pl.ANY)
    return pl.pallas_call(
        functools.partial(sum_kernel, capacity, k),
        in_specs=[
            pl.BlockSpec(memory_space=pltpu.SMEM),
            pl.BlockSpec(memory_space=pltpu.VMEM),
            *[anywhere] * (3 + len(earlier)),
        ],
        out_specs=[anywhere] * 2,
        out_shape=[jax.ShapeDtypeStruct((2, rows, wide), jnp.bfloat16)] * 2,
        scratch_shapes=[
            pltpu.VMEM((2, tall, units), jnp.bfloat16),
            pltpu.VMEM((depth, wide), jnp.bfloat16),
            pltpu.VMEM((4, rows, wide), jnp.bfloat16),
            pltpu.SemaphoreType.DMA((2 + 3 * (wide // 512),)),
        ],
        compiler_params=pltpu.CompilerParams(vmem_limit_bytes=VMEM),
        cost_estimate=pl.CostEstimate(
            flops=2 * wide * (tall * depth + 4 * rows * capacity),
            bytes_accessed=2 * (2 * mine.size + weight.size + 4 * rows * wide),
            transcendentals=0,
        ),
        name="down",
    )(where, code, mine, other, weight, *earlier)


def codes_of(expert_ids, numerators, experts):
    rows = expert_ids.shape[0]
    named = expert_ids.T[None] == jnp.arange(experts, dtype=jnp.int32)[:, None, None]
    hits = jnp.any(named, axis=1)
    weight = jnp.sum(jnp.where(named, numerators.T[None], 0), axis=1)
    earlier = jnp.arange(rows)[:, None] < jnp.arange(rows)[None, :]
    rank = jnp.dot(hits.astype(jnp.bfloat16), earlier.astype(jnp.bfloat16), preferred_element_type=jnp.float32)
    return jnp.where(hits, rank.astype(jnp.int32) * 256 + weight, -1)


def shards(tokens, expert_ids, numerators, gate_up_weight, down_weight):
    rows, width = tokens.shape
    experts = lax.axis_size("expert")
    capacity = rows * expert_ids.shape[1] * 5 // (4 * experts)
    chips = experts // 2
    across = [[2 * i + c for i in range(chips)] for c in range(2)]
    pairs = [[2 * i, 2 * i + 1] for i in range(chips)]

    codes = lax.all_gather(codes_of(expert_ids, numerators, experts), "expert", axis=0)
    code = lax.dynamic_index_in_dim(codes, lax.axis_index("expert"), 1, keepdims=False)
    code = code.reshape(chips, 2, rows).swapaxes(0, 1).reshape(experts, rows)

    wide = lax.all_gather(tokens, "section", axis=0)
    half = lax.all_gather(wide, "expert", axis=0, axis_index_groups=across)
    whole = lax.all_gather(half, "expert", axis=0, axis_index_groups=pairs)
    whole = whole.reshape((experts,) + wide.shape)

    hidden = up_call(code, whole, gate_up_weight[0], capacity)
    hidden = lax.all_gather(hidden, "section", axis=0)
    part = down_call(code, hidden, down_weight[0], capacity)

    part = part.reshape(2, chips * rows, width)
    part = lax.psum_scatter(part, "expert", scatter_dimension=0, axis_index_groups=pairs, tiled=False)
    return lax.psum_scatter(part, "expert", scatter_dimension=0, axis_index_groups=across, tiled=True)


def pair_shards(tokens, expert_ids, numerators, gate_up_weight, down_weight):
    rows, width = tokens.shape
    experts = lax.axis_size("expert")
    layers = experts // 4
    capacity = rows * expert_ids.shape[1] * 5 // (4 * experts)
    axes = ("section", "expert")
    ring = [0, *range(1, layers, 2), *reversed(range(2, layers, 2))]
    following = {z: ring[(p + 1) % layers] for p, z in enumerate(ring)}

    def perm(place):
        moves = []
        for x in range(2):
            for z in range(layers):
                for y in range(2):
                    for c in range(2):
                        tx, tz, ty, tc = place(x, z, y, c)
                        moves.append(((x * layers + z) * 4 + y * 2 + c, (tx * layers + tz) * 4 + ty * 2 + tc))
        return moves

    onward = perm(lambda x, z, y, c: (x, following[z], y, c))
    backward = [(to, source) for source, to in onward]
    first = perm(lambda x, z, y, c: (x ^ (1 - c), z, y ^ c, c))
    second = perm(lambda x, z, y, c: (x ^ c, z, y ^ (1 - c), c))
    sibling = perm(lambda x, z, y, c: (x, z, y, 1 - c))
    over_x = perm(lambda x, z, y, c: (1 - x, z, y, c))
    over_y = perm(lambda x, z, y, c: (x, z, 1 - y, c))

    def move(value, moves):
        return lax.ppermute(value, axes, moves)

    table = np.zeros((2, layers, 2, 2, layers, 6), np.int32)
    for x, z, y, c, k in np.ndindex(2, layers, 2, 2, layers):
        at = ring[(ring.index(z) - k) % layers] * 4
        table[x, z, y, c, k] = [at + (y ^ (i & 1)) * 2 + (c ^ (i >> 1)) for i in range(4)] + [x, c]
    device = lax.axis_index("section") * experts + lax.axis_index("expert")
    where = lax.dynamic_index_in_dim(jnp.asarray(table.reshape(2 * experts, layers, 6)), device, 0, keepdims=False)
    def after(value, *done):
        return lax.optimization_barrier((value, *done))[0]

    near = move(tokens, first)
    later = move(tokens, onward)
    near_later = move(later, first)
    last = move(later, onward)
    named = codes_of(after(expert_ids, later), numerators, experts)
    code = lax.all_to_all(named, "expert", split_axis=0, concat_axis=0, tiled=True)
    pairs = [jnp.stack([tokens, near]), jnp.stack([later, near_later])]
    crosses = [move(pairs[0], second)]
    near_last = move(after(last, near_later, crosses[0], code), first)
    pairs.append(jnp.stack([last, near_last]))
    pairs.append(move(pairs[2], onward))
    crosses.append(move(after(pairs[1], pairs[2]), second))

    def spread(k, *done):
        return [pairs[k], crosses[k], move(pairs[k], sibling), move(after(crosses[k], *done), sibling)]

    def gate_up(k, shards_of, *earlier):
        return pick_call(k, where, code, shards_of, gate_up_weight[0], earlier, capacity)

    def swap(mine, *done):
        return mine, move(after(mine, *done), over_x)

    def down(k, hidden, *earlier):
        return sum_call(k, where, code, *hidden, down_weight[0], earlier, capacity)

    def give(part, *done):
        return part[0], move(after(part[1], *done), sibling)

    def away(part):
        keep, got = part
        return (keep[1].astype(jnp.float32) + got[1].astype(jnp.float32)).astype(jnp.bfloat16)

    def total(part, back, *hop):
        terms = [v.astype(jnp.float32) for v in (part[0][0], part[1][0], back, *hop)]
        return functools.reduce(jnp.add, terms).astype(jnp.bfloat16)

    mine0 = gate_up(0, spread(0))
    crosses.append(move(after(pairs[2], mine0), second))
    hidden1 = swap(gate_up(1, spread(1, mine0), mine0))
    pairs[3] = after(pairs[3], hidden1[0])
    crosses.append(move(after(pairs[3], hidden1[1]), second))
    hidden2 = swap(gate_up(2, spread(2, hidden1[0]), hidden1[0], pairs[3]))
    part1 = down(1, hidden1, hidden2[0], crosses[3])
    shards3 = spread(3, hidden2[0])
    hidden3 = swap(gate_up(3, shards3, part1[0]))
    part1 = give(part1, shards3[3])
    back1 = move(after(away(part1), hidden3[0]), over_y)
    part2 = give(down(2, hidden2, hidden3[0]), hidden3[1], back1)
    hidden0 = swap(mine0, hidden3[1])
    from_next = move(total(part1, after(back1, hidden3[0])), backward)
    back2 = move(away(part2), over_y)
    part3 = down(3, hidden3, part2[0])
    part0 = give(down(0, hidden0, part3[0]))
    part3 = give(part3, from_next, back2, part0[0])
    from_far = move(total(part2, back2), onward)
    back3 = move(away(part3), over_y)
    from_last = move(total(part3, back3, from_far), onward)
    back0 = move(after(away(part0), back3), over_y)
    return total(part0, back0, from_next, from_last)


def solution(mesh):
    in_specs = (
        P("expert", "section"),
        P("expert", None),
        P("expert", None),
        P("expert", None, "section"),
        P("expert", None, "section"),
    )
    out_specs = P("expert", "section")
    fits = mesh.shape["section"] == 2 and mesh.shape["expert"] == 16
    return jax.shard_map(pair_shards if fits else shards, mesh=mesh, in_specs=in_specs, out_specs=out_specs, check_vma=False)
```
